32 devices in a mesh: dp: 2 (over y), row: 4 (over z), col: 4 (over x, core).
Axes of the slice: x: 2, y: 2, z: 4, core: 2. Of those that a mesh axis runs over, the one named last changes fastest.
Arguments:
- tokens: bfloat16 [2048, 1024], P(('dp', 'row')), may hold values from -6 to 6
- cotangent: bfloat16 [2048, 1024], P(('dp', 'row')), may hold values from -6 to 6
- norm_in: float32 [1024], replicated, may hold values from 0.5 to 1.5
- z_weight: bfloat16 [1024, 1536], P(('dp', 'row'), 'col'), may hold values from -0.1875 to 0.1875
- x_weight: bfloat16 [1024, 1536], P(('dp', 'row'), 'col'), may hold values from -0.1875 to 0.1875
- dt_weight: bfloat16 [1024, 24], P(('dp', 'row'), 'col'), may hold values from -0.1875 to 0.1875
- q_weight: bfloat16 [1024, 512], P(('dp', 'row'), 'col'), may hold values from -0.1875 to 0.1875
- bc_weight: bfloat16 [1024, 256], P(('dp', 'row')), may hold values from -0.1875 to 0.1875
- key_value_weight: bfloat16 [1024, 256], P(('dp', 'row')), may hold values from -0.1875 to 0.1875
- conv_x: float32 [4, 1536], P(None, 'col'), may hold values from -0.5 to 0.5
- conv_bc: float32 [4, 256], replicated, may hold values from -0.5 to 0.5
- dt_bias: float32 [24], P('col'), may hold values from -7 to -2.3
- a_log: float32 [24], P('col'), may hold values from 0 to 2.77
- d_skip: float32 [24], P('col'), may hold values from 0.5 to 1.5
- gate_gain: float32 [1536], P('col'), may hold values from 0.5 to 1.5
- mamba_weight: bfloat16 [1536, 1024], P('col', ('dp', 'row')), may hold values from -0.15625 to 0.15625
- attn_weight: bfloat16 [512, 1024], P('col', ('dp', 'row')), may hold values from -1 to 1
- norm_mid: float32 [1024], replicated, may hold values from 0.5 to 1.5
- gate_weight: bfloat16 [1024, 2048], P(('dp', 'row'), 'col'), may hold values from -0.1875 to 0.1875
- up_weight: bfloat16 [1024, 2048], P(('dp', 'row'), 'col'), may hold values from -0.1875 to 0.1875
- down_weight: bfloat16 [2048, 1024], P('col', ('dp', 'row')), may hold values from -0.125 to 0.125
Outputs:
- layer_out: bfloat16 [2048, 1024], P(('dp', 'row'))
- grad_tokens: float32 [2048, 1024], P(('dp', 'row'))
- grad_norm_in: float32 [1024], replicated
- grad_z_weight: float32 [1024, 1536], P(('dp', 'row'), 'col')
- grad_x_weight: float32 [1024, 1536], P(('dp', 'row'), 'col')
- grad_dt_weight: float32 [1024, 24], P(('dp', 'row'), 'col')
- grad_q_weight: float32 [1024, 512], P(('dp', 'row'), 'col')
- grad_bc_weight: float32 [1024, 256], P(('dp', 'row'))
- grad_kv_weight: float32 [1024, 256], P(('dp', 'row'))
- grad_conv_x: float32 [4, 1536], P(None, 'col')
- grad_conv_bc: float32 [4, 256], replicated
- grad_dt_bias: float32 [24], P('col')
- grad_a_log: float32 [24], P('col')
- grad_d_skip: float32 [24], P('col')
- grad_gate_gain: float32 [1536], P('col')
- grad_mamba_weight: float32 [1536, 1024], P('col', ('dp', 'row'))
- grad_attn_weight: float32 [512, 1024], P('col', ('dp', 'row'))
- grad_norm_mid: float32 [1024], replicated
- grad_gate_weight: float32 [1024, 2048], P(('dp', 'row'), 'col')
- grad_up_weight: float32 [1024, 2048], P(('dp', 'row'), 'col')
- grad_down_weight: float32 [2048, 1024], P('col', ('dp', 'row'))
The draws below stay inside these ranges and needn't reach their ends.
All inputs are finite; a program needn't handle non-finite values.
Results may differ from the reference program's by a relative error of at most 0.03.
Values may be sent and summed in bfloat16 or wider, within the bound.
No kernel may reach another device: no remote copies, remote signals or barrier semaphores. Data moves between devices by JAX's collectives and lax.ppermute only.
A program may use at most 128 MiB of HBM per device.

```python
from functools import partial
import jax
import jax.numpy as jnp
from jax import lax

MODEL_DIM = 1024
HM = 24
PM = 64
NS = 128
KC = 4
QUERY_HEADS = 8
KEY_HEADS = 2
HEAD_DIM = 64
FF = 2048
SEQ = 1024
TOKENS = 2048
N_DP = 2


def level_of(rng, dims, split, least, top_value):
    level = 1.0
    for position, blocks in split:
        draws = jax.random.uniform(jax.random.fold_in(jax.random.fold_in(rng, 6), position), (blocks,), jnp.float32, least / len(split), top_value / len(split))
        level = level * jnp.repeat(jnp.exp(draws), dims[position] // blocks).reshape((-1,) + (1,) * (len(dims) - 1 - position))
    return level


def bell_draw(key, shape, scale, limit, shards=(), kind=jnp.bfloat16):
    array = jax.random.normal(key, shape, jnp.float32) * scale
    if len(shards) > 0:
        array = level_of(key, shape, shards, -0.22, 0.18) * array
    return jnp.clip(array, min=-limit, max=limit).astype(kind)


def setup_inputs(seed: int = 0) -> dict:
    key_of = jax.random.split(jax.random.key(seed), 22)
    tokens = bell_draw(key_of[0], (TOKENS, MODEL_DIM), 1.0, 6.0, ((0, 8),))
    cotangent = bell_draw(key_of[1], (TOKENS, MODEL_DIM), 1.0, 6.0, ((0, 8),))
    norm_in = jnp.clip(1.0 + 0.1 * jax.random.normal(key_of[2], (MODEL_DIM,), jnp.float32), 0.5, 1.5)
    z_weight = bell_draw(key_of[3], (MODEL_DIM, HM * PM), MODEL_DIM ** -0.5, 0.1875, ((0, 8), (1, 4)))
    x_weight = bell_draw(key_of[4], (MODEL_DIM, HM * PM), MODEL_DIM ** -0.5, 0.1875, ((0, 8), (1, 4)))
    dt_weight = bell_draw(key_of[5], (MODEL_DIM, HM), MODEL_DIM ** -0.5, 0.1875, ((0, 8), (1, 4)))
    q_weight = bell_draw(key_of[6], (MODEL_DIM, QUERY_HEADS * HEAD_DIM), MODEL_DIM ** -0.5, 0.1875, ((0, 8), (1, 4)))
    bc_weight = bell_draw(key_of[7], (MODEL_DIM, 2 * NS), MODEL_DIM ** -0.5, 0.1875, ((0, 8),))
    key_value_weight = bell_draw(key_of[8], (MODEL_DIM, 2 * KEY_HEADS * HEAD_DIM), MODEL_DIM ** -0.5, 0.1875, ((0, 8),))
    conv_x = jnp.clip(jax.random.uniform(key_of[9], (KC, HM * PM), jnp.float32, -0.5, 0.5) * level_of(key_of[9], (KC, HM * PM), ((1, 4),), -0.4, 0.0), -0.5, 0.5)
    conv_bc = jnp.clip(jax.random.uniform(key_of[10], (KC, 2 * NS), jnp.float32, -0.5, 0.5), -0.5, 0.5)
    dt_bias = jnp.clip(-7.0 + 4.7 * jax.random.uniform(key_of[11], (HM,), jnp.float32) ** level_of(key_of[11], (HM,), ((0, 4),), -0.2, 0.2), -7.0, -2.3)
    a_log = jnp.clip(2.77 * jax.random.uniform(key_of[12], (HM,), jnp.float32) ** level_of(key_of[12], (HM,), ((0, 4),), -0.2, 0.2), 0.0, 2.77)
    d_skip = jnp.clip(0.5 + 1.0 * jax.random.uniform(key_of[13], (HM,), jnp.float32) ** level_of(key_of[13], (HM,), ((0, 4),), -0.2, 0.2), 0.5, 1.5)
    gate_gain = jnp.clip(1.0 + 0.1 * jax.random.normal(key_of[14], (HM * PM,), jnp.float32), 0.5, 1.5)
    mamba_weight = bell_draw(key_of[15], (HM * PM, MODEL_DIM), (HM * PM) ** -0.5, 0.15625, ((0, 4), (1, 8)))
    attn_weight = bell_draw(key_of[16], (QUERY_HEADS * HEAD_DIM, MODEL_DIM), (QUERY_HEADS * HEAD_DIM // 16) ** -0.5, 1.0, ((0, 4), (1, 8)))
    norm_mid = jnp.clip(1.0 + 0.1 * jax.random.normal(key_of[17], (MODEL_DIM,), jnp.float32), 0.5, 1.5)
    gate_weight = bell_draw(key_of[18], (MODEL_DIM, FF), MODEL_DIM ** -0.5, 0.1875, ((0, 8), (1, 4)))
    up_weight = bell_draw(key_of[19], (MODEL_DIM, FF), MODEL_DIM ** -0.5, 0.1875, ((0, 8), (1, 4)))
    down_weight = bell_draw(key_of[20], (FF, MODEL_DIM), FF ** -0.5, 0.125, ((0, 4), (1, 8)))
    return dict(tokens=tokens, cotangent=cotangent, norm_in=norm_in, z_weight=z_weight, x_weight=x_weight, dt_weight=dt_weight, q_weight=q_weight, bc_weight=bc_weight, key_value_weight=key_value_weight, conv_x=conv_x, conv_bc=conv_bc, dt_bias=dt_bias, a_log=a_log, d_skip=d_skip, gate_gain=gate_gain, mamba_weight=mamba_weight, attn_weight=attn_weight, norm_mid=norm_mid, gate_weight=gate_weight, up_weight=up_weight, down_weight=down_weight)


EPSILON = 1e-05
ROPE_BASE = 100000000000.0
NEG_LARGE = -1e+30
HIGHEST = lax.Precision.HIGHEST

@jax.custom_vjp
def lower_precision(v):
    return lax.optimization_barrier(v.astype(jnp.bfloat16)).astype(jnp.float32)

@jax.custom_vjp
def low_back(v):
    return v

def low_keep(v):
    return (lower_precision(v), None)

def low_pass(kept, grad):
    return (grad,)

def back_keep(v):
    return (v, None)

def back_low(kept, grad):
    return (lower_precision(grad),)
lower_precision.defvjp(low_keep, low_pass)
low_back.defvjp(back_keep, back_low)

def matmul(left, right):
    return jnp.dot(left, right, precision=HIGHEST, preferred_element_type=jnp.float32)

def rms_scale(values, gain):
    return values * lax.rsqrt(lax.optimization_barrier(jnp.mean(values * values, axis=-1, keepdims=True)) + EPSILON) * gain

def rotary_embedding(values, token_positions):
    half_width = values.shape[-1] // 2
    frequency = ROPE_BASE ** (-jnp.arange(half_width).astype(jnp.float32) / half_width)
    angles = token_positions[:, None].astype(jnp.float32) * frequency[None, :]
    cosine = jnp.cos(angles)[:, None, :]
    sine_part = jnp.sin(angles)[:, None, :]
    first_half = values[..., :half_width]
    second_half = values[..., half_width:]
    return jnp.concatenate([first_half * cosine - second_half * sine_part, second_half * cosine + first_half * sine_part], axis=-1)

def ssd_block(neg_rate, carry_in, pieces):
    state_now, offset = carry_in
    x_heads, step_size, b_map, c_map = pieces
    step_rate = step_size * neg_rate[None, :]
    cumulative = jnp.cumsum(step_rate, axis=0)
    token_order = jnp.arange(step_rate.shape[0])
    causal = (token_order[:, None] >= token_order[None, :])[:, :, None]
    log_gap = jnp.where(causal, cumulative[:, None, :] - cumulative[None, :, :], 0.0)
    decay_mat = jnp.where(causal, jnp.exp(log_gap), 0.0)
    intersection_cb = jnp.dot(c_map, b_map.T, precision=HIGHEST, preferred_element_type=jnp.float32)
    mixing = decay_mat * intersection_cb[:, :, None] * step_size[None, :, :]
    block_out = jnp.einsum('tuh,uhp->thp', mixing, x_heads, precision=HIGHEST)
    block_out = block_out + jnp.exp(cumulative)[:, :, None] * jnp.einsum('tn,hnp->thp', c_map, state_now, precision=HIGHEST)
    tail_weight = jnp.exp(cumulative[-1][None, :] - cumulative) * step_size
    state_next = state_now * jnp.exp(cumulative[-1])[:, None, None] + jnp.einsum('uh,un,uhp->hnp', tail_weight, b_map, x_heads, precision=HIGHEST)
    return ((state_next, offset + cumulative[-1]), (block_out, offset[None, :] + cumulative))

def layer_forward(params, sequence):
    norm_in, z_weight, x_weight, dt_weight, q_weight, bc_weight, key_value_weight, conv_x, conv_bc, dt_bias, a_log, d_skip, gate_gain, mamba_weight, attn_weight, norm_mid, gate_weight, up_weight, down_weight = params
    sequence_length = sequence.shape[0]
    inner_width = HM * PM
    hidden_in = lower_precision(rms_scale(sequence, norm_in))

    def project(weight):
        return low_back(lower_precision(matmul(hidden_in, weight)))
    z_proj = project(z_weight)
    x_proj = project(x_weight)
    dt_proj = project(dt_weight)
    q_proj = project(q_weight)
    bc_proj = project(bc_weight)
    key_value_projected = project(key_value_weight)
    conv_in = jnp.concatenate([x_proj, bc_proj], axis=1)
    conv_weights = jnp.concatenate([conv_x, conv_bc], axis=1)
    padded = jnp.pad(conv_in, ((KC - 1, 0), (0, 0)))
    conv_out = conv_weights[0][None, :] * padded[0:sequence_length]
    for offset in range(1, KC):
        conv_out = conv_out + conv_weights[offset][None, :] * padded[offset:offset + sequence_length]
    conv_out = jax.nn.silu(conv_out)
    x_heads = conv_out[:, :inner_width].reshape(sequence_length, HM, PM)
    b_map = conv_out[:, inner_width:inner_width + NS]
    c_map = conv_out[:, inner_width + NS:]
    step_size = jax.nn.softplus(dt_proj + dt_bias[None, :])
    neg_rate = -jnp.exp(a_log)
    block_len = min(128, sequence_length)
    block_count = sequence_length // block_len
    pieces = (x_heads.reshape(block_count, block_len, HM, PM), step_size.reshape(block_count, block_len, HM), b_map.reshape(block_count, block_len, NS), c_map.reshape(block_count, block_len, NS))
    initial = (jnp.zeros((HM, NS, PM), jnp.float32), jnp.zeros((HM,), jnp.float32))
    end_state, scan_out = lax.scan(jax.checkpoint(partial(ssd_block, neg_rate)), initial, pieces)
    y_full = (scan_out[0].reshape(sequence_length, HM, PM) + d_skip[None, :, None] * x_heads).reshape(sequence_length, inner_width)
    gated_out = y_full * jax.nn.silu(z_proj)
    mamba_normed = lower_precision(rms_scale(gated_out, gate_gain))
    mamba_out = matmul(mamba_normed, mamba_weight)
    token_positions = jnp.arange(sequence_length).astype(jnp.int32)
    key_value_width = KEY_HEADS * HEAD_DIM
    query_rot = lower_precision(rotary_embedding(q_proj.reshape(sequence_length, QUERY_HEADS, HEAD_DIM), token_positions))
    key_rotated = lower_precision(rotary_embedding(key_value_projected[:, :key_value_width].reshape(sequence_length, KEY_HEADS, HEAD_DIM), token_positions))
    value_gathered = key_value_projected[:, key_value_width:].reshape(sequence_length, KEY_HEADS, HEAD_DIM)
    key_repeated = jnp.repeat(key_rotated, QUERY_HEADS // KEY_HEADS, axis=1)
    value_repeated = jnp.repeat(value_gathered, QUERY_HEADS // KEY_HEADS, axis=1)
    query_block = min(512, sequence_length)
    score_scale = HEAD_DIM ** (-0.5)

    def attend(block_id):
        query_piece = lax.dynamic_slice_in_dim(query_rot, block_id * query_block, query_block, 0)
        scores = low_back(jnp.einsum('qhd,khd->hqk', query_piece, key_repeated, precision=HIGHEST) * score_scale)
        query_pos = block_id * query_block + jnp.arange(query_block).astype(jnp.int32)
        allowed = query_pos[:, None] >= token_positions[None, :]
        scores = jnp.where(allowed[None], scores, NEG_LARGE)
        row_max = lax.optimization_barrier(jnp.max(scores, axis=-1, keepdims=True))
        exponent = jnp.exp(scores - row_max)
        soft_probs = exponent / lax.optimization_barrier(jnp.sum(exponent, axis=-1, keepdims=True))
        return jnp.einsum('hqk,khd->qhd', lower_precision(soft_probs), value_repeated, precision=HIGHEST)
    attn_blocks = lax.map(jax.checkpoint(attend), jnp.arange(sequence_length // query_block).astype(jnp.int32))
    attn_value = low_back(lower_precision(attn_blocks.reshape(sequence_length, QUERY_HEADS * HEAD_DIM)))
    attn_out = matmul(attn_value, attn_weight)
    middle = sequence + low_back(mamba_out + attn_out)
    hidden_mid = lower_precision(rms_scale(middle, norm_mid))
    gate_proj = low_back(lower_precision(matmul(hidden_mid, gate_weight)))
    up_proj = low_back(lower_precision(matmul(hidden_mid, up_weight)))
    swiglu = lower_precision(jax.nn.silu(gate_proj) * up_proj)
    return middle + low_back(matmul(swiglu, down_weight))

def reference(tokens, cotangent, norm_in, z_weight, x_weight, dt_weight, q_weight, bc_weight, key_value_weight, conv_x, conv_bc, dt_bias, a_log, d_skip, gate_gain, mamba_weight, attn_weight, norm_mid, gate_weight, up_weight, down_weight):
    params = (norm_in.astype(jnp.float32), z_weight.astype(jnp.float32), x_weight.astype(jnp.float32), dt_weight.astype(jnp.float32), q_weight.astype(jnp.float32), bc_weight.astype(jnp.float32), key_value_weight.astype(jnp.float32), conv_x.astype(jnp.float32), conv_bc.astype(jnp.float32), dt_bias.astype(jnp.float32), a_log.astype(jnp.float32), d_skip.astype(jnp.float32), gate_gain.astype(jnp.float32), mamba_weight.astype(jnp.float32), attn_weight.astype(jnp.float32), norm_mid.astype(jnp.float32), gate_weight.astype(jnp.float32), up_weight.astype(jnp.float32), down_weight.astype(jnp.float32))
    inputs = tokens.astype(jnp.float32)

    def whole_layer(weights, values):
        sequences = values.reshape(N_DP, SEQ, MODEL_DIM)
        outputs = lax.map(jax.checkpoint(partial(layer_forward, weights)), sequences)
        return outputs.reshape(N_DP * SEQ, MODEL_DIM)
    result, pullback = jax.vjp(whole_layer, params, inputs)
    grad_params, grad_tokens = pullback(cotangent.astype(jnp.float32))
    grad_norm_in, grad_z_weight, grad_x_weight, grad_dt_weight, grad_q_weight, grad_bc_weight, grad_kv_weight, grad_conv_x, grad_conv_bc, grad_dt_bias, grad_a_log, grad_d_skip, grad_gate_gain, grad_mamba_weight, grad_attn_weight, grad_norm_mid, grad_gate_weight, grad_up_weight, grad_down_weight = grad_params
    return (result.astype(jnp.bfloat16), grad_tokens, grad_norm_in, grad_z_weight, grad_x_weight, grad_dt_weight, grad_q_weight, grad_bc_weight, grad_kv_weight, grad_conv_x, grad_conv_bc, grad_dt_bias, grad_a_log, grad_d_skip, grad_gate_gain, grad_mamba_weight, grad_attn_weight, grad_norm_mid, grad_gate_weight, grad_up_weight, grad_down_weight)
```

```python
from functools import partial

import jax
import jax.numpy as jnp
from jax import lax
from jax.experimental import pallas as pl
from jax.experimental.pallas import tpu as pltpu
from jax.sharding import PartitionSpec as P

HM = 24
PM = 64
NS = 128
KC = 4
QUERY_HEADS = 8
KEY_HEADS = 2
HEAD_DIM = 64
HALO = 16
LANES = 128

EPSILON = 1e-05
ROPE_BASE = 100000000000.0
NEG_LARGE = -1e30
HIGHEST = lax.Precision.HIGHEST
F32 = jnp.float32
BF16 = jnp.bfloat16


def mm(a, b, precision=None):
    return lax.dot_general(
        a, b, (((1,), (0,)), ((), ())), precision=precision, preferred_element_type=F32
    )


def mm_nt(a, b, precision=None):
    return lax.dot_general(
        a, b, (((1,), (1,)), ((), ())), precision=precision, preferred_element_type=F32
    )


def mm_tn(a, b, precision=None):
    return lax.dot_general(
        a, b, (((0,), (0,)), ((), ())), precision=precision, preferred_element_type=F32
    )


def low(v):
    return v.astype(BF16)


def sigmoid(v):
    return 1.0 / (1.0 + jnp.exp(-v))


def softplus(v):
    return jnp.maximum(v, 0.0) + jnp.log1p(jnp.exp(-jnp.abs(v)))


def head_lanes(heads):
    head = lax.broadcasted_iota(jnp.int32, (LANES, heads * PM), 0)
    column = lax.broadcasted_iota(jnp.int32, (LANES, heads * PM), 1)
    return ((column >= head * PM) & (column < head * PM + PM)).astype(F32)


def lower_triangle(size):
    later = lax.broadcasted_iota(jnp.int32, (size, size), 0)
    earlier = lax.broadcasted_iota(jnp.int32, (size, size), 1)
    return later >= earlier


def split_pair(pair):
    first = lax.broadcasted_iota(jnp.int32, pair.shape, 1) < PM
    zero = jnp.zeros_like(pair)
    return jnp.concatenate([jnp.where(first, pair, zero), jnp.where(first, zero, pair)], axis=0)


def kernel_call(body, outs, cost, *operands):
    flops, traffic, exps = cost
    return pl.pallas_call(
        body,
        out_shape=tuple(jax.ShapeDtypeStruct(s, d) for s, d in outs),
        in_specs=[pl.BlockSpec(memory_space=pltpu.VMEM)] * len(operands),
        out_specs=tuple(pl.BlockSpec(memory_space=pltpu.VMEM) for _ in outs),
        compiler_params=pltpu.CompilerParams(vmem_limit_bytes=40 * 1024 * 1024),
        cost_estimate=pl.CostEstimate(flops=flops, bytes_accessed=traffic, transcendentals=exps),
    )(*operands)


def scan_local(
    heads, proj_ref, taps_ref, par_ref, skip_ref, y_ref, msg_ref, x_ref, bc_ref, slope_ref, cum_ref, step_ref
):
    width = heads * PM
    conv_width = width + 2 * NS
    rows = y_ref.shape[0]
    ext = proj_ref[:, :conv_width].astype(F32)
    pre = taps_ref[KC - 1 : KC, :] * ext[HALO:]
    for k in range(KC - 1):
        pre = pre + taps_ref[k : k + 1, :] * pltpu.roll(ext, KC - 1 - k, 0)[HALO:]
    sig = sigmoid(pre)
    conv_out = pre * sig
    slope_ref[...] = sig * (1.0 + pre * (1.0 - sig))
    x = conv_out[:, :width]
    x_ref[...] = x
    bc_ref[...] = conv_out[:, width:]
    b_map = low(conv_out[:, width : width + NS])
    c_map = low(conv_out[:, width + NS :])
    raw = proj_ref[HALO:, conv_width + LANES : conv_width + 2 * LANES].astype(F32) + par_ref[0:1, :]
    lane = lax.broadcasted_iota(jnp.int32, raw.shape, 1)
    step = jnp.where(lane < heads, softplus(raw), 0.0)
    step_ref[...] = step
    causal = lower_triangle(rows)
    cum = mm(causal.astype(F32), step * par_ref[1:2, :], HIGHEST)
    cum_ref[...] = cum
    cum_t = jnp.transpose(cum)
    step_t = jnp.transpose(step)
    meet = jnp.where(causal, mm_nt(c_map, b_map), 0.0)
    for pair in range(heads // 2):
        mixing = []
        for h in (2 * pair, 2 * pair + 1):
            gap = jnp.minimum(cum[:, h : h + 1] - cum_t[h : h + 1, :], 0.0)
            mixing.append(low(meet * jnp.exp(gap) * step_t[h : h + 1, :]))
        lanes = slice(pair * LANES, (pair + 1) * LANES)
        y_ref[:, lanes] = (
            mm(jnp.concatenate(mixing, axis=1), split_pair(low(x[:, lanes])))
            + skip_ref[0:1, lanes] * x[:, lanes]
        )
    spread = head_lanes(heads)
    last = cum[rows - 1 : rows, :]
    tail = mm(jnp.exp(last - cum) * step, spread, HIGHEST)
    msg_ref[:NS, :] = low(mm_tn(b_map, low(x * tail)))
    decay = mm(jnp.exp(jnp.broadcast_to(last, (HALO, LANES))), spread, HIGHEST)
    coarse = low(decay)
    fine = low(decay - coarse.astype(F32))
    place = lax.broadcasted_iota(jnp.int32, decay.shape, 0)
    msg_ref[NS:, :] = low(jnp.where(place == 0, coarse.astype(F32), fine.astype(F32)))


def scan_back_local(
    heads, dy_ref, x_ref, bc_ref, cum_ref, step_ref, carried_ref, state_ref, skip_ref,
    dx_ref, dbc_ref, dcum_ref, dstep_ref, dskip_ref,
):
    rows = dy_ref.shape[0]
    dy = dy_ref[...]
    x = x_ref[...]
    b_map = low(bc_ref[:, :NS])
    c_map = low(bc_ref[:, NS:])
    cum = cum_ref[...]
    step = step_ref[...]
    cum_t = jnp.transpose(cum)
    step_t = jnp.transpose(step)
    causal = lower_triangle(rows)
    meet = jnp.where(causal, mm_nt(c_map, b_map), 0.0)
    lane = lax.broadcasted_iota(jnp.int32, (rows, LANES), 1)
    dmeet = jnp.zeros((rows, rows), F32)
    row_part = jnp.zeros((rows, LANES), F32)
    column_sums = []
    for pair in range(heads // 2):
        lanes = slice(pair * LANES, (pair + 1) * LANES)
        x_pair = low(x[:, lanes])
        dy_split = split_pair(low(dy[:, lanes]))
        dmix_both = mm_nt(dy_split, x_pair)
        mixing = []
        for i in range(2):
            h = 2 * pair + i
            dmix = dmix_both[i * rows : (i + 1) * rows]
            gap = jnp.minimum(cum[:, h : h + 1] - cum_t[h : h + 1, :], 0.0)
            decay = jnp.where(causal, jnp.exp(gap), 0.0)
            row_step = step_t[h : h + 1, :]
            decay_step = decay * row_step
            dmeet = dmeet + dmix * decay_step
            mixing.append(low(meet * decay_step))
            ratio = dmix * meet * decay
            column_sums.append(jnp.sum(ratio, axis=0, keepdims=True))
            row_sum = jnp.sum(ratio * row_step, axis=1, keepdims=True)
            row_part = row_part + jnp.where(lane == h, row_sum, 0.0)
        dx_ref[:, lanes] = (
            mm_tn(jnp.concatenate(mixing, axis=0), dy_split) + skip_ref[0:1, lanes] * dy[:, lanes]
        )
    column_sums.append(jnp.zeros((LANES - heads, rows), F32))
    dstep = jnp.transpose(jnp.concatenate(column_sums, axis=0))
    dstep_ref[...] = dstep
    spread = head_lanes(heads)
    weighted = dy * mm(jnp.exp(cum), spread, HIGHEST)
    dcum_ref[...] = row_part - dstep * step + mm_nt(weighted * carried_ref[...], spread, HIGHEST)
    dmeet_low = low(dmeet)
    dbc_ref[:, :NS] = mm_tn(dmeet_low, c_map)
    dbc_ref[:, NS:] = mm(dmeet_low, b_map) + mm_nt(low(weighted), low(state_ref[...]))
    dskip = jnp.broadcast_to(jnp.sum(dy * x, axis=0, keepdims=True), (8, dy.shape[1]))
    dskip_ref[...] = mm_nt(dskip, spread, HIGHEST)


def scan_back_end(
    heads, got_1, got_2, got_3, state_ref, x_ref, bc_ref, cum_ref, step_ref, dx_ref, dbc_ref, dcum_ref,
    dstep_ref, slope_ref, proj_ref, par_ref,
    dpre_ref, dbc_out_ref, ddt_ref, small_ref, dtaps_ref,
):
    width = heads * PM
    conv_width = width + 2 * NS
    rows = x_ref.shape[0]
    dstate = got_1[...].astype(F32) + got_2[...].astype(F32) + got_3[...].astype(F32)
    x = x_ref[...]
    b_map = low(bc_ref[:, :NS])
    cum = cum_ref[...]
    step = step_ref[...]
    spread = head_lanes(heads)
    last = cum[rows - 1 : rows, :]
    fade = jnp.exp(last - cum)
    tail = fade * step
    wide_tail = mm(tail, spread, HIGHEST)
    dstate_low = low(dstate)
    reach = mm(b_map, dstate_low)
    dx = dx_ref[...] + wide_tail * reach
    dbc_out_ref[:, :NS] = dbc_ref[:, :NS] + mm_nt(low(x * wide_tail), dstate_low)
    dbc_out_ref[:, NS:] = dbc_ref[:, NS:]
    value = mm_nt(x * reach, spread, HIGHEST)
    total = jnp.sum(dstate * state_ref[...], axis=0, keepdims=True)
    dtotal = mm_nt(jnp.broadcast_to(total, (8, width)), spread, HIGHEST)[0:1, :]
    held = tail * value
    at_end = jnp.exp(last) * dtotal + jnp.sum(held, axis=0, keepdims=True)
    upper = jnp.where(lower_triangle(rows), 1.0, 0.0)
    drate = mm_tn(upper, dcum_ref[...] - held, HIGHEST) + at_end
    dstep = dstep_ref[...] + fade * value + drate * par_ref[1:2, :]
    raw = proj_ref[HALO:, conv_width + LANES : conv_width + 2 * LANES].astype(F32) + par_ref[0:1, :]
    lane = lax.broadcasted_iota(jnp.int32, raw.shape, 1)
    ddt = jnp.where(lane < heads, dstep * sigmoid(raw), 0.0)
    ddt_ref[...] = low(ddt)
    dbias = jnp.sum(ddt, axis=0, keepdims=True)
    dlog = jnp.sum(drate * step, axis=0, keepdims=True) * par_ref[1:2, :]
    place = lax.broadcasted_iota(jnp.int32, (8, LANES), 0)
    small_ref[...] = jnp.where(place == 0, dbias, jnp.where(place == 1, dlog, 0.0))
    dpre = dx * slope_ref[:, :width]
    dpre_ref[...] = dpre
    ext = proj_ref[:, :width].astype(F32)
    sums = [
        jnp.sum(dpre * (pltpu.roll(ext, KC - 1 - k, 0) if k < KC - 1 else ext)[HALO:], axis=0, keepdims=True)
        for k in range(KC)
    ]
    dtaps_ref[...] = jnp.concatenate(sums + [jnp.zeros((8 - KC, width), F32)], axis=0)


def heads_to_rows(v):
    return jnp.concatenate([v[:, i * HEAD_DIM : (i + 1) * HEAD_DIM] for i in range(v.shape[1] // HEAD_DIM)], axis=0)


def rows_to_heads(v, count):
    rows = v.shape[0] // count
    return jnp.concatenate([v[i * rows : (i + 1) * rows] for i in range(count)], axis=1)


def quarter_turn(width):
    source = lax.broadcasted_iota(jnp.int32, (width, width), 0)
    target = lax.broadcasted_iota(jnp.int32, (width, width), 1)
    half = HEAD_DIM // 2
    upper = (target & (HEAD_DIM - 1)) >= half
    return jnp.where(upper & (source == target - half), 1.0, jnp.where((~upper) & (source == target + half), -1.0, 0.0))


def attend(row_ref, q_ref, cos_ref, sin_ref, key_ref, value_ref, out_ref, probs_ref, query_ref):
    row = row_ref[0]
    rows = q_ref.shape[0]
    count = q_ref.shape[1] // HEAD_DIM
    q = q_ref[...]
    turned = mm(q, low(quarter_turn(q.shape[1])))
    query = heads_to_rows(low(q.astype(F32) * cos_ref[...] + turned * sin_ref[...]))
    query_ref[...] = query
    scores = mm_nt(query, key_ref[...]) * (HEAD_DIM ** (-0.5))
    place = lax.broadcasted_iota(jnp.int32, scores.shape, 0)
    column = lax.broadcasted_iota(jnp.int32, scores.shape, 1)
    place = place & (rows - 1)
    limit = jnp.where(column < rows, place, (row + 1) * rows - 1)
    scores = jnp.where(column <= limit, scores, NEG_LARGE)
    exponent = jnp.exp(scores - jnp.max(scores, axis=1, keepdims=True))
    probs = low(exponent * (1.0 / jnp.sum(exponent, axis=1, keepdims=True)))
    probs_ref[...] = probs
    out_ref[...] = low(rows_to_heads(mm(probs, value_ref[...]), count))


def attend_back(grad_ref, probs_ref, query_ref, cos_ref, sin_ref, key_ref, value_ref, dq_ref, dk_ref, dv_ref):
    count = grad_ref.shape[1] // HEAD_DIM
    scale = HEAD_DIM ** (-0.5)
    grad = heads_to_rows(low(grad_ref[...]))
    probs_low = probs_ref[...]
    probs = probs_low.astype(F32)
    dprobs = mm_nt(grad, value_ref[...])
    delta = jnp.sum(probs * dprobs, axis=1, keepdims=True)
    dscores = low(probs * (dprobs - delta))
    dquery = rows_to_heads(mm(dscores, key_ref[...]), count) * scale
    turned = mm(dquery, quarter_turn(dquery.shape[1]), HIGHEST)
    dq_ref[...] = low(dquery * cos_ref[...] - turned * sin_ref[...])
    dk_ref[...] = mm_tn(dscores, query_ref[...]) * scale
    dv_ref[...] = mm_tn(probs_low, grad)


def send(x, axis, pairs):
    return lax.ppermute(x, axis, pairs)


def from_ahead(x, axis, distance):
    n = lax.axis_size(axis)
    return send(x, axis, [((i + distance) % n, i) for i in range(n)])


def from_earlier(x, distance):
    n = lax.axis_size("row")
    return send(x, "row", [(i - distance, i) for i in range(distance, n)])


def from_later(x, distance):
    n = lax.axis_size("row")
    return send(x, "row", [(i + distance, i) for i in range(n - distance)])


def swap(x, axis, bit):
    return send(x, axis, [(i, i ^ bit) for i in range(lax.axis_size(axis))])


def gather(shard):
    dp_n, row_n = lax.axis_size("dp"), lax.axis_size("row")
    rows = [shard] + [from_ahead(shard, "row", k) for k in range(1, row_n)]
    if dp_n == 2:
        return jnp.concatenate(rows + [from_ahead(block, "dp", 1) for block in rows], axis=0)
    group = jnp.concatenate(rows, axis=0)
    everything = lax.all_gather(group, "dp", axis=0, tiled=True)
    return jnp.roll(everything, -lax.axis_index("dp") * group.shape[0], axis=0)


def scatter(full):
    dp_n, row_n = lax.axis_size("dp"), lax.axis_size("row")
    if dp_n == 2:
        blk = full.shape[0] // (dp_n * row_n)
        sums = []
        for k in range(row_n):
            theirs = low(full[(row_n + k) * blk : (row_n + k + 1) * blk])
            sums.append(full[k * blk : (k + 1) * blk] + from_ahead(theirs, "dp", 1).astype(F32))
    else:
        group = full.shape[0] // dp_n
        ordered = jnp.roll(low(full), lax.axis_index("dp") * group, axis=0)
        mine = lax.psum_scatter(ordered, "dp", scatter_dimension=0, tiled=True).astype(F32)
        blk = group // row_n
        sums = [mine[k * blk : (k + 1) * blk] for k in range(row_n)]
    total = sums[0]
    for k in range(1, row_n):
        total = total + from_ahead(low(sums[k]), "row", row_n - k).astype(F32)
    return total


def col_sum(values):
    if lax.axis_size("col") != 4:
        return lax.psum(low(values), "col").astype(F32)
    even = lax.axis_index("col") % 2 == 0
    half = values.shape[0] // 2
    first, second = values[:half], values[half:]
    keep = jnp.where(even, first, second)
    got = swap(low(jnp.where(even, second, first)), "col", 1)
    part = low(keep + got.astype(F32))
    total = low(part.astype(F32) + swap(part, "col", 2).astype(F32))
    other = swap(total, "col", 1)
    return jnp.concatenate(
        [jnp.where(even, total, other), jnp.where(even, other, total)], axis=0
    ).astype(F32)


def tiny_col_sum(values):
    if lax.axis_size("col") != 4:
        return lax.psum(values, "col")
    values = values + swap(values, "col", 1)
    return values + swap(values, "col", 2)


def tiny_row_sum(values):
    if lax.axis_size("dp") == 2:
        values = values + swap(values, "dp", 1)
    else:
        values = lax.psum(values, "dp")
    if lax.axis_size("row") != 4:
        return lax.psum(values, "row")
    values = values + swap(values, "row", 1)
    return values + swap(values, "row", 2)


def per_device(
    tokens, cotangent, norm_in, z_weight, x_weight, dt_weight, q_weight, bc_weight, key_value_weight,
    conv_x, conv_bc, dt_bias, a_log, d_skip, gate_gain, mamba_weight, attn_weight, norm_mid,
    gate_weight, up_weight, down_weight,
):
    dp_n, row_n, col_n = (lax.axis_size(a) for a in ("dp", "row", "col"))
    dp, row, col = (lax.axis_index(a) for a in ("dp", "row", "col"))
    rows, model = tokens.shape
    seq = rows * row_n
    heads = dt_bias.shape[0]
    width = heads * PM
    q_width = q_weight.shape[1]
    q_heads = q_width // HEAD_DIM
    hidden = gate_weight.shape[1]
    blk = model // (dp_n * row_n)
    bc_part = 2 * NS // col_n
    kv_group = col * q_heads * KEY_HEADS // QUERY_HEADS
    is_value = col % 2
    kv_start = is_value * KEY_HEADS * HEAD_DIM + kv_group * HEAD_DIM

    order = [((dp + i) % dp_n) * row_n + (row + k) % row_n for i in range(dp_n) for k in range(row_n)]
    place = [((b // row_n - dp) % dp_n) * row_n + (b % row_n - row) % row_n for b in range(dp_n * row_n)]

    def arranged(v, blocks):
        axis = v.ndim - 1
        return jnp.concatenate(
            [lax.dynamic_slice_in_dim(v, b * blk, blk, axis) for b in blocks], axis=axis
        )

    shard_in = jnp.concatenate(
        [
            x_weight,
            bc_weight,
            q_weight,
            dt_weight,
            jnp.zeros((blk, HEAD_DIM - heads), BF16),
            lax.dynamic_slice_in_dim(key_value_weight, kv_start, HEAD_DIM, 1),
        ],
        axis=1,
    )
    shard_mix = jnp.concatenate([z_weight, mamba_weight.T, attn_weight.T], axis=1)
    shard_ff = jnp.concatenate([gate_weight, up_weight, down_weight.T], axis=1)
    halo = from_earlier(tokens[rows - HALO :], 1)
    full_in = gather(shard_in)
    full_mix = gather(shard_mix)
    full_ff = gather(shard_ff)
    z_full = full_mix[:, :width]
    mamba_full = full_mix[:, width : 2 * width]
    attn_full = full_mix[:, 2 * width :]
    gate_up_full = full_ff[:, : 2 * hidden]
    down_full = full_ff[:, 2 * hidden :]
    conv_width = width + 2 * NS
    at_q = conv_width
    at_dt = at_q + q_width
    at_kv = at_dt + HEAD_DIM

    gain_in = arranged(norm_in, order)
    gain_mid = arranged(norm_mid, order)
    cot_low = arranged(cotangent, order)
    ext = arranged(jnp.concatenate([halo, tokens], axis=0), order).astype(F32)
    inv_in_ext = lax.rsqrt(jnp.mean(ext * ext, axis=-1, keepdims=True) + EPSILON)
    hidden_ext = low(ext * inv_in_ext * gain_in)
    hidden_in = hidden_ext[HALO:]
    residual = ext[HALO:]
    inv_in = inv_in_ext[HALO:]
    proj = low(mm(hidden_ext, full_in))

    positions = (row * rows + jnp.arange(rows, dtype=jnp.int32)).astype(F32)
    half = HEAD_DIM // 2
    frequency = ROPE_BASE ** (-jnp.arange(half).astype(F32) / half)
    angles = positions[:, None] * frequency[None, :]
    cos_head = jnp.concatenate([jnp.cos(angles)] * 2, axis=1)
    sin_head = jnp.concatenate([jnp.sin(angles)] * 2, axis=1)
    cos_q = jnp.concatenate([cos_head] * q_heads, axis=1)
    sin_q = jnp.concatenate([sin_head] * q_heads, axis=1)
    cos_own = jnp.where(is_value == 1, 1.0, cos_head)
    sin_own = jnp.where(is_value == 1, 0.0, sin_head)

    def turn(v, sine):
        other = jnp.concatenate([-v[:, half:], v[:, :half]], axis=1)
        return v * cos_own + other * sine

    kv_own = low(turn(proj[HALO:, at_kv : at_kv + HEAD_DIM].astype(F32), sin_own))
    kv_mine = jnp.concatenate([kv_own] + [from_earlier(kv_own, j) for j in range(1, row_n)], axis=0)
    kv_other = swap(kv_mine, "col", 1)
    key = jnp.where(is_value == 1, kv_other, kv_mine)
    value = jnp.where(is_value == 1, kv_mine, kv_other)

    taps = jnp.concatenate([conv_x, conv_bc], axis=1)
    rate = -jnp.exp(a_log)

    def lane_row(v):
        return jnp.pad(v, (0, LANES - heads))[None, :]

    params = jnp.concatenate([lane_row(dt_bias), lane_row(rate), jnp.zeros((6, LANES), F32)], axis=0)
    skip = jnp.repeat(d_skip, PM)[None, :]
    area = rows * rows * heads
    y_base, msg, x_heads, bc_map, slope, cum, step = kernel_call(
        partial(scan_local, heads),
        (
            ((rows, width), F32),
            ((NS + HALO, width), BF16),
            ((rows, width), F32),
            ((rows, 2 * NS), F32),
            ((rows, conv_width), F32),
            ((rows, LANES), F32),
            ((rows, LANES), F32),
        ),
        (area * 2 * PM * 10, 4000000, area),
        proj,
        taps,
        params,
        skip,
    )
    msgs = [from_earlier(msg, j) for j in range(1, row_n)]

    row_ref = jnp.reshape(row, (1,)).astype(jnp.int32)
    q_low = proj[HALO:, at_q : at_q + q_width]
    attn_value, probs, query = pl.pallas_call(
        attend,
        out_shape=(
            jax.ShapeDtypeStruct((rows, q_width), BF16),
            jax.ShapeDtypeStruct((q_heads * rows, seq), BF16),
            jax.ShapeDtypeStruct((q_heads * rows, HEAD_DIM), BF16),
        ),
        in_specs=[pl.BlockSpec(memory_space=pltpu.SMEM)] + [pl.BlockSpec(memory_space=pltpu.VMEM)] * 5,
        out_specs=tuple(pl.BlockSpec(memory_space=pltpu.VMEM) for _ in range(3)),
        compiler_params=pltpu.CompilerParams(vmem_limit_bytes=40 * 1024 * 1024),
        cost_estimate=pl.CostEstimate(
            flops=4 * q_width * rows * seq * 2, bytes_accessed=4000000, transcendentals=q_heads * rows * seq
        ),
    )(row_ref, q_low, cos_q, sin_q, key, value)

    decays = [m[NS].astype(F32) + m[NS + 1].astype(F32) for m in msgs]
    state_in = msgs[-1][:NS].astype(F32)
    for j in range(row_n - 3, -1, -1):
        state_in = msgs[j][:NS].astype(F32) + decays[j] * state_in
    c_low = low(bc_map[:, NS:])
    wide_decay = jnp.repeat(jnp.exp(cum[:, :heads]), PM, axis=1)
    carried = mm(c_low, low(state_in))
    y = y_base + wide_decay * carried
    z_value = low(mm(hidden_in, z_full)).astype(F32)
    z_sig = sigmoid(z_value)
    gated = y * (z_value * z_sig)
    square_sum = tiny_col_sum(jnp.sum(gated * gated, axis=1))
    inv_gate = lax.rsqrt(square_sum / (HM * PM) + EPSILON)[:, None]
    mamba_normed = low(gated * inv_gate * gate_gain)
    mixed = col_sum(mm_nt(mamba_normed, mamba_full) + mm_nt(attn_value, attn_full))

    middle = residual + mixed
    inv_mid = lax.rsqrt(jnp.mean(middle * middle, axis=-1, keepdims=True) + EPSILON)
    mid_rows = middle * inv_mid
    hidden_mid = low(mid_rows * gain_mid)
    gate_up = low(mm(hidden_mid, gate_up_full)).astype(F32)
    gate_value, up_value = gate_up[:, :hidden], gate_up[:, hidden:]
    gate_sig = sigmoid(gate_value)
    swiglu = low(gate_value * gate_sig * up_value)
    grad_swiglu = mm(cot_low, down_full)
    grad_gate = low(grad_swiglu * up_value * gate_sig * (1.0 + gate_value * (1.0 - gate_sig)))
    grad_up = low(grad_swiglu * gate_value * gate_sig)
    grad_gate_up = jnp.concatenate([grad_gate, grad_up], axis=1)
    grad_hidden_mid = col_sum(mm_nt(grad_gate_up, gate_up_full))
    grad_out = cot_low.astype(F32)
    grad_norm_mid = jnp.sum(grad_hidden_mid * mid_rows, axis=0)
    scaled_mid = grad_hidden_mid * gain_mid
    grad_middle = grad_out + inv_mid * (
        scaled_mid - mid_rows * jnp.mean(scaled_mid * mid_rows, axis=-1, keepdims=True)
    )
    grad_mix = low(grad_middle)
    layer_out = low(middle + col_sum(mm_nt(swiglu, down_full)))

    grad_ff = scatter(
        jnp.concatenate([mm_tn(hidden_mid, grad_gate_up), mm_tn(cot_low, swiglu)], axis=1)
    )

    grad_normed = mm(grad_mix, mamba_full)
    grad_attn = mm(grad_mix, attn_full)
    scaled_grad = grad_normed * gate_gain
    cross = tiny_col_sum(jnp.sum(scaled_grad * gated, axis=1))[:, None]
    grad_gain = jnp.sum(grad_normed * gated * inv_gate, axis=0)
    grad_query, grad_key, grad_value = kernel_call(
        attend_back,
        (
            ((rows, q_width), BF16),
            ((seq, HEAD_DIM), F32),
            ((seq, HEAD_DIM), F32),
        ),
        (8 * q_width * rows * seq * 2, 4000000, 0),
        grad_attn,
        probs,
        query,
        cos_q,
        sin_q,
        key,
        value,
    )
    kept = jnp.where(is_value == 1, grad_value, grad_key)
    given = jnp.where(is_value == 1, grad_key, grad_value)
    grad_kv_rows = kept + swap(low(given), "col", 1).astype(F32)
    grad_kv = grad_kv_rows[:rows]
    for j in range(1, row_n):
        grad_kv = grad_kv + from_later(low(grad_kv_rows[j * rows : (j + 1) * rows]), j).astype(F32)
    grad_kv = low(turn(grad_kv, -sin_own))

    grad_gated = inv_gate * scaled_grad - gated * (inv_gate * inv_gate * inv_gate * cross / (HM * PM))
    grad_y = grad_gated * (z_value * z_sig)
    grad_z = low(grad_gated * y * z_sig * (1.0 + z_value * (1.0 - z_sig)))
    grad_state = mm_tn(c_low, low(wide_decay * grad_y))
    got = []
    for j in range(1, row_n):
        got.append(from_later(low(grad_state), j))
        grad_state = grad_state * decays[j - 1]
    dx_local, dbc_local, dcum, dstep, dskip = kernel_call(
        partial(scan_back_local, heads),
        (
            ((rows, width), F32),
            ((rows, 2 * NS), F32),
            ((rows, LANES), F32),
            ((rows, LANES), F32),
            ((8, LANES), F32),
        ),
        (area * 2 * PM * 20, 4000000, area),
        grad_y,
        x_heads,
        bc_map,
        cum,
        step,
        carried,
        state_in,
        skip,
    )
    grad_mix_w = scatter(mm_tn(grad_mix, jnp.concatenate([mamba_normed, attn_value], axis=1)))
    grad_zqk = jnp.concatenate([grad_z, grad_query, grad_kv], axis=1)
    grad_zqk_w = scatter(mm_tn(hidden_in, grad_zqk))

    dpre_x, dbc, grad_dt, dsmall, dtaps_x = kernel_call(
        partial(scan_back_end, heads),
        (
            ((rows, width), F32),
            ((rows, 2 * NS), F32),
            ((rows, LANES), BF16),
            ((8, LANES), F32),
            ((8, width), F32),
        ),
        (rows * NS * width * 10, 4000000, rows * LANES * 3),
        got[0],
        got[1],
        got[2],
        state_in,
        x_heads,
        bc_map,
        cum,
        step,
        dx_local,
        dbc_local,
        dcum,
        dstep,
        slope,
        proj,
        params,
    )

    def conv_back(dpre, weights):
        following = from_later(dpre[:8], 1)
        longer = jnp.concatenate([dpre, following], axis=0)
        total = weights[KC - 1][None, :] * dpre
        for k in range(KC - 1):
            total = total + weights[k][None, :] * longer[KC - 1 - k : KC - 1 - k + rows]
        return low(total)

    grad_x = conv_back(dpre_x, conv_x)
    dpre_bc = col_sum(dbc) * slope[:, width:]
    grad_bc = conv_back(dpre_bc, conv_bc)
    bc_ext = proj[:, width:conv_width].astype(F32)
    dtaps_bc = jnp.stack(
        [
            jnp.sum(dpre_bc * bc_ext[HALO - (KC - 1) + k : HALO - (KC - 1) + k + rows], axis=0)
            for k in range(KC)
        ]
    )

    grad_dt = grad_dt[:, :HEAD_DIM]
    input_part = (
        mm_nt(grad_z, z_full)
        + mm_nt(grad_x, full_in[:, :width])
        + mm_nt(
            jnp.concatenate([grad_query, grad_dt, grad_kv], axis=1), full_in[:, at_q : at_kv + HEAD_DIM]
        )
    )
    grad_hidden_in = col_sum(input_part) + mm_nt(grad_bc, full_in[:, width:conv_width])
    in_rows = residual * inv_in
    grad_norm_in = jnp.sum(grad_hidden_in * in_rows, axis=0)
    scaled_in = grad_hidden_in * gain_in
    grad_tokens = grad_middle + inv_in * (
        scaled_in - in_rows * jnp.mean(scaled_in * in_rows, axis=-1, keepdims=True)
    )

    bc_own = lax.dynamic_slice_in_dim(grad_bc, col * bc_part, bc_part, 1)
    grad_in_w = scatter(mm_tn(hidden_in, jnp.concatenate([grad_x, bc_own, grad_dt], axis=1)))

    shared = jnp.concatenate(
        [grad_in_w[:, width : width + bc_part], grad_zqk_w[:, width + q_width :]], axis=1
    )
    if col_n == 4:
        pair = jnp.stack([shared, swap(shared, "col", 1)])
        both = jnp.concatenate([pair, swap(pair, "col", 2)], axis=0)
        pieces = [lax.dynamic_index_in_dim(both, c ^ col, 0, False) for c in range(col_n)]
    else:
        both = lax.all_gather(shared, "col")
        pieces = [both[c] for c in range(col_n)]
    grad_bc_w = jnp.concatenate([p[:, :bc_part] for p in pieces], axis=1)
    keys_first = [pieces[c] for c in range(0, col_n, 2)] + [pieces[c] for c in range(1, col_n, 2)]
    grad_kv_w = jnp.concatenate([p[:, bc_part:] for p in keys_first], axis=1)

    small = jnp.concatenate(
        [
            arranged(grad_norm_in, place),
            arranged(grad_norm_mid, place),
            dtaps_x[:KC].reshape(-1),
            dtaps_bc.reshape(-1),
            grad_gain,
            dsmall[0],
            dsmall[1],
            dskip[0],
        ]
    )
    small = tiny_row_sum(small.reshape(-1, LANES)).reshape(-1)
    cuts = [model, model, KC * width, KC * 2 * NS, width, LANES, LANES, LANES]
    parts = []
    start = 0
    for size in cuts:
        parts.append(small[start : start + size])
        start += size
    return (
        arranged(layer_out, place),
        arranged(grad_tokens, place),
        parts[0],
        grad_zqk_w[:, :width],
        grad_in_w[:, :width],
        grad_in_w[:, width + bc_part : width + bc_part + heads],
        grad_zqk_w[:, width : width + q_width],
        grad_bc_w,
        grad_kv_w,
        parts[2].reshape(KC, width),
        parts[3].reshape(KC, 2 * NS),
        parts[5][:heads],
        parts[6][:heads],
        parts[7][:heads],
        parts[4],
        grad_mix_w[:, :width].T,
        grad_mix_w[:, width:].T,
        parts[1],
        grad_ff[:, :hidden],
        grad_ff[:, hidden : 2 * hidden],
        grad_ff[:, 2 * hidden :].T,
    )


def solution(mesh):
    by_rows = P(("dp", "row"), None)
    both = P(("dp", "row"), "col")
    turned = P("col", ("dp", "row"))
    per_col = P("col")
    taps = P(None, "col")
    in_specs = (
        by_rows, by_rows, P(), both, both, both, both, by_rows, by_rows, taps, P(), per_col, per_col,
        per_col, per_col, turned, turned, P(), both, both, turned,
    )
    out_specs = (
        by_rows, by_rows, P(), both, both, both, both, by_rows, by_rows, taps, P(), per_col, per_col,
        per_col, per_col, turned, turned, P(), both, both, turned,
    )
    return jax.shard_map(
        per_device, mesh=mesh, in_specs=in_specs, out_specs=out_specs, check_vma=False
    )
```

```python
from functools import partial

import jax
import jax.numpy as jnp
from jax import lax
from jax.experimental import pallas as pl
from jax.experimental.pallas import tpu as pltpu
from jax.sharding import PartitionSpec as P

HM = 24
PM = 64
NS = 128
KC = 4
QUERY_HEADS = 8
KEY_HEADS = 2
HEAD_DIM = 64
HALO = 16
LANES = 128

EPSILON = 1e-05
ROPE_BASE = 100000000000.0
NEG_LARGE = -1e30
HIGHEST = lax.Precision.HIGHEST
F32 = jnp.float32
BF16 = jnp.bfloat16


def mm(a, b, precision=None):
    return lax.dot_general(
        a, b, (((1,), (0,)), ((), ())), precision=precision, preferred_element_type=F32
    )


def mm_nt(a, b, precision=None):
    return lax.dot_general(
        a, b, (((1,), (1,)), ((), ())), precision=precision, preferred_element_type=F32
    )


def mm_tn(a, b, precision=None):
    return lax.dot_general(
        a, b, (((0,), (0,)), ((), ())), precision=precision, preferred_element_type=F32
    )


def low(v):
    return v.astype(BF16)


def sigmoid(v):
    return 1.0 / (1.0 + jnp.exp(-v))


def softplus(v):
    return jnp.maximum(v, 0.0) + jnp.log1p(jnp.exp(-jnp.abs(v)))


def head_lanes(heads):
    head = lax.broadcasted_iota(jnp.int32, (LANES, heads * PM), 0)
    column = lax.broadcasted_iota(jnp.int32, (LANES, heads * PM), 1)
    return ((column >= head * PM) & (column < head * PM + PM)).astype(F32)


def lower_triangle(size):
    later = lax.broadcasted_iota(jnp.int32, (size, size), 0)
    earlier = lax.broadcasted_iota(jnp.int32, (size, size), 1)
    return later >= earlier


def split_pair(pair):
    first = lax.broadcasted_iota(jnp.int32, pair.shape, 1) < PM
    zero = jnp.zeros_like(pair)
    return jnp.concatenate([jnp.where(first, pair, zero), jnp.where(first, zero, pair)], axis=0)


def kernel_call(body, outs, cost, scalars, *operands, keep=False):
    flops, traffic, exps = cost
    flat, in_specs, scratch, plan = [], [], [], []
    if scalars is not None:
        flat.append(scalars)
        in_specs.append(pl.BlockSpec(memory_space=pltpu.SMEM))
    for operand in operands:
        parts = operand if isinstance(operand, list) else [operand]
        plan.append((len(flat), len(parts), isinstance(operand, list)))
        flat += parts
        space = pltpu.HBM if isinstance(operand, list) else pltpu.VMEM
        in_specs += [pl.BlockSpec(memory_space=space)] * len(parts)
        if isinstance(operand, list):
            whole = (sum(v.shape[0] for v in parts), parts[0].shape[1])
            scratch.append(pltpu.VMEM(whole, parts[0].dtype))
            last = (whole, parts[0].dtype)
    if keep:
        scratch.pop()
        outs = tuple(outs) + (last,)
    copied = sum(n for _, n, outside in plan if outside)
    if copied:
        scratch.append(pltpu.SemaphoreType.DMA((copied,)))

    def run(*refs):
        ins, results, held = refs[: len(flat)], refs[len(flat) : len(flat) + len(outs)], refs[len(flat) + len(outs) :]
        views = [ins[0]] if scalars is not None else []
        copies, taken = [], 0
        for start, n, outside in plan:
            if not outside:
                views.append(ins[start])
                continue
            target = results[-1] if keep and taken == len(scratch) - 1 else held[taken]
            taken += 1
            views.append(target)
            for i in range(n):
                size = ins[start + i].shape[0]
                place = target if n == 1 else target.at[lanes_of(ins[0], i, size), :]
                copies.append(pltpu.make_async_copy(ins[start + i], place, held[-1].at[len(copies)]))
        for c in copies:
            c.start()
        for c in copies:
            c.wait()
        body(*views, *(results[:-1] if keep else results))

    return pl.pallas_call(
        run,
        out_shape=tuple(jax.ShapeDtypeStruct(s, d) for s, d in outs),
        in_specs=in_specs,
        out_specs=tuple(pl.BlockSpec(memory_space=pltpu.VMEM) for _ in outs),
        scratch_shapes=scratch,
        compiler_params=pltpu.CompilerParams(vmem_limit_bytes=24 * 1024 * 1024),
        cost_estimate=pl.CostEstimate(flops=flops, bytes_accessed=traffic, transcendentals=exps),
    )(*flat)


def lanes_of(scalars, p, size):
    return pl.ds(pl.multiple_of(scalars[p] * size, size), size)


def rows_half(parity, rows, own):
    half = rows // 2
    return pl.ds(pl.multiple_of((parity if own else 1 - parity) * half, half), half)


def halves_to_sum(parity, full_ref, keep_ref, give_ref):
    rows = full_ref.shape[0]
    keep_ref[...] = full_ref[rows_half(parity, rows, True), :]
    give_ref[...] = low(full_ref[rows_half(parity, rows, False), :])


def halves_joined(parity, total_ref, other_ref, full_ref):
    rows = full_ref.shape[0]
    full_ref[rows_half(parity, rows, True), :] = total_ref[...].astype(F32)
    full_ref[rows_half(parity, rows, False), :] = other_ref[...].astype(F32)


def pack_rows(v, width):
    count = width // HEAD_DIM
    chunk = packed_rows(v.shape[0], width)
    pieces = []
    for i in range(count):
        piece = v[i * chunk : min((i + 1) * chunk, v.shape[0])]
        if piece.shape[0] < chunk:
            piece = jnp.concatenate([piece, jnp.zeros((chunk - piece.shape[0], HEAD_DIM), v.dtype)], axis=0)
        pieces.append(piece)
    return jnp.concatenate(pieces, axis=1)


def packed_rows(rows, width):
    count = width // HEAD_DIM
    return -(-rows // (16 * count)) * 16


def unpack_rows(v, rows):
    count = v.shape[1] // HEAD_DIM
    return jnp.concatenate([v[:, i * HEAD_DIM : (i + 1) * HEAD_DIM] for i in range(count)], axis=0)[:rows]


def token_sums(v):
    return mm_nt(jnp.ones((8, v.shape[1]), F32), v, HIGHEST)


def as_column(v):
    return jnp.transpose(v)[:, :1]


def scan_local(
    heads, scalars, hidden_ref, taps_ref, par_ref, skip_ref, cos_ref, sin_ref, w_ref,
    y_ref, msg_ref, proj_ref, x_ref, bc_ref, slope_ref, cum_ref, step_ref,
):
    width = heads * PM
    conv_width = width + 2 * NS
    rows = y_ref.shape[0]
    proj = low(mm(hidden_ref[...], w_ref[...]))
    proj_ref[...] = proj
    ext = proj[:, :conv_width].astype(F32)
    pre = taps_ref[KC - 1 : KC, :] * ext[HALO:]
    for k in range(KC - 1):
        pre = pre + taps_ref[k : k + 1, :] * pltpu.roll(ext, KC - 1 - k, 0)[HALO:]
    sig = sigmoid(pre)
    conv_out = pre * sig
    slope_ref[...] = sig * (1.0 + pre * (1.0 - sig))
    x = conv_out[:, :width]
    x_ref[...] = x
    bc_ref[...] = conv_out[:, width:]
    b_map = low(conv_out[:, width : width + NS])
    c_map = low(conv_out[:, width + NS :])
    raw = proj[HALO:, conv_width + LANES :].astype(F32) + par_ref[0:1, :]
    lane = lax.broadcasted_iota(jnp.int32, raw.shape, 1)
    step = jnp.where(lane < heads, softplus(raw), 0.0)
    step_ref[...] = step
    causal = lower_triangle(rows)
    cum = mm(causal.astype(F32), step * par_ref[1:2, :], HIGHEST)
    cum_ref[...] = cum
    spread = head_lanes(heads)
    last = cum[rows - 1 : rows, :]
    tail = mm(jnp.exp(last - cum) * step, spread, HIGHEST)
    msg_ref[:NS, :] = low(mm_tn(b_map, low(x * tail)))
    decay = mm(jnp.exp(jnp.broadcast_to(last, (HALO, LANES))), spread, HIGHEST)
    coarse = low(decay)
    fine = low(decay - coarse.astype(F32))
    place = lax.broadcasted_iota(jnp.int32, decay.shape, 0)
    msg_ref[NS : NS + HALO, :] = low(jnp.where(place == 0, coarse.astype(F32), fine.astype(F32)))
    kv = proj[HALO:, conv_width : conv_width + LANES]
    turned = mm(kv, low(quarter_turn(LANES)))
    kv = low(kv.astype(F32) * cos_ref[...] + turned * sin_ref[...])
    part = packed_rows(rows, width)
    at = NS + HALO
    msg_ref[at : at + part, :] = pack_rows(kv[:, :HEAD_DIM], width)
    msg_ref[at + part : at + 2 * part, :] = pack_rows(kv[:, HEAD_DIM:], width)
    cum_t = jnp.transpose(cum)
    step_t = jnp.transpose(step)
    meet = jnp.where(causal, mm_nt(c_map, b_map), 0.0)
    for pair in range(heads // 2):
        mixing = []
        for h in (2 * pair, 2 * pair + 1):
            gap = jnp.minimum(cum[:, h : h + 1] - cum_t[h : h + 1, :], 0.0)
            mixing.append(low(meet * jnp.exp(gap) * step_t[h : h + 1, :]))
        lanes = slice(pair * LANES, (pair + 1) * LANES)
        y_ref[:, lanes] = (
            mm(jnp.concatenate(mixing, axis=1), split_pair(low(x[:, lanes])))
            + skip_ref[0:1, lanes] * x[:, lanes]
        )


def scan_back_local(
    heads, dy_ref, x_ref, bc_ref, cum_ref, step_ref, carried_ref, state_ref, skip_ref,
    dx_ref, dbc_ref, dcum_ref, dstep_ref, dskip_ref,
):
    rows = dy_ref.shape[0]
    dy = dy_ref[...]
    x = x_ref[...]
    b_map = low(bc_ref[:, :NS])
    c_map = low(bc_ref[:, NS:])
    cum = cum_ref[...]
    step = step_ref[...]
    cum_t = jnp.transpose(cum)
    step_t = jnp.transpose(step)
    causal = lower_triangle(rows)
    meet = jnp.where(causal, mm_nt(c_map, b_map), 0.0)
    lane = lax.broadcasted_iota(jnp.int32, (rows, LANES), 1)
    dmeet = jnp.zeros((rows, rows), F32)
    row_part = jnp.zeros((rows, LANES), F32)
    column_sums = []
    for pair in range(heads // 2):
        lanes = slice(pair * LANES, (pair + 1) * LANES)
        x_pair = low(x[:, lanes])
        dy_split = split_pair(low(dy[:, lanes]))
        dmix_both = mm_nt(dy_split, x_pair)
        mixing = []
        for i in range(2):
            h = 2 * pair + i
            dmix = dmix_both[i * rows : (i + 1) * rows]
            gap = jnp.minimum(cum[:, h : h + 1] - cum_t[h : h + 1, :], 0.0)
            decay = jnp.where(causal, jnp.exp(gap), 0.0)
            row_step = step_t[h : h + 1, :]
            decay_step = decay * row_step
            dmeet = dmeet + dmix * decay_step
            mixing.append(low(meet * decay_step))
            ratio = dmix * meet * decay
            column_sums.append(jnp.sum(ratio, axis=0, keepdims=True))
            row_sum = jnp.sum(ratio * row_step, axis=1, keepdims=True)
            row_part = row_part + jnp.where(lane == h, row_sum, 0.0)
        dx_ref[:, lanes] = (
            mm_tn(jnp.concatenate(mixing, axis=0), dy_split) + skip_ref[0:1, lanes] * dy[:, lanes]
        )
    column_sums.append(jnp.zeros((LANES - heads, rows), F32))
    dstep = jnp.transpose(jnp.concatenate(column_sums, axis=0))
    dstep_ref[...] = dstep
    spread = head_lanes(heads)
    weighted = dy * mm(jnp.exp(cum), spread, HIGHEST)
    dcum_ref[...] = row_part - dstep * step + mm_nt(weighted * carried_ref[...], spread, HIGHEST)
    dmeet_low = low(dmeet)
    dbc_ref[:, :NS] = mm_tn(dmeet_low, c_map)
    dbc_ref[:, NS:] = mm(dmeet_low, b_map) + mm_nt(low(weighted), low(state_ref[...]))
    dskip = jnp.broadcast_to(jnp.sum(dy * x, axis=0, keepdims=True), (8, dy.shape[1]))
    dskip_ref[...] = mm_nt(dskip, spread, HIGHEST)


def scan_back_end(
    heads, count, *refs
):
    got = refs[:count]
    (
        state_ref, x_ref, bc_ref, cum_ref, step_ref, dx_ref, dbc_ref, dcum_ref, dstep_ref, slope_ref,
        proj_ref, par_ref, dkv_ref, cos_ref, sin_ref,
        dpre_ref, first_ref, ddt_ref, dkv_out_ref, small_ref, dtaps_ref,
    ) = refs[count:]
    width = heads * PM
    conv_width = width + 2 * NS
    rows = x_ref.shape[0]
    part = packed_rows(rows, width)
    dkv = dkv_ref[...]
    dstate = jnp.zeros((NS, width), F32)
    for g in got:
        dstate = dstate + g[:NS, :].astype(F32)
        key = unpack_rows(g[NS : NS + part, :], rows)
        value = unpack_rows(g[NS + part : NS + 2 * part, :], rows)
        dkv = dkv + jnp.concatenate([key, value], axis=1).astype(F32)
    turned = mm(dkv, quarter_turn(LANES), HIGHEST)
    dkv_out_ref[...] = low(dkv * cos_ref[...] - turned * sin_ref[...])
    x = x_ref[...]
    b_map = low(bc_ref[:, :NS])
    cum = cum_ref[...]
    step = step_ref[...]
    spread = head_lanes(heads)
    last = cum[rows - 1 : rows, :]
    fade = jnp.exp(last - cum)
    tail = fade * step
    wide_tail = mm(tail, spread, HIGHEST)
    dstate_low = low(dstate)
    reach = mm(b_map, dstate_low)
    dx = dx_ref[...] + wide_tail * reach
    db = dbc_ref[:, :NS] + mm_nt(low(x * wide_tail), dstate_low)
    value = mm_nt(x * reach, spread, HIGHEST)
    total = jnp.sum(dstate * state_ref[...], axis=0, keepdims=True)
    dtotal = mm_nt(jnp.broadcast_to(total, (8, width)), spread, HIGHEST)[0:1, :]
    held = tail * value
    at_end = jnp.exp(last) * dtotal + jnp.sum(held, axis=0, keepdims=True)
    upper = jnp.where(lower_triangle(rows), 1.0, 0.0)
    drate = mm_tn(upper, dcum_ref[...] - held, HIGHEST) + at_end
    dstep = dstep_ref[...] + fade * value + drate * par_ref[1:2, :]
    raw = proj_ref[HALO:, conv_width + LANES :].astype(F32) + par_ref[0:1, :]
    lane = lax.broadcasted_iota(jnp.int32, raw.shape, 1)
    ddt = jnp.where(lane < heads, dstep * sigmoid(raw), 0.0)
    ddt_ref[...] = low(ddt)
    dbias = jnp.sum(ddt, axis=0, keepdims=True)
    dlog = jnp.sum(drate * step, axis=0, keepdims=True) * par_ref[1:2, :]
    place = lax.broadcasted_iota(jnp.int32, (8, LANES), 0)
    small_ref[...] = jnp.where(place == 0, dbias, jnp.where(place == 1, dlog, 0.0))
    dpre = jnp.concatenate([dx, db, dbc_ref[:, NS:]], axis=1) * slope_ref[...]
    dpre_ref[...] = dpre
    first_ref[...] = dpre[:8]
    ext = proj_ref[:, :conv_width].astype(F32)
    sums = [
        jnp.sum(dpre * (pltpu.roll(ext, KC - 1 - k, 0) if k < KC - 1 else ext)[HALO:], axis=0, keepdims=True)
        for k in range(KC)
    ]
    dtaps_ref[...] = jnp.concatenate(sums + [jnp.zeros((8 - KC, conv_width), F32)], axis=0)


def heads_to_rows(v):
    return jnp.concatenate([v[:, i * HEAD_DIM : (i + 1) * HEAD_DIM] for i in range(v.shape[1] // HEAD_DIM)], axis=0)


def rows_to_heads(v, count):
    rows = v.shape[0] // count
    return jnp.concatenate([v[i * rows : (i + 1) * rows] for i in range(count)], axis=1)


def quarter_turn(width):
    source = lax.broadcasted_iota(jnp.int32, (width, width), 0)
    target = lax.broadcasted_iota(jnp.int32, (width, width), 1)
    half = HEAD_DIM // 2
    upper = (target & (HEAD_DIM - 1)) >= half
    from_first = jnp.where(source == target - half, 1.0, 0.0)
    from_second = jnp.where(source == target + half, -1.0, 0.0)
    return jnp.where(upper, from_first, from_second)


def mix_tokens(
    heads, count, scalars, own_ref, *refs
):
    msgs = refs[:count]
    (
        y_ref, cum_ref, bc_ref, zq_ref, cos_ref, sin_ref,
        out_ref, probs_ref, query_ref, key_ref, value_ref, state_ref, carried_ref, y_out_ref, gated_ref, sums_ref,
    ) = refs[count:]
    row = scalars[scalars.shape[0] - 1]
    rows, width = y_ref.shape
    at = NS + HALO
    part = packed_rows(rows, width)
    everyone = (own_ref,) + msgs
    key = jnp.concatenate([unpack_rows(m[at : at + part, :], rows) for m in everyone], axis=0)
    value = jnp.concatenate([unpack_rows(m[at + part : at + 2 * part, :], rows) for m in everyone], axis=0)
    key_ref[...] = key
    value_ref[...] = value

    state = msgs[-1][:NS, :].astype(F32)
    for m in reversed(msgs[:-1]):
        decay = m[NS : NS + HALO, :].astype(F32)
        state = m[:NS, :].astype(F32) + (decay[0:1, :] + decay[1:2, :]) * state
    state_ref[...] = state
    carried = mm(low(bc_ref[:, NS:]), low(state))
    carried_ref[...] = carried
    y = y_ref[...] + mm(jnp.exp(cum_ref[...]), head_lanes(heads), HIGHEST) * carried
    y_out_ref[...] = y
    z = zq_ref[:, :width].astype(F32)
    gated = y * (z * sigmoid(z))
    gated_ref[...] = gated
    sums_ref[...] = token_sums(gated * gated)

    q = zq_ref[:, width:]
    q_heads = q.shape[1] // HEAD_DIM
    turned = mm(q, low(quarter_turn(q.shape[1])))
    query = heads_to_rows(low(q.astype(F32) * cos_ref[...] + turned * sin_ref[...]))
    query_ref[...] = query
    scores = mm_nt(query, key) * (HEAD_DIM ** (-0.5))
    place = lax.broadcasted_iota(jnp.int32, scores.shape, 0)
    column = lax.broadcasted_iota(jnp.int32, scores.shape, 1)
    place = place & (rows - 1)
    limit = jnp.where(column < rows, place, (row + 1) * rows - 1)
    scores = jnp.where(column <= limit, scores, NEG_LARGE)
    exponent = jnp.exp(scores - jnp.max(scores, axis=1, keepdims=True))
    probs = low(exponent * (1.0 / jnp.sum(exponent, axis=1, keepdims=True)))
    probs_ref[...] = probs
    out_ref[...] = low(rows_to_heads(mm(probs, value), q_heads))


def attend_back(grad_ref, probs_ref, query_ref, cos_ref, sin_ref, key_ref, value_ref, dq_ref, dkv_ref, *sent):
    count = grad_ref.shape[1] // HEAD_DIM
    rows = dkv_ref.shape[0]
    scale = HEAD_DIM ** (-0.5)
    grad = heads_to_rows(grad_ref[...])
    probs_low = probs_ref[...]
    probs = probs_low.astype(F32)
    dprobs = mm_nt(grad, value_ref[...])
    delta = jnp.sum(probs * dprobs, axis=1, keepdims=True)
    dscores = low(probs * (dprobs - delta))
    dquery = rows_to_heads(mm(dscores, key_ref[...]), count) * scale
    turned = mm(dquery, quarter_turn(dquery.shape[1]), HIGHEST)
    dq_ref[...] = low(dquery * cos_ref[...] - turned * sin_ref[...])
    dkey = mm_tn(dscores, query_ref[...]) * scale
    dvalue = mm_tn(probs_low, grad)
    dkv_ref[...] = jnp.concatenate([dkey[:rows], dvalue[:rows]], axis=1)
    for j, out in enumerate(sent):
        at = slice((j + 1) * rows, (j + 2) * rows)
        part = packed_rows(rows, out.shape[1])
        out[:part, :] = pack_rows(low(dkey[at]), out.shape[1])
        out[part:, :] = pack_rows(low(dvalue[at]), out.shape[1])


def project(scalars, hidden_ref, w_ref, out_ref):
    out_ref[...] = low(mm(hidden_ref[...], w_ref[:, : out_ref.shape[1]]))


def mix_out(
    total_heads, scalars, sums_ref, gated_ref, gain_ref, attn_ref, w_ref, normed_ref, keep_ref, give_ref, full_ref
):
    parity = scalars[scalars.shape[0] - 2]
    inv = as_column(lax.rsqrt(sums_ref[...] / (total_heads * PM) + EPSILON))
    normed = low(gated_ref[...] * inv * gain_ref[...])
    normed_ref[...] = normed
    act = jnp.concatenate([normed, attn_ref[...]], axis=1)
    full_ref[...] = mm_nt(act, w_ref[:, w_ref.shape[1] - act.shape[1] :])
    halves_to_sum(parity, full_ref, keep_ref, give_ref)


def feed_forward(
    scalars, total_ref, other_ref, tokens_ref, cot_ref, gain_ref, w_ref,
    middle_ref, hidden_ref, dgu_ref, swiglu_ref, keep_ref, give_ref, out_keep_ref, out_give_ref, full_ref,
):
    parity = scalars[scalars.shape[0] - 2]
    halves_joined(parity, total_ref, other_ref, full_ref)
    middle = tokens_ref[...].astype(F32) + full_ref[...]
    middle_ref[...] = middle
    inv = lax.rsqrt(jnp.mean(middle * middle, axis=-1, keepdims=True) + EPSILON)
    hidden_ref[...] = low(middle * inv * gain_ref[...])
    width = swiglu_ref.shape[1]
    gate_up = low(mm(hidden_ref[...], w_ref[:, : 2 * width])).astype(F32)
    gate, up = gate_up[:, :width], gate_up[:, width:]
    sig = sigmoid(gate)
    swish = gate * sig
    swiglu = low(swish * up)
    swiglu_ref[...] = swiglu
    grad = mm(cot_ref[...], w_ref[:, 2 * width :])
    dgate = low(grad * up * sig * (1.0 + gate * (1.0 - sig)))
    dup = low(grad * swish)
    dgu = jnp.concatenate([dgate, dup], axis=1)
    dgu_ref[...] = dgu
    full_ref[...] = mm_nt(dgu, w_ref[:, : 2 * width])
    halves_to_sum(parity, full_ref, keep_ref, give_ref)
    full_ref[...] = mm_nt(swiglu, w_ref[:, 2 * width :])
    halves_to_sum(parity, full_ref, out_keep_ref, out_give_ref)


def weight_products(count, scalars, *refs):
    outs = 1 if count == 1 else 2
    pairs, results = refs[:-outs], refs[-outs:]
    size = pairs[0].shape[1] // count
    for p in range(count):
        out = results[p * outs // count]
        rows = slice((p % (count // outs)) * size, (p % (count // outs) + 1) * size)
        at = 0
        for left, right in zip(pairs[0::2], pairs[1::2]):
            out[rows, at : at + right.shape[1]] = low(mm_tn(left[:, lanes_of(scalars, p, size)], right[...]))
            at += right.shape[1]


def middle_back(
    total_heads, scalars, total_ref, other_ref, middle_ref, cot_ref, gain_ref, sums_ref, gated_ref,
    gate_gain_ref, w_ref,
    dmiddle_ref, dmix_ref, dgain_ref, dnormed_ref, dattn_ref, cross_ref, dgate_gain_ref, full_ref,
):
    parity = scalars[scalars.shape[0] - 2]
    halves_joined(parity, total_ref, other_ref, full_ref)
    grad = full_ref[...]
    middle = middle_ref[...]
    inv = lax.rsqrt(jnp.mean(middle * middle, axis=-1, keepdims=True) + EPSILON)
    rows = middle * inv
    dgain_ref[...] = jnp.broadcast_to(jnp.sum(grad * rows, axis=0, keepdims=True), dgain_ref.shape)
    scaled = grad * gain_ref[...]
    dmiddle = cot_ref[...].astype(F32) + inv * (
        scaled - rows * jnp.mean(scaled * rows, axis=-1, keepdims=True)
    )
    dmiddle_ref[...] = dmiddle
    dmix_ref[...] = low(dmiddle)
    width = gated_ref.shape[1]
    first = w_ref.shape[1] - width - dattn_ref.shape[1]
    both = mm(dmix_ref[...], w_ref[:, first:])
    dnormed = both[:, :width]
    dnormed_ref[...] = dnormed
    dattn_ref[...] = low(both[:, width:])
    gated = gated_ref[...]
    product = dnormed * gated
    cross_ref[...] = token_sums(product * gate_gain_ref[...])
    inv_gate = as_column(lax.rsqrt(sums_ref[...] / (total_heads * PM) + EPSILON))
    dgate_gain_ref[...] = jnp.broadcast_to(
        jnp.sum(product * inv_gate, axis=0, keepdims=True), dgate_gain_ref.shape
    )


def gate_back(
    heads, total_heads, count, cross_ref, sums_ref, dnormed_ref, gated_ref, gain_ref, zq_ref, y_ref, cum_ref,
    bc_ref, *refs,
):
    msgs, kv = refs[: count - 1], refs[count - 1 : 2 * count - 1]
    dy_ref, dz_ref = refs[2 * count - 1 : 2 * count + 1]
    sent = refs[2 * count + 1 :]
    width = y_ref.shape[1]
    size = total_heads * PM
    inv = as_column(lax.rsqrt(sums_ref[...] / size + EPSILON))
    cross = as_column(cross_ref[...])
    dgated = inv * dnormed_ref[...] * gain_ref[...] - gated_ref[...] * (inv * inv * inv * cross / size)
    z = zq_ref[:, :width].astype(F32)
    sig = sigmoid(z)
    dy = dgated * (z * sig)
    dy_ref[...] = dy
    dz_ref[...] = low(dgated * y_ref[...] * sig * (1.0 + z * (1.0 - sig)))
    weighted = dy * mm(jnp.exp(cum_ref[...]), head_lanes(heads), HIGHEST)
    state = mm_tn(low(bc_ref[:, NS:]), low(weighted))
    for j in range(count):
        sent[j][:NS, :] = low(state)
        sent[j][NS:, :] = kv[j][...]
        if j < count - 1:
            decay = msgs[j][NS : NS + HALO, :].astype(F32)
            state = state * (decay[0:1, :] + decay[1:2, :])


def conv_and_input_back(
    scalars, dpre_ref, next_ref, taps_ref, dkv_ref, ddt_ref, dzq_ref,
    hidden_ref, dgain_mid_ref, dtaps_ref, dgate_gain_ref, dsmall_ref, dskip_ref, tokens_ref, w_ref, more_ref,
    dall_ref, small_ref, keep_ref, give_ref, full_ref,
):
    parity = scalars[scalars.shape[0] - 2]
    dpre = dpre_ref[...]
    rows = dpre.shape[0]
    longer = jnp.concatenate([dpre, next_ref[...]], axis=0)
    total = taps_ref[KC - 1 : KC, :] * dpre
    for k in range(KC - 1):
        shift = KC - 1 - k
        total = total + taps_ref[k : k + 1, :] * pltpu.roll(longer, longer.shape[0] - shift, 0)[:rows]
    dall = jnp.concatenate([low(total), dkv_ref[...], ddt_ref[...]], axis=1)
    dall_ref[...] = dall
    dzq = dzq_ref[...]
    full_ref[...] = mm_nt(dall, w_ref[...]) + mm_nt(dzq, more_ref[:, : dzq.shape[1]])
    x = tokens_ref[...].astype(F32)
    inv = lax.rsqrt(jnp.mean(x * x, axis=-1, keepdims=True) + EPSILON)
    dgain = jnp.sum(full_ref[...] * (x * inv), axis=0, keepdims=True)
    model = x.shape[1]
    place = lax.broadcasted_iota(jnp.int32, (8, model), 0)
    ddt_w = mm_tn(ddt_ref[...], hidden_ref[...])[:8]
    small_ref[:, :model] = jnp.where(place == 6, dgain_mid_ref[...], jnp.where(place == 7, dgain, ddt_w))
    rest = jnp.concatenate([dgate_gain_ref[0:1, :], dsmall_ref[0:1, :], dsmall_ref[1:2, :]], axis=1)
    wide = taps_ref.shape[1]
    skip_row = jnp.concatenate([dskip_ref[0:1, :], jnp.zeros((1, wide - LANES), F32)], axis=1)
    place = lax.broadcasted_iota(jnp.int32, (8, wide), 0)
    small_ref[:, model:] = jnp.where(
        place < KC, dtaps_ref[...], jnp.where(place == KC, rest, jnp.where(place == KC + 1, skip_row, 0.0))
    )
    halves_to_sum(parity, full_ref, keep_ref, give_ref)


def input_back(scalars, total_ref, other_ref, tokens_ref, gain_ref, dmiddle_ref, dtokens_ref, full_ref):
    parity = scalars[scalars.shape[0] - 2]
    halves_joined(parity, total_ref, other_ref, full_ref)
    grad = full_ref[...]
    x = tokens_ref[...].astype(F32)
    inv = lax.rsqrt(jnp.mean(x * x, axis=-1, keepdims=True) + EPSILON)
    rows = x * inv
    scaled = grad * gain_ref[...]
    dtokens_ref[...] = dmiddle_ref[...] + inv * (
        scaled - rows * jnp.mean(scaled * rows, axis=-1, keepdims=True)
    )


def output_sum(scalars, total_ref, other_ref, middle_ref, out_ref, full_ref):
    halves_joined(scalars[scalars.shape[0] - 2], total_ref, other_ref, full_ref)
    out_ref[...] = low(middle_ref[...] + full_ref[...])


def send(x, axis, pairs):
    return lax.ppermute(x, axis, pairs)


def from_ahead(x, axis, distance):
    n = lax.axis_size(axis)
    return send(x, axis, [((i + distance) % n, i) for i in range(n)])


def from_earlier(x, distance):
    n = lax.axis_size("row")
    return send(x, "row", [(i - distance, i) for i in range(distance, n)])


def from_later(x, distance):
    n = lax.axis_size("row")
    return send(x, "row", [(i + distance, i) for i in range(n - distance)])


def swap(x, axis, bit):
    return send(x, axis, [(i, i ^ bit) for i in range(lax.axis_size(axis))])


def after(x, *others):
    return lax.optimization_barrier((x,) + others)[0]


def after_all(*values):
    return lax.optimization_barrier(values)


def direct():
    return lax.axis_size("dp") == 2 and lax.axis_size("row") == 4


def scatter_first(parts):
    if len(parts) == 1:
        return [lax.psum_scatter(parts[0], ("dp", "row"), scatter_dimension=0, tiled=True)]
    half = parts[1].shape[0] // 2
    return [swap(parts[1][half:], "dp", 1), swap(parts[1][:half], "dp", 1)]


def scatter_beside(parts, got):
    if len(parts) == 1:
        return got[0]
    half = parts[0].shape[0] // 2
    return swap(low(parts[0][half:].astype(F32) + got[0].astype(F32)), "row", 1)


def scatter_last(parts, got, beside):
    if len(parts) == 1:
        return beside.astype(F32)
    blk = parts[0].shape[0] // 4
    total = parts[0][: 2 * blk].astype(F32) + got[1].astype(F32) + beside.astype(F32)
    return total[:blk] + swap(low(total[blk:]), "row", 2).astype(F32)


def col_sum(keep, give, *others):
    part = low(keep + swap(give, "col", 1).astype(F32))
    if others:
        part = after(part, *others)
    total = low(part.astype(F32) + swap(part, "col", 2).astype(F32))
    return total, swap(total, "col", 1)


def low_col_sum(values):
    values = low(values)
    values = low(values.astype(F32) + swap(values, "col", 1).astype(F32))
    return values.astype(F32) + swap(values, "col", 2).astype(F32)


def tiny_col_sum(values):
    values = values + swap(values, "col", 1)
    return values + swap(values, "col", 2)


def tiny_row_sum(values):
    if lax.axis_size("dp") == 2:
        values = values + swap(values, "dp", 1)
    else:
        values = lax.psum(values, "dp")
    values = values + swap(values, "row", 1)
    return values + swap(values, "row", 2)


def per_device(
    tokens, cotangent, norm_in, z_weight, x_weight, dt_weight, q_weight, bc_weight, key_value_weight,
    conv_x, conv_bc, dt_bias, a_log, d_skip, gate_gain, mamba_weight, attn_weight, norm_mid,
    gate_weight, up_weight, down_weight,
):
    dp_n, row_n, col_n = (lax.axis_size(a) for a in ("dp", "row", "col"))
    dp, row, col = (lax.axis_index(a) for a in ("dp", "row", "col"))
    if row_n != 4 or col_n != 4:
        raise ValueError("row, col: 4")
    rows, model = tokens.shape
    seq = rows * row_n
    heads = dt_bias.shape[0]
    total_heads = heads * col_n
    width = heads * PM
    q_width = q_weight.shape[1]
    q_heads = q_width // HEAD_DIM
    hidden = gate_weight.shape[1]
    blk = model // (dp_n * row_n)
    kv_group = col * q_heads * KEY_HEADS // QUERY_HEADS
    conv_width = width + 2 * NS
    in_width = conv_width + 2 * LANES

    shard_in = jnp.concatenate(
        [
            x_weight,
            bc_weight,
            lax.dynamic_slice_in_dim(key_value_weight, kv_group * HEAD_DIM, HEAD_DIM, 1),
            lax.dynamic_slice_in_dim(key_value_weight, (KEY_HEADS + kv_group) * HEAD_DIM, HEAD_DIM, 1),
            dt_weight,
            jnp.zeros((blk, LANES - heads), BF16),
        ],
        axis=1,
    )
    shard_mix = jnp.concatenate([z_weight, q_weight, mamba_weight.T, attn_weight.T], axis=1)
    shard_ff = jnp.concatenate([gate_weight, up_weight, down_weight.T], axis=1)
    halo = from_earlier(tokens[rows - HALO :], 1)
    ext = jnp.concatenate([halo, tokens], axis=0).astype(F32)
    inv_in = lax.rsqrt(jnp.mean(ext * ext, axis=-1, keepdims=True) + EPSILON)
    hidden_ext = low(ext * inv_in * norm_in)
    hidden_in = hidden_ext[HALO:]

    if direct():
        order = [((dp + i) % 2) * row_n + (row ^ x) for i in range(2) for x in (0, 2, 1, 3)]
        across, beside = swap(shard_in, "row", 2), swap(shard_in, "row", 1)
        own, mix_own = swap(shard_in, "dp", 1), swap(shard_mix, "dp", 1)
        across, beside, own, mix_own, hidden_ext = after_all(across, beside, own, mix_own, hidden_ext)
        corner = swap(across, "row", 1)
        over = [swap(across, "dp", 1), swap(beside, "dp", 1)]
        corner, shard_mix, shard_ff, *over = after_all(corner, shard_mix, shard_ff, *over)
        last = swap(corner, "dp", 1)
        mix_across, mix_beside = swap(shard_mix, "row", 2), swap(shard_mix, "row", 1)
        ff_own = swap(shard_ff, "dp", 1)
        last, mix_across, mix_beside, ff_own = after_all(last, mix_across, mix_beside, ff_own)
        in_blocks = [shard_in, across, beside, corner, own] + over + [last]
        mix_corner = swap(mix_across, "row", 1)
    else:
        in_blocks = [lax.all_gather(shard_in, ("dp", "row"), axis=0, tiled=True)]
        mix_blocks = [lax.all_gather(shard_mix, ("dp", "row"), axis=0, tiled=True)]
        ff_blocks = [lax.all_gather(shard_ff, ("dp", "row"), axis=0, tiled=True)]
        order = [jnp.int32(0)]
    scalars = jnp.stack([jnp.int32(v) for v in order] + [jnp.int32(col % 2), jnp.int32(row)])

    positions = (row * rows + jnp.arange(rows, dtype=jnp.int32)).astype(F32)
    half = HEAD_DIM // 2
    frequency = ROPE_BASE ** (-jnp.arange(half).astype(F32) / half)
    angles = positions[:, None] * frequency[None, :]
    cosine, sine = jnp.cos(angles), jnp.sin(angles)
    cos_q = jnp.concatenate([cosine] * (2 * q_heads), axis=1)
    sin_q = jnp.concatenate([sine] * (2 * q_heads), axis=1)
    cos_kv = jnp.concatenate([cosine, cosine, jnp.ones((rows, HEAD_DIM), F32)], axis=1)
    sin_kv = jnp.concatenate([sine, sine, jnp.zeros((rows, HEAD_DIM), F32)], axis=1)

    taps = jnp.concatenate([conv_x, conv_bc], axis=1)
    rate = -jnp.exp(a_log)

    def lane_row(v):
        return jnp.pad(v, (0, LANES - heads))[None, :]

    params = jnp.concatenate([lane_row(dt_bias), lane_row(rate), jnp.zeros((6, LANES), F32)], axis=0)
    skip = jnp.repeat(d_skip, PM)[None, :]
    area = rows * rows * heads
    part = packed_rows(rows, width)
    y_base, msg, proj, x_heads, bc_map, slope, cum, step, in_full = kernel_call(
        partial(scan_local, heads),
        (
            ((rows, width), F32),
            ((NS + HALO + 2 * part, width), BF16),
            ((HALO + rows, in_width), BF16),
            ((rows, width), F32),
            ((rows, 2 * NS), F32),
            ((rows, conv_width), F32),
            ((rows, LANES), F32),
            ((rows, LANES), F32),
        ),
        (area * 2 * PM * 10, 4000000, area),
        scalars,
        hidden_ext,
        taps,
        params,
        skip,
        cos_kv,
        sin_kv,
        in_blocks,
        keep=True,
    )
    if direct():
        msg, mix_corner, mix_across, mix_beside, shard_ff = after_all(
            msg, mix_corner, mix_across, mix_beside, shard_ff
        )
        msgs = [from_earlier(msg, j) for j in range(1, row_n)]
        mix_over = [swap(v, "dp", 1) for v in (mix_across, mix_beside, mix_corner)]
        ff_across, ff_beside = swap(shard_ff, "row", 2), swap(shard_ff, "row", 1)
        ff_across, ff_beside, *moved = after_all(ff_across, ff_beside, *mix_over, *msgs)
        mix_over, msgs = moved[:3], moved[3:]
        ff_corner = swap(ff_across, "row", 1)
        ff_over = [swap(v, "dp", 1) for v in (ff_across, ff_beside)]
        mix_blocks = [shard_mix, mix_across, mix_beside, mix_corner, mix_own] + mix_over
    else:
        msgs = [from_earlier(msg, j) for j in range(1, row_n)]
    zq, mix_full = kernel_call(
        project,
        (((rows, width + q_width), BF16),),
        (2 * rows * model * (width + q_width), 4000000, 0),
        scalars,
        hidden_in,
        mix_blocks,
        keep=True,
    )

    (
        attn_value, probs, query, key, value, state_in, carried, y, gated, sums,
    ) = kernel_call(
        partial(mix_tokens, heads, row_n - 1),
        (
            ((rows, q_width), BF16),
            ((q_heads * rows, seq), BF16),
            ((q_heads * rows, HEAD_DIM), BF16),
            ((seq, HEAD_DIM), BF16),
            ((seq, HEAD_DIM), BF16),
            ((NS, width), F32),
            ((rows, width), F32),
            ((rows, width), F32),
            ((rows, width), F32),
            ((8, rows), F32),
        ),
        (8 * q_width * rows * seq, 6000000, q_heads * rows * seq),
        scalars,
        msg,
        *msgs,
        y_base,
        cum,
        bc_map,
        zq,
        cos_q,
        sin_q,
    )
    sums = tiny_col_sum(sums)
    gain_row = gate_gain[None, :]
    halves = (((rows // 2, model), F32), ((rows // 2, model), BF16))
    full_scratch = ((rows, model), F32)
    mamba_normed, keep, give, _ = kernel_call(
        partial(mix_out, total_heads),
        (((rows, width), BF16),) + halves + (full_scratch,),
        (2 * rows * model * (width + q_width), 4000000, 0),
        scalars,
        sums,
        gated,
        gain_row,
        attn_value,
        mix_full,
    )
    if direct():
        give, ff_corner, *ff_over = after_all(give, ff_corner, *ff_over)
        ff_blocks = [shard_ff, ff_across, ff_beside, ff_corner, ff_own] + ff_over + [swap(ff_corner, "dp", 1)]
    total, other = col_sum(keep, give)

    gain_mid = norm_mid[None, :]
    middle, hidden_mid, grad_gate_up, swiglu, keep, give, out_keep, out_give, _ = kernel_call(
        feed_forward,
        (
            ((rows, model), F32),
            ((rows, model), BF16),
            ((rows, 2 * hidden), BF16),
            ((rows, hidden), BF16),
        )
        + halves
        + halves
        + (full_scratch,),
        (14 * rows * model * hidden, 8000000, rows * hidden),
        scalars,
        total,
        other,
        [tokens],
        [cotangent],
        gain_mid,
        ff_blocks,
    )

    def weight_grad(*operands):
        columns = sum(v.shape[1] for v in operands[1::2])
        outs = 2 if direct() else 1
        return kernel_call(
            partial(weight_products, len(order)),
            (((model // outs, columns), BF16),) * outs,
            (2 * rows * model * columns, 5000000, 0),
            scalars,
            *operands,
        )

    ff_parts = weight_grad(hidden_mid, grad_gate_up, cotangent, swiglu)
    total, other = col_sum(keep, give, *ff_parts)
    if direct():
        near = ff_parts[1].shape[0] // 2
        ff_got = [swap(ff_parts[1][near:], "dp", 1)]
    else:
        ff_got = scatter_first(ff_parts)

    grad_middle, grad_mix, dgain_mid, grad_normed, grad_attn, cross, dgate_gain, _ = kernel_call(
        partial(middle_back, total_heads),
        (
            ((rows, model), F32),
            ((rows, model), BF16),
            ((8, model), F32),
            ((rows, width), F32),
            ((rows, q_width), BF16),
            ((8, rows), F32),
            ((8, width), F32),
            full_scratch,
        ),
        (2 * rows * model * (width + q_width), 6000000, 0),
        scalars,
        total,
        other,
        middle,
        [cotangent],
        gain_mid,
        sums,
        gated,
        gain_row,
        mix_full,
    )
    cross = tiny_col_sum(cross)
    grad_query, grad_kv_own, *kv_sent = kernel_call(
        attend_back,
        (((rows, q_width), BF16), ((rows, LANES), F32)) + (((2 * part, width), BF16),) * (row_n - 1),
        (16 * q_width * rows * seq, 4000000, 0),
        None,
        grad_attn,
        probs,
        query,
        cos_q,
        sin_q,
        key,
        value,
    )
    grad_y, grad_z, *sent = kernel_call(
        partial(gate_back, heads, total_heads, row_n - 1),
        (((rows, width), F32), ((rows, width), BF16)) + (((NS + 2 * part, width), BF16),) * (row_n - 1),
        (2 * rows * NS * width, 4000000, rows * width),
        None,
        cross,
        sums,
        grad_normed,
        gated,
        gain_row,
        zq,
        y,
        cum,
        bc_map,
        *msgs[: row_n - 2],
        *kv_sent,
    )
    got = [from_later(sent[j - 1], j) for j in range(1, row_n)]
    if direct():
        ff_got.append(swap(after(ff_parts[1][:near], grad_y), "dp", 1))
    dx_local, dbc_local, dcum, dstep, dskip = kernel_call(
        partial(scan_back_local, heads),
        (
            ((rows, width), F32),
            ((rows, 2 * NS), F32),
            ((rows, LANES), F32),
            ((rows, LANES), F32),
            ((8, LANES), F32),
        ),
        (area * 2 * PM * 20, 4000000, area),
        None,
        grad_y,
        x_heads,
        bc_map,
        cum,
        step,
        carried,
        state_in,
        skip,
    )
    grad_zq = jnp.concatenate([grad_z, grad_query], axis=1)
    act = jnp.concatenate([mamba_normed, attn_value], axis=1)
    mix_parts = weight_grad(hidden_in, grad_zq, grad_mix, act)
    mix_got = scatter_first(mix_parts)
    got = list(after(tuple(got), mix_parts, ff_got[0]))

    dpre, first, grad_dt, grad_kv, dsmall, dtaps = kernel_call(
        partial(scan_back_end, heads, row_n - 1),
        (
            ((rows, conv_width), F32),
            ((8, conv_width), F32),
            ((rows, LANES), BF16),
            ((rows, LANES), BF16),
            ((8, LANES), F32),
            ((8, conv_width), F32),
        ),
        (rows * NS * width * 10, 4000000, rows * LANES * 3),
        None,
        *got,
        state_in,
        x_heads,
        bc_map,
        cum,
        step,
        dx_local,
        dbc_local,
        dcum,
        dstep,
        slope,
        proj,
        params,
        grad_kv_own,
        cos_kv,
        sin_kv,
    )
    following = from_later(first, 1)
    following = after(following, ff_got)
    ff_beside = scatter_beside(ff_parts, [after(ff_got[0], following)])

    grad_all, small, keep, give, _ = kernel_call(
        conv_and_input_back,
        (((rows, in_width), BF16), ((8, model + conv_width), F32)) + halves + (full_scratch,),
        (2 * rows * model * (in_width + width + q_width), 8000000, 0),
        scalars,
        dpre,
        following,
        taps,
        grad_kv,
        grad_dt,
        grad_zq,
        hidden_in,
        dgain_mid,
        dtaps,
        dgate_gain,
        dsmall,
        dskip,
        [tokens],
        in_full,
        mix_full,
    )
    tail_width = conv_width + LANES
    tail_parts = weight_grad(hidden_in, after(grad_all, mix_got[0])[:, :tail_width])
    mix_got = mix_got[:1] + [after(v, *tail_parts) for v in mix_got[1:]]
    tail_got = scatter_first(tail_parts)
    mix_beside = scatter_beside(mix_parts, [after(mix_got[0], ff_beside, tail_got)])
    total, other = col_sum(keep, give)
    grad_ff = scatter_last(ff_parts, ff_got, after(ff_beside, tail_got[0]))
    out_total, out_other = col_sum(out_keep, after(out_give, total))
    layer_out, _ = kernel_call(
        output_sum,
        (((rows, model), BF16), full_scratch),
        (rows * model, 3000000, 0),
        scalars,
        out_total,
        out_other,
        middle,
    )
    tail_beside = scatter_beside(tail_parts, [after(tail_got[0], ff_beside)])
    grad_in_w = scatter_last(tail_parts, tail_got, tail_beside)
    grad_mix_w = scatter_last(mix_parts, mix_got, after(mix_beside, tail_beside))
    grad_tokens, _ = kernel_call(
        input_back,
        (((rows, model), F32), full_scratch),
        (rows * model * 10, 4000000, 0),
        scalars,
        total,
        other,
        [tokens],
        norm_in[None, :],
        [grad_middle],
    )

    bc_w = grad_in_w[:, width:conv_width]
    kv_w = grad_in_w[:, conv_width:]
    spot = (jnp.arange(KEY_HEADS) == kv_group).astype(F32)
    wide = [spot[i] * kv_w[:, :HEAD_DIM] for i in range(KEY_HEADS)]
    wide += [spot[i] * kv_w[:, HEAD_DIM:] for i in range(KEY_HEADS)]
    shared = jnp.concatenate([bc_w] + wide, axis=1)
    shared = low_col_sum(shared)

    line = lax.broadcasted_iota(jnp.int32, small.shape, 0)
    lane = lax.broadcasted_iota(jnp.int32, small.shape, 1)
    partial_lanes = ((line == 7) & (lane < model)) | ((line < KC) & (lane >= model + width))
    small = jnp.where(partial_lanes, tiny_col_sum(small), small)
    small = tiny_row_sum(after(small, tail_beside))
    taps_at = model + width
    place = (dp * row_n + row) * blk
    return (
        layer_out,
        grad_tokens,
        small[7, :model],
        grad_mix_w[:, :width],
        grad_in_w[:, :width],
        lax.dynamic_slice(small, (0, place), (heads, blk)).T,
        grad_mix_w[:, width : width + q_width],
        shared[:, : 2 * NS],
        shared[:, 2 * NS :],
        small[:KC, model:taps_at],
        small[:KC, taps_at:],
        small[KC, taps_at : taps_at + heads],
        small[KC, taps_at + LANES : taps_at + LANES + heads],
        small[KC + 1, model : model + heads],
        small[KC, model:taps_at],
        grad_mix_w[:, width + q_width : 2 * width + q_width].T,
        grad_mix_w[:, 2 * width + q_width :].T,
        small[6, :model],
        grad_ff[:, :hidden],
        grad_ff[:, hidden : 2 * hidden],
        grad_ff[:, 2 * hidden :].T,
    )


def solution(mesh):
    by_rows = P(("dp", "row"), None)
    both = P(("dp", "row"), "col")
    turned = P("col", ("dp", "row"))
    per_col = P("col")
    taps = P(None, "col")
    in_specs = (
        by_rows, by_rows, P(), both, both, both, both, by_rows, by_rows, taps, P(), per_col, per_col,
        per_col, per_col, turned, turned, P(), both, both, turned,
    )
    out_specs = (
        by_rows, by_rows, P(), both, both, both, both, by_rows, by_rows, taps, P(), per_col, per_col,
        per_col, per_col, turned, turned, P(), both, both, turned,
    )
    return jax.shard_map(
        per_device, mesh=mesh, in_specs=in_specs, out_specs=out_specs, check_vma=False
    )
```

```python
from functools import partial

import jax
import jax.numpy as jnp
from jax import lax
from jax.experimental import pallas as pl
from jax.experimental.pallas import tpu as pltpu
from jax.sharding import PartitionSpec as P

HM = 24
PM = 64
NS = 128
KC = 4
QUERY_HEADS = 8
KEY_HEADS = 2
HEAD_DIM = 64
HALO = 16
LANES = 128

EPSILON = 1e-05
ROPE_BASE = 100000000000.0
NEG_LARGE = -1e30
HIGHEST = lax.Precision.HIGHEST
F32 = jnp.float32
BF16 = jnp.bfloat16


def mm(a, b, precision=None):
    return lax.dot_general(
        a, b, (((1,), (0,)), ((), ())), precision=precision, preferred_element_type=F32
    )


def mm_nt(a, b, precision=None):
    return lax.dot_general(
        a, b, (((1,), (1,)), ((), ())), precision=precision, preferred_element_type=F32
    )


def mm_tn(a, b, precision=None):
    return lax.dot_general(
        a, b, (((0,), (0,)), ((), ())), precision=precision, preferred_element_type=F32
    )


def low(v):
    return v.astype(BF16)


def sigmoid(v):
    return 1.0 / (1.0 + jnp.exp(-v))


def softplus(v):
    return jnp.maximum(v, 0.0) + jnp.log1p(jnp.exp(-jnp.abs(v)))


def head_lanes(heads):
    head = lax.broadcasted_iota(jnp.int32, (LANES, heads * PM), 0)
    column = lax.broadcasted_iota(jnp.int32, (LANES, heads * PM), 1)
    return ((column >= head * PM) & (column < head * PM + PM)).astype(F32)


def lower_triangle(size):
    later = lax.broadcasted_iota(jnp.int32, (size, size), 0)
    earlier = lax.broadcasted_iota(jnp.int32, (size, size), 1)
    return later >= earlier


def split_pair(pair):
    first = lax.broadcasted_iota(jnp.int32, pair.shape, 1) < PM
    zero = jnp.zeros_like(pair)
    return jnp.concatenate([jnp.where(first, pair, zero), jnp.where(first, zero, pair)], axis=0)


def kernel_call(body, outs, cost, scalars, *operands, keep=False, near=False):
    flops, traffic, exps = cost
    flat, in_specs, scratch, plan = [], [], [], []
    if scalars is not None:
        flat.append(scalars)
        in_specs.append(pl.BlockSpec(memory_space=pltpu.SMEM))
    for operand in operands:
        parts = operand if isinstance(operand, list) else [operand]
        plan.append((len(flat), len(parts), isinstance(operand, list)))
        flat += parts
        space = pl.ANY if isinstance(operand, list) and not near else pltpu.VMEM
        in_specs += [pl.BlockSpec(memory_space=space)] * len(parts)
        if isinstance(operand, list):
            whole = (sum(v.shape[0] for v in parts), parts[0].shape[1])
            scratch.append(pltpu.VMEM(whole, parts[0].dtype))
            last = (whole, parts[0].dtype)
    if keep:
        scratch.pop()
        outs = tuple(outs) + (last,)
    copied = sum(n for _, n, outside in plan if outside)
    if copied:
        scratch.append(pltpu.SemaphoreType.DMA((copied,)))

    def run(*refs):
        ins, results, held = refs[: len(flat)], refs[len(flat) : len(flat) + len(outs)], refs[len(flat) + len(outs) :]
        views = [ins[0]] if scalars is not None else []
        copies, taken = [], 0
        for start, n, outside in plan:
            if not outside:
                views.append(ins[start])
                continue
            target = results[-1] if keep and taken == len(scratch) - 1 else held[taken]
            taken += 1
            views.append(target)
            for i in range(n):
                size = ins[start + i].shape[0]
                place = target if n == 1 else target.at[lanes_of(ins[0], i, size), :]
                copies.append(pltpu.make_async_copy(ins[start + i], place, held[-1].at[len(copies)]))
        for c in copies:
            c.start()
        for c in copies:
            c.wait()
        body(*views, *(results[:-1] if keep else results))

    return pl.pallas_call(
        run,
        out_shape=tuple(jax.ShapeDtypeStruct(s, d) for s, d in outs),
        in_specs=in_specs,
        out_specs=tuple(pl.BlockSpec(memory_space=pltpu.VMEM) for _ in outs),
        scratch_shapes=scratch,
        compiler_params=pltpu.CompilerParams(vmem_limit_bytes=24 * 1024 * 1024),
        cost_estimate=pl.CostEstimate(flops=flops, bytes_accessed=traffic, transcendentals=exps),
    )(*flat)


def lanes_of(scalars, p, size):
    return pl.ds(pl.multiple_of(scalars[p] * size, size), size)


def rows_half(parity, rows, own):
    half = rows // 2
    return pl.ds(pl.multiple_of((parity if own else 1 - parity) * half, half), half)


def halves_to_sum(parity, full_ref, keep_ref, give_ref):
    rows = full_ref.shape[0]
    keep_ref[...] = full_ref[rows_half(parity, rows, True), :]
    give_ref[...] = low(full_ref[rows_half(parity, rows, False), :])


def halves_joined(parity, total_ref, other_ref, full_ref):
    rows = full_ref.shape[0]
    full_ref[rows_half(parity, rows, True), :] = total_ref[...].astype(F32)
    full_ref[rows_half(parity, rows, False), :] = other_ref[...].astype(F32)


def pack_rows(v, width):
    count = width // HEAD_DIM
    chunk = packed_rows(v.shape[0], width)
    pieces = []
    for i in range(count):
        piece = v[i * chunk : min((i + 1) * chunk, v.shape[0])]
        if piece.shape[0] < chunk:
            piece = jnp.concatenate([piece, jnp.zeros((chunk - piece.shape[0], HEAD_DIM), v.dtype)], axis=0)
        pieces.append(piece)
    return jnp.concatenate(pieces, axis=1)


def packed_rows(rows, width):
    count = width // HEAD_DIM
    return -(-rows // (16 * count)) * 16


def unpack_rows(v, rows):
    count = v.shape[1] // HEAD_DIM
    return jnp.concatenate([v[:, i * HEAD_DIM : (i + 1) * HEAD_DIM] for i in range(count)], axis=0)[:rows]


def token_sums(v):
    return mm_nt(jnp.ones((8, v.shape[1]), F32), v, HIGHEST)


def as_column(v):
    return jnp.transpose(v)[:, :1]


def scan_local(
    heads, scalars, hidden_ref, taps_ref, par_ref, skip_ref, cos_ref, sin_ref, w_ref,
    y_ref, msg_ref, proj_ref, x_ref, bc_ref, slope_ref, cum_ref, step_ref,
):
    width = heads * PM
    conv_width = width + 2 * NS
    rows = y_ref.shape[0]
    proj = low(mm(hidden_ref[...], w_ref[...]))
    proj_ref[...] = proj
    ext = proj[:, :conv_width].astype(F32)
    pre = taps_ref[KC - 1 : KC, :] * ext[HALO:]
    for k in range(KC - 1):
        pre = pre + taps_ref[k : k + 1, :] * pltpu.roll(ext, KC - 1 - k, 0)[HALO:]
    sig = sigmoid(pre)
    conv_out = pre * sig
    slope_ref[...] = sig * (1.0 + pre * (1.0 - sig))
    x = conv_out[:, :width]
    x_ref[...] = x
    bc_ref[...] = conv_out[:, width:]
    b_map = low(conv_out[:, width : width + NS])
    c_map = low(conv_out[:, width + NS :])
    raw = proj[HALO:, conv_width + LANES :].astype(F32) + par_ref[0:1, :]
    lane = lax.broadcasted_iota(jnp.int32, raw.shape, 1)
    step = jnp.where(lane < heads, softplus(raw), 0.0)
    step_ref[...] = step
    causal = lower_triangle(rows)
    cum = mm(causal.astype(F32), step * par_ref[1:2, :], HIGHEST)
    cum_ref[...] = cum
    spread = head_lanes(heads)
    last = cum[rows - 1 : rows, :]
    tail = mm(jnp.exp(last - cum) * step, spread, HIGHEST)
    msg_ref[:NS, :] = low(mm_tn(b_map, low(x * tail)))
    decay = mm(jnp.exp(jnp.broadcast_to(last, (HALO, LANES))), spread, HIGHEST)
    coarse = low(decay)
    fine = low(decay - coarse.astype(F32))
    place = lax.broadcasted_iota(jnp.int32, decay.shape, 0)
    msg_ref[NS : NS + HALO, :] = low(jnp.where(place == 0, coarse.astype(F32), fine.astype(F32)))
    kv = proj[HALO:, conv_width : conv_width + LANES]
    turned = mm(kv, low(quarter_turn(LANES)))
    kv = low(kv.astype(F32) * cos_ref[...] + turned * sin_ref[...])
    part = packed_rows(rows, width)
    at = NS + HALO
    msg_ref[at : at + part, :] = pack_rows(kv[:, :HEAD_DIM], width)
    msg_ref[at + part : at + 2 * part, :] = pack_rows(kv[:, HEAD_DIM:], width)
    cum_t = jnp.transpose(cum)
    step_t = jnp.transpose(step)
    meet = jnp.where(causal, mm_nt(c_map, b_map), 0.0)
    for pair in range(heads // 2):
        mixing = []
        for h in (2 * pair, 2 * pair + 1):
            gap = jnp.minimum(cum[:, h : h + 1] - cum_t[h : h + 1, :], 0.0)
            mixing.append(low(meet * jnp.exp(gap) * step_t[h : h + 1, :]))
        lanes = slice(pair * LANES, (pair + 1) * LANES)
        y_ref[:, lanes] = (
            mm(jnp.concatenate(mixing, axis=1), split_pair(low(x[:, lanes])))
            + skip_ref[0:1, lanes] * x[:, lanes]
        )


def scan_back_local(
    heads, dy_ref, x_ref, bc_ref, cum_ref, step_ref, carried_ref, state_ref, skip_ref,
    dx_ref, dbc_ref, dcum_ref, dstep_ref, dskip_ref,
):
    rows = dy_ref.shape[0]
    dy = dy_ref[...]
    x = x_ref[...]
    b_map = low(bc_ref[:, :NS])
    c_map = low(bc_ref[:, NS:])
    cum = cum_ref[...]
    step = step_ref[...]
    cum_t = jnp.transpose(cum)
    step_t = jnp.transpose(step)
    causal = lower_triangle(rows)
    meet = jnp.where(causal, mm_nt(c_map, b_map), 0.0)
    lane = lax.broadcasted_iota(jnp.int32, (rows, LANES), 1)
    dmeet = jnp.zeros((rows, rows), F32)
    row_part = jnp.zeros((rows, LANES), F32)
    column_sums = []
    for pair in range(heads // 2):
        lanes = slice(pair * LANES, (pair + 1) * LANES)
        x_pair = low(x[:, lanes])
        dy_split = split_pair(low(dy[:, lanes]))
        dmix_both = mm_nt(dy_split, x_pair)
        mixing = []
        for i in range(2):
            h = 2 * pair + i
            dmix = dmix_both[i * rows : (i + 1) * rows]
            gap = jnp.minimum(cum[:, h : h + 1] - cum_t[h : h + 1, :], 0.0)
            decay = jnp.where(causal, jnp.exp(gap), 0.0)
            row_step = step_t[h : h + 1, :]
            decay_step = decay * row_step
            dmeet = dmeet + dmix * decay_step
            mixing.append(low(meet * decay_step))
            ratio = dmix * meet * decay
            column_sums.append(jnp.sum(ratio, axis=0, keepdims=True))
            row_sum = jnp.sum(ratio * row_step, axis=1, keepdims=True)
            row_part = row_part + jnp.where(lane == h, row_sum, 0.0)
        dx_ref[:, lanes] = (
            mm_tn(jnp.concatenate(mixing, axis=0), dy_split) + skip_ref[0:1, lanes] * dy[:, lanes]
        )
    column_sums.append(jnp.zeros((LANES - heads, rows), F32))
    dstep = jnp.transpose(jnp.concatenate(column_sums, axis=0))
    dstep_ref[...] = dstep
    spread = head_lanes(heads)
    weighted = dy * mm(jnp.exp(cum), spread, HIGHEST)
    dcum_ref[...] = row_part - dstep * step + mm_nt(weighted * carried_ref[...], spread, HIGHEST)
    dmeet_low = low(dmeet)
    dbc_ref[:, :NS] = mm_tn(dmeet_low, c_map)
    dbc_ref[:, NS:] = mm(dmeet_low, b_map) + mm_nt(low(weighted), low(state_ref[...]))
    dskip = jnp.broadcast_to(jnp.sum(dy * x, axis=0, keepdims=True), (8, dy.shape[1]))
    dskip_ref[...] = mm_nt(dskip, spread, HIGHEST)


def scan_back_end(
    heads, count, *refs
):
    got = refs[:count]
    (
        state_ref, x_ref, bc_ref, cum_ref, step_ref, dx_ref, dbc_ref, dcum_ref, dstep_ref, slope_ref,
        proj_ref, par_ref, dkv_ref, cos_ref, sin_ref,
        dpre_ref, first_ref, ddt_ref, dkv_out_ref, small_ref, dtaps_ref,
    ) = refs[count:]
    width = heads * PM
    conv_width = width + 2 * NS
    rows = x_ref.shape[0]
    part = packed_rows(rows, width)
    dkv = dkv_ref[...]
    dstate = jnp.zeros((NS, width), F32)
    for g in got:
        dstate = dstate + g[:NS, :].astype(F32)
        key = unpack_rows(g[NS : NS + part, :], rows)
        value = unpack_rows(g[NS + part : NS + 2 * part, :], rows)
        dkv = dkv + jnp.concatenate([key, value], axis=1).astype(F32)
    turned = mm(dkv, quarter_turn(LANES), HIGHEST)
    dkv_out_ref[...] = low(dkv * cos_ref[...] - turned * sin_ref[...])
    x = x_ref[...]
    b_map = low(bc_ref[:, :NS])
    cum = cum_ref[...]
    step = step_ref[...]
    spread = head_lanes(heads)
    last = cum[rows - 1 : rows, :]
    fade = jnp.exp(last - cum)
    tail = fade * step
    wide_tail = mm(tail, spread, HIGHEST)
    dstate_low = low(dstate)
    reach = mm(b_map, dstate_low)
    dx = dx_ref[...] + wide_tail * reach
    db = dbc_ref[:, :NS] + mm_nt(low(x * wide_tail), dstate_low)
    value = mm_nt(x * reach, spread, HIGHEST)
    total = jnp.sum(dstate * state_ref[...], axis=0, keepdims=True)
    dtotal = mm_nt(jnp.broadcast_to(total, (8, width)), spread, HIGHEST)[0:1, :]
    held = tail * value
    at_end = jnp.exp(last) * dtotal + jnp.sum(held, axis=0, keepdims=True)
    upper = jnp.where(lower_triangle(rows), 1.0, 0.0)
    drate = mm_tn(upper, dcum_ref[...] - held, HIGHEST) + at_end
    dstep = dstep_ref[...] + fade * value + drate * par_ref[1:2, :]
    raw = proj_ref[HALO:, conv_width + LANES :].astype(F32) + par_ref[0:1, :]
    lane = lax.broadcasted_iota(jnp.int32, raw.shape, 1)
    ddt = jnp.where(lane < heads, dstep * sigmoid(raw), 0.0)
    ddt_ref[...] = low(ddt)
    dbias = jnp.sum(ddt, axis=0, keepdims=True)
    dlog = jnp.sum(drate * step, axis=0, keepdims=True) * par_ref[1:2, :]
    place = lax.broadcasted_iota(jnp.int32, (8, LANES), 0)
    small_ref[...] = jnp.where(place == 0, dbias, jnp.where(place == 1, dlog, 0.0))
    dpre = jnp.concatenate([dx, db, dbc_ref[:, NS:]], axis=1) * slope_ref[...]
    dpre_ref[...] = dpre
    first_ref[...] = dpre[:8]
    ext = proj_ref[:, :conv_width].astype(F32)
    sums = [
        jnp.sum(dpre * (pltpu.roll(ext, KC - 1 - k, 0) if k < KC - 1 else ext)[HALO:], axis=0, keepdims=True)
        for k in range(KC)
    ]
    dtaps_ref[...] = jnp.concatenate(sums + [jnp.zeros((8 - KC, conv_width), F32)], axis=0)


def heads_to_rows(v):
    return jnp.concatenate([v[:, i * HEAD_DIM : (i + 1) * HEAD_DIM] for i in range(v.shape[1] // HEAD_DIM)], axis=0)


def rows_to_heads(v, count):
    rows = v.shape[0] // count
    return jnp.concatenate([v[i * rows : (i + 1) * rows] for i in range(count)], axis=1)


def quarter_turn(width):
    source = lax.broadcasted_iota(jnp.int32, (width, width), 0)
    target = lax.broadcasted_iota(jnp.int32, (width, width), 1)
    half = HEAD_DIM // 2
    upper = (target & (HEAD_DIM - 1)) >= half
    from_first = jnp.where(source == target - half, 1.0, 0.0)
    from_second = jnp.where(source == target + half, -1.0, 0.0)
    return jnp.where(upper, from_first, from_second)


def mix_tokens(
    heads, count, scalars, own_ref, *refs
):
    msgs = refs[:count]
    (
        y_ref, cum_ref, bc_ref, zq_ref, cos_ref, sin_ref,
        out_ref, probs_ref, query_ref, key_ref, value_ref, state_ref, carried_ref, y_out_ref, gated_ref, sums_ref,
    ) = refs[count:]
    row = scalars[scalars.shape[0] - 1]
    rows, width = y_ref.shape
    at = NS + HALO
    part = packed_rows(rows, width)
    everyone = (own_ref,) + msgs
    key = jnp.concatenate([unpack_rows(m[at : at + part, :], rows) for m in everyone], axis=0)
    value = jnp.concatenate([unpack_rows(m[at + part : at + 2 * part, :], rows) for m in everyone], axis=0)
    key_ref[...] = key
    value_ref[...] = value

    state = msgs[-1][:NS, :].astype(F32)
    for m in reversed(msgs[:-1]):
        decay = m[NS : NS + HALO, :].astype(F32)
        state = m[:NS, :].astype(F32) + (decay[0:1, :] + decay[1:2, :]) * state
    state_ref[...] = state
    carried = mm(low(bc_ref[:, NS:]), low(state))
    carried_ref[...] = carried
    y = y_ref[...] + mm(jnp.exp(cum_ref[...]), head_lanes(heads), HIGHEST) * carried
    y_out_ref[...] = y
    z = zq_ref[:, :width].astype(F32)
    gated = y * (z * sigmoid(z))
    gated_ref[...] = gated
    sums_ref[...] = token_sums(gated * gated)

    q = zq_ref[:, width:]
    q_heads = q.shape[1] // HEAD_DIM
    turned = mm(q, low(quarter_turn(q.shape[1])))
    query = heads_to_rows(low(q.astype(F32) * cos_ref[...] + turned * sin_ref[...]))
    query_ref[...] = query
    scores = mm_nt(query, key) * (HEAD_DIM ** (-0.5))
    place = lax.broadcasted_iota(jnp.int32, scores.shape, 0)
    column = lax.broadcasted_iota(jnp.int32, scores.shape, 1)
    place = place & (rows - 1)
    limit = jnp.where(column < rows, place, (row + 1) * rows - 1)
    scores = jnp.where(column <= limit, scores, NEG_LARGE)
    exponent = jnp.exp(scores - jnp.max(scores, axis=1, keepdims=True))
    probs = low(exponent * (1.0 / jnp.sum(exponent, axis=1, keepdims=True)))
    probs_ref[...] = probs
    out_ref[...] = low(rows_to_heads(mm(probs, value), q_heads))


def attend_back(grad_ref, probs_ref, query_ref, cos_ref, sin_ref, key_ref, value_ref, dq_ref, dkv_ref, *sent):
    count = grad_ref.shape[1] // HEAD_DIM
    rows = dkv_ref.shape[0]
    scale = HEAD_DIM ** (-0.5)
    grad = heads_to_rows(grad_ref[...])
    probs_low = probs_ref[...]
    probs = probs_low.astype(F32)
    dprobs = mm_nt(grad, value_ref[...])
    delta = jnp.sum(probs * dprobs, axis=1, keepdims=True)
    dscores = low(probs * (dprobs - delta))
    dquery = rows_to_heads(mm(dscores, key_ref[...]), count) * scale
    turned = mm(dquery, quarter_turn(dquery.shape[1]), HIGHEST)
    dq_ref[...] = low(dquery * cos_ref[...] - turned * sin_ref[...])
    dkey = mm_tn(dscores, query_ref[...]) * scale
    dvalue = mm_tn(probs_low, grad)
    dkv_ref[...] = jnp.concatenate([dkey[:rows], dvalue[:rows]], axis=1)
    for j, out in enumerate(sent):
        at = slice((j + 1) * rows, (j + 2) * rows)
        part = packed_rows(rows, out.shape[1])
        out[:part, :] = pack_rows(low(dkey[at]), out.shape[1])
        out[part:, :] = pack_rows(low(dvalue[at]), out.shape[1])


def project(scalars, hidden_ref, w_ref, out_ref):
    out_ref[...] = low(mm(hidden_ref[...], w_ref[:, : out_ref.shape[1]]))


def mix_out(
    total_heads, scalars, sums_ref, gated_ref, gain_ref, attn_ref, w_ref, normed_ref, keep_ref, give_ref, full_ref
):
    parity = scalars[scalars.shape[0] - 2]
    inv = as_column(lax.rsqrt(sums_ref[...] / (total_heads * PM) + EPSILON))
    normed = low(gated_ref[...] * inv * gain_ref[...])
    normed_ref[...] = normed
    act = jnp.concatenate([normed, attn_ref[...]], axis=1)
    full_ref[...] = mm_nt(act, w_ref[:, w_ref.shape[1] - act.shape[1] :])
    halves_to_sum(parity, full_ref, keep_ref, give_ref)


def feed_forward(
    scalars, total_ref, other_ref, tokens_ref, cot_ref, gain_ref, w_ref,
    middle_ref, hidden_ref, dgu_ref, swiglu_ref, keep_ref, give_ref, out_keep_ref, out_give_ref, full_ref,
):
    parity = scalars[scalars.shape[0] - 2]
    halves_joined(parity, total_ref, other_ref, full_ref)
    middle = tokens_ref[...].astype(F32) + full_ref[...]
    middle_ref[...] = middle
    inv = lax.rsqrt(jnp.mean(middle * middle, axis=-1, keepdims=True) + EPSILON)
    hidden_ref[...] = low(middle * inv * gain_ref[...])
    width = swiglu_ref.shape[1]
    gate_up = low(mm(hidden_ref[...], w_ref[:, : 2 * width])).astype(F32)
    gate, up = gate_up[:, :width], gate_up[:, width:]
    sig = sigmoid(gate)
    swish = gate * sig
    swiglu = low(swish * up)
    swiglu_ref[...] = swiglu
    grad = mm(cot_ref[...], w_ref[:, 2 * width :])
    dgate = low(grad * up * sig * (1.0 + gate * (1.0 - sig)))
    dup = low(grad * swish)
    dgu = jnp.concatenate([dgate, dup], axis=1)
    dgu_ref[...] = dgu
    full_ref[...] = mm_nt(dgu, w_ref[:, : 2 * width])
    halves_to_sum(parity, full_ref, keep_ref, give_ref)
    full_ref[...] = mm_nt(swiglu, w_ref[:, 2 * width :])
    halves_to_sum(parity, full_ref, out_keep_ref, out_give_ref)


def weight_products(count, scalars, *refs):
    outs = 1 if count == 1 else 2
    pairs, results = refs[:-outs], refs[-outs:]
    size = pairs[0].shape[1] // count
    for p in range(count):
        out = results[p * outs // count]
        rows = slice((p % (count // outs)) * size, (p % (count // outs) + 1) * size)
        at = 0
        for left, right in zip(pairs[0::2], pairs[1::2]):
            out[rows, at : at + right.shape[1]] = low(mm_tn(left[:, lanes_of(scalars, p, size)], right[...]))
            at += right.shape[1]


def middle_back(
    total_heads, scalars, total_ref, other_ref, middle_ref, cot_ref, gain_ref, sums_ref, gated_ref,
    gate_gain_ref, w_ref,
    dmiddle_ref, dmix_ref, dgain_ref, dnormed_ref, dattn_ref, cross_ref, dgate_gain_ref, full_ref,
):
    parity = scalars[scalars.shape[0] - 2]
    halves_joined(parity, total_ref, other_ref, full_ref)
    grad = full_ref[...]
    middle = middle_ref[...]
    inv = lax.rsqrt(jnp.mean(middle * middle, axis=-1, keepdims=True) + EPSILON)
    rows = middle * inv
    dgain_ref[...] = jnp.broadcast_to(jnp.sum(grad * rows, axis=0, keepdims=True), dgain_ref.shape)
    scaled = grad * gain_ref[...]
    dmiddle = cot_ref[...].astype(F32) + inv * (
        scaled - rows * jnp.mean(scaled * rows, axis=-1, keepdims=True)
    )
    dmiddle_ref[...] = dmiddle
    dmix_ref[...] = low(dmiddle)
    width = gated_ref.shape[1]
    first = w_ref.shape[1] - width - dattn_ref.shape[1]
    both = mm(dmix_ref[...], w_ref[:, first:])
    dnormed = both[:, :width]
    dnormed_ref[...] = dnormed
    dattn_ref[...] = low(both[:, width:])
    gated = gated_ref[...]
    product = dnormed * gated
    cross_ref[...] = token_sums(product * gate_gain_ref[...])
    inv_gate = as_column(lax.rsqrt(sums_ref[...] / (total_heads * PM) + EPSILON))
    dgate_gain_ref[...] = jnp.broadcast_to(
        jnp.sum(product * inv_gate, axis=0, keepdims=True), dgate_gain_ref.shape
    )


def gate_back(
    heads, total_heads, count, cross_ref, sums_ref, dnormed_ref, gated_ref, gain_ref, zq_ref, y_ref, cum_ref,
    bc_ref, dq_ref, *refs,
):
    msgs, kv = refs[: count - 1], refs[count - 1 : 2 * count - 1]
    dy_ref, dzq_ref = refs[2 * count - 1 : 2 * count + 1]
    sent = refs[2 * count + 1 :]
    width = y_ref.shape[1]
    size = total_heads * PM
    inv = as_column(lax.rsqrt(sums_ref[...] / size + EPSILON))
    cross = as_column(cross_ref[...])
    dgated = inv * dnormed_ref[...] * gain_ref[...] - gated_ref[...] * (inv * inv * inv * cross / size)
    z = zq_ref[:, :width].astype(F32)
    sig = sigmoid(z)
    dy = dgated * (z * sig)
    dy_ref[...] = dy
    dz = low(dgated * y_ref[...] * sig * (1.0 + z * (1.0 - sig)))
    dzq_ref[...] = jnp.concatenate([dz, dq_ref[...]], axis=1)
    weighted = dy * mm(jnp.exp(cum_ref[...]), head_lanes(heads), HIGHEST)
    state = mm_tn(low(bc_ref[:, NS:]), low(weighted))
    for j in range(count):
        sent[j][:NS, :] = low(state)
        sent[j][NS:, :] = kv[j][...]
        if j < count - 1:
            decay = msgs[j][NS : NS + HALO, :].astype(F32)
            state = state * (decay[0:1, :] + decay[1:2, :])


def conv_and_input_back(
    scalars, dpre_ref, next_ref, taps_ref, dkv_ref, ddt_ref, dzq_ref,
    hidden_ref, dgain_mid_ref, dtaps_ref, dgate_gain_ref, dsmall_ref, dskip_ref, tokens_ref, w_ref, more_ref,
    dall_ref, small_ref, keep_ref, give_ref, full_ref,
):
    parity = scalars[scalars.shape[0] - 2]
    dpre = dpre_ref[...]
    rows = dpre.shape[0]
    longer = jnp.concatenate([dpre, next_ref[...]], axis=0)
    total = taps_ref[KC - 1 : KC, :] * dpre
    for k in range(KC - 1):
        shift = KC - 1 - k
        total = total + taps_ref[k : k + 1, :] * pltpu.roll(longer, longer.shape[0] - shift, 0)[:rows]
    dall = jnp.concatenate([low(total), dkv_ref[...], ddt_ref[...]], axis=1)
    dall_ref[...] = dall
    dzq = dzq_ref[...]
    full_ref[...] = mm_nt(dall, w_ref[...]) + mm_nt(dzq, more_ref[:, : dzq.shape[1]])
    x = tokens_ref[...].astype(F32)
    inv = lax.rsqrt(jnp.mean(x * x, axis=-1, keepdims=True) + EPSILON)
    dgain = jnp.sum(full_ref[...] * (x * inv), axis=0, keepdims=True)
    model = x.shape[1]
    place = lax.broadcasted_iota(jnp.int32, (8, model), 0)
    ddt_w = mm_tn(ddt_ref[...], hidden_ref[...])[:8]
    small_ref[:, :model] = jnp.where(place == 6, dgain_mid_ref[...], jnp.where(place == 7, dgain, ddt_w))
    rest = jnp.concatenate([dgate_gain_ref[0:1, :], dsmall_ref[0:1, :], dsmall_ref[1:2, :]], axis=1)
    wide = taps_ref.shape[1]
    skip_row = jnp.concatenate([dskip_ref[0:1, :], jnp.zeros((1, wide - LANES), F32)], axis=1)
    place = lax.broadcasted_iota(jnp.int32, (8, wide), 0)
    small_ref[:, model:] = jnp.where(
        place < KC, dtaps_ref[...], jnp.where(place == KC, rest, jnp.where(place == KC + 1, skip_row, 0.0))
    )
    halves_to_sum(parity, full_ref, keep_ref, give_ref)


def input_back(scalars, total_ref, other_ref, tokens_ref, gain_ref, dmiddle_ref, dtokens_ref, full_ref):
    parity = scalars[scalars.shape[0] - 2]
    halves_joined(parity, total_ref, other_ref, full_ref)
    grad = full_ref[...]
    x = tokens_ref[...].astype(F32)
    inv = lax.rsqrt(jnp.mean(x * x, axis=-1, keepdims=True) + EPSILON)
    rows = x * inv
    scaled = grad * gain_ref[...]
    dtokens_ref[...] = dmiddle_ref[...] + inv * (
        scaled - rows * jnp.mean(scaled * rows, axis=-1, keepdims=True)
    )


def output_sum(scalars, total_ref, other_ref, middle_ref, out_ref, full_ref):
    halves_joined(scalars[scalars.shape[0] - 2], total_ref, other_ref, full_ref)
    out_ref[...] = low(middle_ref[...] + full_ref[...])


def send(x, axis, pairs):
    return lax.ppermute(x, axis, pairs)


def from_ahead(x, axis, distance):
    n = lax.axis_size(axis)
    return send(x, axis, [((i + distance) % n, i) for i in range(n)])


def from_earlier(x, distance):
    n = lax.axis_size("row")
    return send(x, "row", [(i - distance, i) for i in range(distance, n)])


def from_later(x, distance):
    n = lax.axis_size("row")
    return send(x, "row", [(i + distance, i) for i in range(n - distance)])


def swap(x, axis, bit):
    return send(x, axis, [(i, i ^ bit) for i in range(lax.axis_size(axis))])


def after(x, *others):
    return lax.optimization_barrier((x,) + others)[0]


def after_all(*values):
    return lax.optimization_barrier(values)


def direct():
    return lax.axis_size("dp") == 2 and lax.axis_size("row") == 4


def scatter_first(parts):
    if len(parts) == 1:
        return [lax.psum_scatter(parts[0], ("dp", "row"), scatter_dimension=0, tiled=True)]
    half = parts[1].shape[0] // 2
    return [swap(parts[1][half:], "dp", 1), swap(parts[1][:half], "dp", 1)]


def scatter_beside(parts, got):
    if len(parts) == 1:
        return got[0]
    half = parts[0].shape[0] // 2
    return swap(low(parts[0][half:].astype(F32) + got[0].astype(F32)), "row", 1)


def scatter_last(parts, got, beside):
    if len(parts) == 1:
        return beside.astype(F32)
    blk = parts[0].shape[0] // 4
    total = parts[0][: 2 * blk].astype(F32) + got[1].astype(F32) + beside.astype(F32)
    return total[:blk] + swap(low(total[blk:]), "row", 2).astype(F32)


def col_sum(keep, give, *others):
    part = low(keep + swap(give, "col", 1).astype(F32))
    if others:
        part = after(part, *others)
    total = low(part.astype(F32) + swap(part, "col", 2).astype(F32))
    return total, swap(total, "col", 1)


def low_col_sum(values):
    values = low(values)
    values = low(values.astype(F32) + swap(values, "col", 1).astype(F32))
    return values.astype(F32) + swap(values, "col", 2).astype(F32)


def tiny_col_sum(values):
    values = values + swap(values, "col", 1)
    return values + swap(values, "col", 2)


def tiny_row_sum(values):
    if lax.axis_size("dp") == 2:
        values = values + swap(values, "dp", 1)
    else:
        values = lax.psum(values, "dp")
    values = values + swap(values, "row", 1)
    return values + swap(values, "row", 2)


def per_device(
    tokens, cotangent, norm_in, z_weight, x_weight, dt_weight, q_weight, bc_weight, key_value_weight,
    conv_x, conv_bc, dt_bias, a_log, d_skip, gate_gain, mamba_weight, attn_weight, norm_mid,
    gate_weight, up_weight, down_weight,
):
    dp_n, row_n, col_n = (lax.axis_size(a) for a in ("dp", "row", "col"))
    dp, row, col = (lax.axis_index(a) for a in ("dp", "row", "col"))
    if row_n != 4 or col_n != 4:
        raise ValueError("row, col: 4")
    rows, model = tokens.shape
    seq = rows * row_n
    heads = dt_bias.shape[0]
    total_heads = heads * col_n
    width = heads * PM
    q_width = q_weight.shape[1]
    q_heads = q_width // HEAD_DIM
    hidden = gate_weight.shape[1]
    blk = model // (dp_n * row_n)
    kv_group = col * q_heads * KEY_HEADS // QUERY_HEADS
    conv_width = width + 2 * NS
    in_width = conv_width + 2 * LANES

    shard_in = jnp.concatenate(
        [
            x_weight,
            bc_weight,
            lax.dynamic_slice_in_dim(key_value_weight, kv_group * HEAD_DIM, HEAD_DIM, 1),
            lax.dynamic_slice_in_dim(key_value_weight, (KEY_HEADS + kv_group) * HEAD_DIM, HEAD_DIM, 1),
            dt_weight,
            jnp.zeros((blk, LANES - heads), BF16),
        ],
        axis=1,
    )
    shard_mix = jnp.concatenate([z_weight, q_weight, mamba_weight.T, attn_weight.T], axis=1)
    shard_ff = jnp.concatenate([gate_weight, up_weight, down_weight.T], axis=1)
    halo = from_earlier(tokens[rows - HALO :], 1)
    ext = jnp.concatenate([halo, tokens], axis=0).astype(F32)
    inv_in = lax.rsqrt(jnp.mean(ext * ext, axis=-1, keepdims=True) + EPSILON)
    hidden_ext = low(ext * inv_in * norm_in)
    hidden_in = hidden_ext[HALO:]

    if direct():
        order = [((dp + i) % 2) * row_n + (row ^ x) for i in range(2) for x in (0, 2, 1, 3)]
        across, beside = swap(shard_in, "row", 2), swap(shard_in, "row", 1)
        own = swap(shard_in, "dp", 1)
        across, beside, own, hidden_ext, shard_ff = after_all(across, beside, own, hidden_ext, shard_ff)
        corner = swap(across, "row", 1)
        over = [swap(across, "dp", 1), swap(beside, "dp", 1)]
        ff_across = swap(shard_ff, "row", 2)
        corner, ff_across, shard_mix, shard_ff, *over = after_all(corner, ff_across, shard_mix, shard_ff, *over)
        last = swap(corner, "dp", 1)
        mix_across, mix_beside = swap(shard_mix, "row", 2), swap(shard_mix, "row", 1)
        ff_beside = swap(shard_ff, "row", 1)
        mix_own, ff_own = swap(shard_mix, "dp", 1), swap(shard_ff, "dp", 1)
        last, mix_across, mix_beside, ff_beside, mix_own, ff_own = after_all(
            last, mix_across, mix_beside, ff_beside, mix_own, ff_own
        )
        in_blocks = [shard_in, across, beside, corner, own] + over + [last]
        mix_corner = swap(mix_across, "row", 1)
        mix_over = [swap(v, "dp", 1) for v in (mix_across, mix_beside)]
    else:
        in_blocks = [lax.all_gather(shard_in, ("dp", "row"), axis=0, tiled=True)]
        mix_blocks = [lax.all_gather(shard_mix, ("dp", "row"), axis=0, tiled=True)]
        ff_blocks = [lax.all_gather(shard_ff, ("dp", "row"), axis=0, tiled=True)]
        order = [jnp.int32(0)]
    scalars = jnp.stack([jnp.int32(v) for v in order] + [jnp.int32(col % 2), jnp.int32(row)])

    positions = (row * rows + jnp.arange(rows, dtype=jnp.int32)).astype(F32)
    half = HEAD_DIM // 2
    frequency = ROPE_BASE ** (-jnp.arange(half).astype(F32) / half)
    angles = positions[:, None] * frequency[None, :]
    cosine, sine = jnp.cos(angles), jnp.sin(angles)
    cos_q = jnp.concatenate([cosine] * (2 * q_heads), axis=1)
    sin_q = jnp.concatenate([sine] * (2 * q_heads), axis=1)
    cos_kv = jnp.concatenate([cosine, cosine, jnp.ones((rows, HEAD_DIM), F32)], axis=1)
    sin_kv = jnp.concatenate([sine, sine, jnp.zeros((rows, HEAD_DIM), F32)], axis=1)

    taps = jnp.concatenate([conv_x, conv_bc], axis=1)
    rate = -jnp.exp(a_log)

    def lane_row(v):
        return jnp.pad(v, (0, LANES - heads))[None, :]

    params = jnp.concatenate([lane_row(dt_bias), lane_row(rate), jnp.zeros((6, LANES), F32)], axis=0)
    skip = jnp.repeat(d_skip, PM)[None, :]
    area = rows * rows * heads
    part = packed_rows(rows, width)
    y_base, msg, proj, x_heads, bc_map, slope, cum, step, in_full = kernel_call(
        partial(scan_local, heads),
        (
            ((rows, width), F32),
            ((NS + HALO + 2 * part, width), BF16),
            ((HALO + rows, in_width), BF16),
            ((rows, width), F32),
            ((rows, 2 * NS), F32),
            ((rows, conv_width), F32),
            ((rows, LANES), F32),
            ((rows, LANES), F32),
        ),
        (area * 2 * PM * 10, 4000000, area),
        scalars,
        hidden_ext,
        taps,
        params,
        skip,
        cos_kv,
        sin_kv,
        in_blocks,
        keep=True,
        near=True,
    )
    if direct():
        msg, mix_corner, ff_across, *mix_over = after_all(msg, mix_corner, ff_across, *mix_over)
        msgs = [from_earlier(msg, j) for j in range(1, row_n)]
        mix_over.append(swap(mix_corner, "dp", 1))
        ff_over = [swap(ff_across, "dp", 1)]
        ff_across, ff_beside, ff_over[0], *moved = after_all(ff_across, ff_beside, ff_over[0], *mix_over, *msgs)
        mix_over, msgs = moved[:3], moved[3:]
        mix_blocks = [shard_mix, mix_across, mix_beside, mix_corner, mix_own] + mix_over
        ff_corner = swap(ff_across, "row", 1)
        ff_over.append(swap(ff_beside, "dp", 1))
    else:
        msgs = [from_earlier(msg, j) for j in range(1, row_n)]
    zq, mix_full = kernel_call(
        project,
        (((rows, width + q_width), BF16),),
        (2 * rows * model * (width + q_width), 4000000, 0),
        scalars,
        hidden_in,
        mix_blocks,
        keep=True,
    )

    (
        attn_value, probs, query, key, value, state_in, carried, y, gated, sums,
    ) = kernel_call(
        partial(mix_tokens, heads, row_n - 1),
        (
            ((rows, q_width), BF16),
            ((q_heads * rows, seq), BF16),
            ((q_heads * rows, HEAD_DIM), BF16),
            ((seq, HEAD_DIM), BF16),
            ((seq, HEAD_DIM), BF16),
            ((NS, width), F32),
            ((rows, width), F32),
            ((rows, width), F32),
            ((rows, width), F32),
            ((8, rows), F32),
        ),
        (8 * q_width * rows * seq, 6000000, q_heads * rows * seq),
        scalars,
        msg,
        *msgs,
        y_base,
        cum,
        bc_map,
        zq,
        cos_q,
        sin_q,
    )
    sums = tiny_col_sum(sums)
    gain_row = gate_gain[None, :]
    halves = (((rows // 2, model), F32), ((rows // 2, model), BF16))
    full_scratch = ((rows, model), F32)
    mamba_normed, keep, give, _ = kernel_call(
        partial(mix_out, total_heads),
        (((rows, width), BF16),) + halves + (full_scratch,),
        (2 * rows * model * (width + q_width), 4000000, 0),
        scalars,
        sums,
        gated,
        gain_row,
        attn_value,
        mix_full,
    )
    if direct():
        give, ff_corner, *ff_over = after_all(give, ff_corner, *ff_over)
        ff_blocks = [shard_ff, ff_across, ff_beside, ff_corner, ff_own] + ff_over + [swap(ff_corner, "dp", 1)]
    total, other = col_sum(keep, give)

    gain_mid = norm_mid[None, :]
    middle, hidden_mid, grad_gate_up, swiglu, keep, give, out_keep, out_give, _ = kernel_call(
        feed_forward,
        (
            ((rows, model), F32),
            ((rows, model), BF16),
            ((rows, 2 * hidden), BF16),
            ((rows, hidden), BF16),
        )
        + halves
        + halves
        + (full_scratch,),
        (14 * rows * model * hidden, 8000000, rows * hidden),
        scalars,
        total,
        other,
        [tokens],
        [cotangent],
        gain_mid,
        ff_blocks,
    )

    def weight_grad(*operands):
        columns = sum(v.shape[1] for v in operands[1::2])
        outs = 2 if direct() else 1
        return kernel_call(
            partial(weight_products, len(order)),
            (((model // outs, columns), BF16),) * outs,
            (2 * rows * model * columns, 5000000, 0),
            scalars,
            *operands,
        )

    ff_parts = weight_grad(hidden_mid, grad_gate_up, cotangent, swiglu)
    total, other = col_sum(keep, give, *ff_parts)
    if direct():
        near = ff_parts[1].shape[0] // 2
        ff_got = [swap(ff_parts[1][near:], "dp", 1)]
    else:
        ff_got = scatter_first(ff_parts)

    grad_middle, grad_mix, dgain_mid, grad_normed, grad_attn, cross, dgate_gain, _ = kernel_call(
        partial(middle_back, total_heads),
        (
            ((rows, model), F32),
            ((rows, model), BF16),
            ((8, model), F32),
            ((rows, width), F32),
            ((rows, q_width), BF16),
            ((8, rows), F32),
            ((8, width), F32),
            full_scratch,
        ),
        (2 * rows * model * (width + q_width), 6000000, 0),
        scalars,
        total,
        other,
        middle,
        [cotangent],
        gain_mid,
        sums,
        gated,
        gain_row,
        mix_full,
    )
    cross = tiny_col_sum(cross)
    if direct():
        ff_got.append(swap(after(ff_parts[1][:near], grad_mix), "dp", 1))
        cross, ff_got[0] = after_all(cross, ff_got[0])
    grad_query, grad_kv_own, *kv_sent = kernel_call(
        attend_back,
        (((rows, q_width), BF16), ((rows, LANES), F32)) + (((2 * part, width), BF16),) * (row_n - 1),
        (16 * q_width * rows * seq, 4000000, 0),
        None,
        grad_attn,
        probs,
        query,
        cos_q,
        sin_q,
        key,
        value,
    )
    grad_y, grad_zq, *sent = kernel_call(
        partial(gate_back, heads, total_heads, row_n - 1),
        (((rows, width), F32), ((rows, width + q_width), BF16)) + (((NS + 2 * part, width), BF16),) * (row_n - 1),
        (2 * rows * NS * width, 4000000, rows * width),
        None,
        cross,
        sums,
        grad_normed,
        gated,
        gain_row,
        zq,
        y,
        cum,
        bc_map,
        grad_query,
        *msgs[: row_n - 2],
        *kv_sent,
    )
    got = [from_later(sent[j - 1], j) for j in range(1, row_n)]
    dx_local, dbc_local, dcum, dstep, dskip = kernel_call(
        partial(scan_back_local, heads),
        (
            ((rows, width), F32),
            ((rows, 2 * NS), F32),
            ((rows, LANES), F32),
            ((rows, LANES), F32),
            ((8, LANES), F32),
        ),
        (area * 2 * PM * 20, 4000000, area),
        None,
        grad_y,
        x_heads,
        bc_map,
        cum,
        step,
        carried,
        state_in,
        skip,
    )
    act = jnp.concatenate([mamba_normed, attn_value], axis=1)
    mix_parts = weight_grad(hidden_in, grad_zq, grad_mix, act)
    mix_got = scatter_first(mix_parts)
    got = list(after(tuple(got), mix_parts, mix_got[0]))

    dpre, first, grad_dt, grad_kv, dsmall, dtaps = kernel_call(
        partial(scan_back_end, heads, row_n - 1),
        (
            ((rows, conv_width), F32),
            ((8, conv_width), F32),
            ((rows, LANES), BF16),
            ((rows, LANES), BF16),
            ((8, LANES), F32),
            ((8, conv_width), F32),
        ),
        (rows * NS * width * 10, 4000000, rows * LANES * 3),
        None,
        *got,
        state_in,
        x_heads,
        bc_map,
        cum,
        step,
        dx_local,
        dbc_local,
        dcum,
        dstep,
        slope,
        proj,
        params,
        grad_kv_own,
        cos_kv,
        sin_kv,
    )
    following = from_later(first, 1)
    following = after(following, ff_got, mix_got)
    ff_beside = scatter_beside(ff_parts, [after(ff_got[0], following)])

    grad_all, small, keep, give, _ = kernel_call(
        conv_and_input_back,
        (((rows, in_width), BF16), ((8, model + conv_width), F32)) + halves + (full_scratch,),
        (2 * rows * model * (in_width + width + q_width), 8000000, 0),
        scalars,
        dpre,
        following,
        taps,
        grad_kv,
        grad_dt,
        grad_zq,
        hidden_in,
        dgain_mid,
        dtaps,
        dgate_gain,
        dsmall,
        dskip,
        [tokens],
        in_full,
        mix_full,
    )
    tail_width = conv_width + LANES
    tail_parts = weight_grad(hidden_in, grad_all[:, :tail_width])
    tail_got = scatter_first(tail_parts)
    mix_beside = scatter_beside(mix_parts, [after(mix_got[0], ff_beside, tail_got)])
    total, other = col_sum(keep, give)
    grad_ff = scatter_last(ff_parts, ff_got, after(ff_beside, tail_got[0]))
    out_total, out_other = col_sum(out_keep, after(out_give, total))
    layer_out, _ = kernel_call(
        output_sum,
        (((rows, model), BF16), full_scratch),
        (rows * model, 3000000, 0),
        scalars,
        out_total,
        out_other,
        middle,
    )
    tail_beside = scatter_beside(tail_parts, [after(tail_got[0], ff_beside)])
    grad_in_w = scatter_last(tail_parts, tail_got, tail_beside)
    grad_mix_w = scatter_last(mix_parts, mix_got, after(mix_beside, tail_beside))
    grad_tokens, _ = kernel_call(
        input_back,
        (((rows, model), F32), full_scratch),
        (rows * model * 10, 4000000, 0),
        scalars,
        total,
        other,
        [tokens],
        norm_in[None, :],
        [grad_middle],
    )

    bc_w = grad_in_w[:, width:conv_width]
    kv_w = grad_in_w[:, conv_width:]
    spot = (jnp.arange(KEY_HEADS) == kv_group).astype(F32)
    wide = [spot[i] * kv_w[:, :HEAD_DIM] for i in range(KEY_HEADS)]
    wide += [spot[i] * kv_w[:, HEAD_DIM:] for i in range(KEY_HEADS)]
    shared = jnp.concatenate([bc_w] + wide, axis=1)
    shared = low_col_sum(shared)

    line = lax.broadcasted_iota(jnp.int32, small.shape, 0)
    lane = lax.broadcasted_iota(jnp.int32, small.shape, 1)
    partial_lanes = ((line == 7) & (lane < model)) | ((line < KC) & (lane >= model + width))
    small = jnp.where(partial_lanes, tiny_col_sum(small), small)
    small = tiny_row_sum(after(small, tail_beside))
    taps_at = model + width
    place = (dp * row_n + row) * blk
    return (
        layer_out,
        grad_tokens,
        small[7, :model],
        grad_mix_w[:, :width],
        grad_in_w[:, :width],
        lax.dynamic_slice(small, (0, place), (heads, blk)).T,
        grad_mix_w[:, width : width + q_width],
        shared[:, : 2 * NS],
        shared[:, 2 * NS :],
        small[:KC, model:taps_at],
        small[:KC, taps_at:],
        small[KC, taps_at : taps_at + heads],
        small[KC, taps_at + LANES : taps_at + LANES + heads],
        small[KC + 1, model : model + heads],
        small[KC, model:taps_at],
        grad_mix_w[:, width + q_width : 2 * width + q_width].T,
        grad_mix_w[:, 2 * width + q_width :].T,
        small[6, :model],
        grad_ff[:, :hidden],
        grad_ff[:, hidden : 2 * hidden],
        grad_ff[:, 2 * hidden :].T,
    )


def solution(mesh):
    by_rows = P(("dp", "row"), None)
    both = P(("dp", "row"), "col")
    turned = P("col", ("dp", "row"))
    per_col = P("col")
    taps = P(None, "col")
    in_specs = (
        by_rows, by_rows, P(), both, both, both, both, by_rows, by_rows, taps, P(), per_col, per_col,
        per_col, per_col, turned, turned, P(), both, both, turned,
    )
    out_specs = (
        by_rows, by_rows, P(), both, both, both, both, by_rows, by_rows, taps, P(), per_col, per_col,
        per_col, per_col, turned, turned, P(), both, both, turned,
    )
    return jax.shard_map(
        per_device, mesh=mesh, in_specs=in_specs, out_specs=out_specs, check_vma=False
    )
```

```python
from functools import partial

import jax
import jax.numpy as jnp
from jax import lax
from jax.experimental import pallas as pl
from jax.experimental.pallas import tpu as pltpu
from jax.sharding import PartitionSpec as P

HM = 24
PM = 64
NS = 128
KC = 4
QUERY_HEADS = 8
KEY_HEADS = 2
HEAD_DIM = 64
HALO = 16
LANES = 128

EPSILON = 1e-05
ROPE_BASE = 100000000000.0
NEG_LARGE = -1e30
HIGHEST = lax.Precision.HIGHEST
F32 = jnp.float32
BF16 = jnp.bfloat16


def mm(a, b, precision=None):
    return lax.dot_general(
        a, b, (((1,), (0,)), ((), ())), precision=precision, preferred_element_type=F32
    )


def mm_nt(a, b, precision=None):
    return lax.dot_general(
        a, b, (((1,), (1,)), ((), ())), precision=precision, preferred_element_type=F32
    )


def mm_tn(a, b, precision=None):
    return lax.dot_general(
        a, b, (((0,), (0,)), ((), ())), precision=precision, preferred_element_type=F32
    )


def low(v):
    return v.astype(BF16)


def sigmoid(v):
    return 1.0 / (1.0 + jnp.exp(-v))


def softplus(v):
    return jnp.maximum(v, 0.0) + jnp.log1p(jnp.exp(-jnp.abs(v)))


def head_lanes(heads):
    head = lax.broadcasted_iota(jnp.int32, (LANES, heads * PM), 0)
    column = lax.broadcasted_iota(jnp.int32, (LANES, heads * PM), 1)
    return ((column >= head * PM) & (column < head * PM + PM)).astype(F32)


def lower_triangle(size):
    later = lax.broadcasted_iota(jnp.int32, (size, size), 0)
    earlier = lax.broadcasted_iota(jnp.int32, (size, size), 1)
    return later >= earlier


def split_pair(pair):
    first = lax.broadcasted_iota(jnp.int32, pair.shape, 1) < PM
    zero = jnp.zeros_like(pair)
    return jnp.concatenate([jnp.where(first, pair, zero), jnp.where(first, zero, pair)], axis=0)


def kernel_call(body, outs, cost, scalars, *operands, keep=False, near=False):
    flops, traffic, exps = cost
    flat, in_specs, scratch, plan = [], [], [], []
    if scalars is not None:
        flat.append(scalars)
        in_specs.append(pl.BlockSpec(memory_space=pltpu.SMEM))
    for operand in operands:
        parts = operand if isinstance(operand, list) else [operand]
        plan.append((len(flat), len(parts), isinstance(operand, list)))
        flat += parts
        space = pl.ANY if isinstance(operand, list) and not near else pltpu.VMEM
        in_specs += [pl.BlockSpec(memory_space=space)] * len(parts)
        if isinstance(operand, list):
            whole = (sum(v.shape[0] for v in parts), parts[0].shape[1])
            scratch.append(pltpu.VMEM(whole, parts[0].dtype))
            last = (whole, parts[0].dtype)
    if keep:
        scratch.pop()
        outs = tuple(outs) + (last,)
    copied = sum(n for _, n, outside in plan if outside)
    if copied:
        scratch.append(pltpu.SemaphoreType.DMA((copied,)))

    def run(*refs):
        ins, results, held = refs[: len(flat)], refs[len(flat) : len(flat) + len(outs)], refs[len(flat) + len(outs) :]
        views = [ins[0]] if scalars is not None else []
        copies, taken = [], 0
        for start, n, outside in plan:
            if not outside:
                views.append(ins[start])
                continue
            target = results[-1] if keep and taken == len(scratch) - 1 else held[taken]
            taken += 1
            views.append(target)
            for i in range(n):
                size = ins[start + i].shape[0]
                place = target if n == 1 else target.at[lanes_of(ins[0], i, size), :]
                copies.append(pltpu.make_async_copy(ins[start + i], place, held[-1].at[len(copies)]))
        for c in copies:
            c.start()
        for c in copies:
            c.wait()
        body(*views, *(results[:-1] if keep else results))

    return pl.pallas_call(
        run,
        out_shape=tuple(jax.ShapeDtypeStruct(s, d) for s, d in outs),
        in_specs=in_specs,
        out_specs=tuple(pl.BlockSpec(memory_space=pltpu.VMEM) for _ in outs),
        scratch_shapes=scratch,
        compiler_params=pltpu.CompilerParams(vmem_limit_bytes=24 * 1024 * 1024),
        cost_estimate=pl.CostEstimate(flops=flops, bytes_accessed=traffic, transcendentals=exps),
    )(*flat)


def lanes_of(scalars, p, size):
    return pl.ds(pl.multiple_of(scalars[p] * size, size), size)


def rows_half(parity, rows, own):
    half = rows // 2
    return pl.ds(pl.multiple_of((parity if own else 1 - parity) * half, half), half)


def halves_to_sum(parity, full_ref, keep_ref, give_ref):
    rows = full_ref.shape[0]
    keep_ref[...] = full_ref[rows_half(parity, rows, True), :]
    give_ref[...] = low(full_ref[rows_half(parity, rows, False), :])


def halves_joined(parity, total_ref, other_ref, full_ref):
    rows = full_ref.shape[0]
    full_ref[rows_half(parity, rows, True), :] = total_ref[...].astype(F32)
    full_ref[rows_half(parity, rows, False), :] = other_ref[...].astype(F32)


def pack_rows(v, width):
    count = width // HEAD_DIM
    chunk = packed_rows(v.shape[0], width)
    pieces = []
    for i in range(count):
        piece = v[i * chunk : min((i + 1) * chunk, v.shape[0])]
        if piece.shape[0] < chunk:
            piece = jnp.concatenate([piece, jnp.zeros((chunk - piece.shape[0], HEAD_DIM), v.dtype)], axis=0)
        pieces.append(piece)
    return jnp.concatenate(pieces, axis=1)


def packed_rows(rows, width):
    count = width // HEAD_DIM
    return -(-rows // (16 * count)) * 16


def unpack_rows(v, rows):
    count = v.shape[1] // HEAD_DIM
    return jnp.concatenate([v[:, i * HEAD_DIM : (i + 1) * HEAD_DIM] for i in range(count)], axis=0)[:rows]


def token_sums(v):
    return mm_nt(jnp.ones((8, v.shape[1]), F32), v, HIGHEST)


def as_column(v):
    return jnp.transpose(v)[:, :1]


def scan_local(
    heads, scalars, hidden_ref, taps_ref, par_ref, skip_ref, cos_ref, sin_ref, w_ref,
    y_ref, msg_ref, proj_ref, x_ref, bc_ref, slope_ref, cum_ref, step_ref,
):
    width = heads * PM
    conv_width = width + 2 * NS
    rows = y_ref.shape[0]
    proj = low(mm(hidden_ref[...], w_ref[...]))
    proj_ref[...] = proj
    ext = proj[:, :conv_width].astype(F32)
    pre = taps_ref[KC - 1 : KC, :] * ext[HALO:]
    for k in range(KC - 1):
        pre = pre + taps_ref[k : k + 1, :] * pltpu.roll(ext, KC - 1 - k, 0)[HALO:]
    sig = sigmoid(pre)
    conv_out = pre * sig
    slope_ref[...] = sig * (1.0 + pre * (1.0 - sig))
    x = conv_out[:, :width]
    x_ref[...] = x
    bc_ref[...] = conv_out[:, width:]
    b_map = low(conv_out[:, width : width + NS])
    c_map = low(conv_out[:, width + NS :])
    raw = proj[HALO:, conv_width + LANES :].astype(F32) + par_ref[0:1, :]
    lane = lax.broadcasted_iota(jnp.int32, raw.shape, 1)
    step = jnp.where(lane < heads, softplus(raw), 0.0)
    step_ref[...] = step
    causal = lower_triangle(rows)
    cum = mm(causal.astype(F32), step * par_ref[1:2, :], HIGHEST)
    cum_ref[...] = cum
    spread = head_lanes(heads)
    last = cum[rows - 1 : rows, :]
    tail = mm(jnp.exp(last - cum) * step, spread, HIGHEST)
    msg_ref[:NS, :] = low(mm_tn(b_map, low(x * tail)))
    decay = mm(jnp.exp(jnp.broadcast_to(last, (HALO, LANES))), spread, HIGHEST)
    coarse = low(decay)
    fine = low(decay - coarse.astype(F32))
    place = lax.broadcasted_iota(jnp.int32, decay.shape, 0)
    msg_ref[NS : NS + HALO, :] = low(jnp.where(place == 0, coarse.astype(F32), fine.astype(F32)))
    kv = proj[HALO:, conv_width : conv_width + LANES]
    turned = mm(kv, low(quarter_turn(LANES)))
    kv = low(kv.astype(F32) * cos_ref[...] + turned * sin_ref[...])
    part = packed_rows(rows, width)
    at = NS + HALO
    msg_ref[at : at + part, :] = pack_rows(kv[:, :HEAD_DIM], width)
    msg_ref[at + part : at + 2 * part, :] = pack_rows(kv[:, HEAD_DIM:], width)
    cum_t = jnp.transpose(cum)
    step_t = jnp.transpose(step)
    meet = jnp.where(causal, mm_nt(c_map, b_map), 0.0)
    for pair in range(heads // 2):
        mixing = []
        for h in (2 * pair, 2 * pair + 1):
            gap = jnp.minimum(cum[:, h : h + 1] - cum_t[h : h + 1, :], 0.0)
            mixing.append(low(meet * jnp.exp(gap) * step_t[h : h + 1, :]))
        lanes = slice(pair * LANES, (pair + 1) * LANES)
        y_ref[:, lanes] = (
            mm(jnp.concatenate(mixing, axis=1), split_pair(low(x[:, lanes])))
            + skip_ref[0:1, lanes] * x[:, lanes]
        )


def scan_back_local(
    heads, dy_ref, x_ref, bc_ref, cum_ref, step_ref, carried_ref, state_ref, skip_ref,
    dx_ref, dbc_ref, dcum_ref, dstep_ref, dskip_ref,
):
    rows = dy_ref.shape[0]
    dy = dy_ref[...]
    x = x_ref[...]
    b_map = low(bc_ref[:, :NS])
    c_map = low(bc_ref[:, NS:])
    cum = cum_ref[...]
    step = step_ref[...]
    cum_t = jnp.transpose(cum)
    step_t = jnp.transpose(step)
    causal = lower_triangle(rows)
    meet = jnp.where(causal, mm_nt(c_map, b_map), 0.0)
    lane = lax.broadcasted_iota(jnp.int32, (rows, LANES), 1)
    dmeet = jnp.zeros((rows, rows), F32)
    row_part = jnp.zeros((rows, LANES), F32)
    column_sums = []
    for pair in range(heads // 2):
        lanes = slice(pair * LANES, (pair + 1) * LANES)
        x_pair = low(x[:, lanes])
        dy_split = split_pair(low(dy[:, lanes]))
        dmix_both = mm_nt(dy_split, x_pair)
        mixing = []
        for i in range(2):
            h = 2 * pair + i
            dmix = dmix_both[i * rows : (i + 1) * rows]
            gap = jnp.minimum(cum[:, h : h + 1] - cum_t[h : h + 1, :], 0.0)
            decay = jnp.where(causal, jnp.exp(gap), 0.0)
            row_step = step_t[h : h + 1, :]
            decay_step = decay * row_step
            dmeet = dmeet + dmix * decay_step
            mixing.append(low(meet * decay_step))
            ratio = dmix * meet * decay
            column_sums.append(jnp.sum(ratio, axis=0, keepdims=True))
            row_sum = jnp.sum(ratio * row_step, axis=1, keepdims=True)
            row_part = row_part + jnp.where(lane == h, row_sum, 0.0)
        dx_ref[:, lanes] = (
            mm_tn(jnp.concatenate(mixing, axis=0), dy_split) + skip_ref[0:1, lanes] * dy[:, lanes]
        )
    column_sums.append(jnp.zeros((LANES - heads, rows), F32))
    dstep = jnp.transpose(jnp.concatenate(column_sums, axis=0))
    dstep_ref[...] = dstep
    spread = head_lanes(heads)
    weighted = dy * mm(jnp.exp(cum), spread, HIGHEST)
    dcum_ref[...] = row_part - dstep * step + mm_nt(weighted * carried_ref[...], spread, HIGHEST)
    dmeet_low = low(dmeet)
    dbc_ref[:, :NS] = mm_tn(dmeet_low, c_map)
    dbc_ref[:, NS:] = mm(dmeet_low, b_map) + mm_nt(low(weighted), low(state_ref[...]))
    dskip = jnp.broadcast_to(jnp.sum(dy * x, axis=0, keepdims=True), (8, dy.shape[1]))
    dskip_ref[...] = mm_nt(dskip, spread, HIGHEST)


def scan_back_end(
    heads, count, *refs
):
    got = refs[:count]
    (
        state_ref, x_ref, bc_ref, cum_ref, step_ref, dx_ref, dbc_ref, dcum_ref, dstep_ref, slope_ref,
        proj_ref, par_ref, dkv_ref, cos_ref, sin_ref,
        dpre_ref, first_ref, ddt_ref, dkv_out_ref, small_ref, dtaps_ref,
    ) = refs[count:]
    width = heads * PM
    conv_width = width + 2 * NS
    rows = x_ref.shape[0]
    part = packed_rows(rows, width)
    dkv = dkv_ref[...]
    dstate = jnp.zeros((NS, width), F32)
    for g in got:
        dstate = dstate + g[:NS, :].astype(F32)
        key = unpack_rows(g[NS : NS + part, :], rows)
        value = unpack_rows(g[NS + part : NS + 2 * part, :], rows)
        dkv = dkv + jnp.concatenate([key, value], axis=1).astype(F32)
    turned = mm(dkv, quarter_turn(LANES), HIGHEST)
    dkv_out_ref[...] = low(dkv * cos_ref[...] - turned * sin_ref[...])
    x = x_ref[...]
    b_map = low(bc_ref[:, :NS])
    cum = cum_ref[...]
    step = step_ref[...]
    spread = head_lanes(heads)
    last = cum[rows - 1 : rows, :]
    fade = jnp.exp(last - cum)
    tail = fade * step
    wide_tail = mm(tail, spread, HIGHEST)
    dstate_low = low(dstate)
    reach = mm(b_map, dstate_low)
    dx = dx_ref[...] + wide_tail * reach
    db = dbc_ref[:, :NS] + mm_nt(low(x * wide_tail), dstate_low)
    value = mm_nt(x * reach, spread, HIGHEST)
    total = jnp.sum(dstate * state_ref[...], axis=0, keepdims=True)
    dtotal = mm_nt(jnp.broadcast_to(total, (8, width)), spread, HIGHEST)[0:1, :]
    held = tail * value
    at_end = jnp.exp(last) * dtotal + jnp.sum(held, axis=0, keepdims=True)
    upper = jnp.where(lower_triangle(rows), 1.0, 0.0)
    drate = mm_tn(upper, dcum_ref[...] - held, HIGHEST) + at_end
    dstep = dstep_ref[...] + fade * value + drate * par_ref[1:2, :]
    raw = proj_ref[HALO:, conv_width + LANES :].astype(F32) + par_ref[0:1, :]
    lane = lax.broadcasted_iota(jnp.int32, raw.shape, 1)
    ddt = jnp.where(lane < heads, dstep * sigmoid(raw), 0.0)
    ddt_ref[...] = low(ddt)
    dbias = jnp.sum(ddt, axis=0, keepdims=True)
    dlog = jnp.sum(drate * step, axis=0, keepdims=True) * par_ref[1:2, :]
    place = lax.broadcasted_iota(jnp.int32, (8, LANES), 0)
    small_ref[...] = jnp.where(place == 0, dbias, jnp.where(place == 1, dlog, 0.0))
    dpre = jnp.concatenate([dx, db, dbc_ref[:, NS:]], axis=1) * slope_ref[...]
    dpre_ref[...] = dpre
    first_ref[...] = dpre[:8]
    ext = proj_ref[:, :conv_width].astype(F32)
    sums = [
        jnp.sum(dpre * (pltpu.roll(ext, KC - 1 - k, 0) if k < KC - 1 else ext)[HALO:], axis=0, keepdims=True)
        for k in range(KC)
    ]
    dtaps_ref[...] = jnp.concatenate(sums + [jnp.zeros((8 - KC, conv_width), F32)], axis=0)


def heads_to_rows(v):
    return jnp.concatenate([v[:, i * HEAD_DIM : (i + 1) * HEAD_DIM] for i in range(v.shape[1] // HEAD_DIM)], axis=0)


def rows_to_heads(v, count):
    rows = v.shape[0] // count
    return jnp.concatenate([v[i * rows : (i + 1) * rows] for i in range(count)], axis=1)


def quarter_turn(width):
    source = lax.broadcasted_iota(jnp.int32, (width, width), 0)
    target = lax.broadcasted_iota(jnp.int32, (width, width), 1)
    half = HEAD_DIM // 2
    upper = (target & (HEAD_DIM - 1)) >= half
    from_first = jnp.where(source == target - half, 1.0, 0.0)
    from_second = jnp.where(source == target + half, -1.0, 0.0)
    return jnp.where(upper, from_first, from_second)


def mix_tokens(
    heads, count, scalars, own_ref, *refs
):
    msgs = refs[:count]
    (
        y_ref, cum_ref, bc_ref, zq_ref, cos_ref, sin_ref,
        out_ref, probs_ref, query_ref, key_ref, value_ref, state_ref, carried_ref, y_out_ref, gated_ref, sums_ref,
    ) = refs[count:]
    row = scalars[scalars.shape[0] - 1]
    rows, width = y_ref.shape
    at = NS + HALO
    part = packed_rows(rows, width)
    everyone = (own_ref,) + msgs
    key = jnp.concatenate([unpack_rows(m[at : at + part, :], rows) for m in everyone], axis=0)
    value = jnp.concatenate([unpack_rows(m[at + part : at + 2 * part, :], rows) for m in everyone], axis=0)
    key_ref[...] = key
    value_ref[...] = value

    state = msgs[-1][:NS, :].astype(F32)
    for m in reversed(msgs[:-1]):
        decay = m[NS : NS + HALO, :].astype(F32)
        state = m[:NS, :].astype(F32) + (decay[0:1, :] + decay[1:2, :]) * state
    state_ref[...] = state
    carried = mm(low(bc_ref[:, NS:]), low(state))
    carried_ref[...] = carried
    y = y_ref[...] + mm(jnp.exp(cum_ref[...]), head_lanes(heads), HIGHEST) * carried
    y_out_ref[...] = y
    z = zq_ref[:, :width].astype(F32)
    gated = y * (z * sigmoid(z))
    gated_ref[...] = gated
    sums_ref[...] = token_sums(gated * gated)

    q = zq_ref[:, width:]
    q_heads = q.shape[1] // HEAD_DIM
    turned = mm(q, low(quarter_turn(q.shape[1])))
    query = heads_to_rows(low(q.astype(F32) * cos_ref[...] + turned * sin_ref[...]))
    query_ref[...] = query
    scores = mm_nt(query, key) * (HEAD_DIM ** (-0.5))
    place = lax.broadcasted_iota(jnp.int32, scores.shape, 0)
    column = lax.broadcasted_iota(jnp.int32, scores.shape, 1)
    place = place & (rows - 1)
    limit = jnp.where(column < rows, place, (row + 1) * rows - 1)
    scores = jnp.where(column <= limit, scores, NEG_LARGE)
    exponent = jnp.exp(scores - jnp.max(scores, axis=1, keepdims=True))
    probs = low(exponent * (1.0 / jnp.sum(exponent, axis=1, keepdims=True)))
    probs_ref[...] = probs
    out_ref[...] = low(rows_to_heads(mm(probs, value), q_heads))


def attend_back(grad_ref, probs_ref, query_ref, cos_ref, sin_ref, key_ref, value_ref, dq_ref, dkv_ref, *sent):
    count = grad_ref.shape[1] // HEAD_DIM
    rows = dkv_ref.shape[0]
    scale = HEAD_DIM ** (-0.5)
    grad = heads_to_rows(grad_ref[...])
    probs_low = probs_ref[...]
    probs = probs_low.astype(F32)
    dprobs = mm_nt(grad, value_ref[...])
    delta = jnp.sum(probs * dprobs, axis=1, keepdims=True)
    dscores = low(probs * (dprobs - delta))
    dquery = rows_to_heads(mm(dscores, key_ref[...]), count) * scale
    turned = mm(dquery, quarter_turn(dquery.shape[1]), HIGHEST)
    dq_ref[...] = low(dquery * cos_ref[...] - turned * sin_ref[...])
    dkey = mm_tn(dscores, query_ref[...]) * scale
    dvalue = mm_tn(probs_low, grad)
    dkv_ref[...] = jnp.concatenate([dkey[:rows], dvalue[:rows]], axis=1)
    for j, out in enumerate(sent):
        at = slice((j + 1) * rows, (j + 2) * rows)
        part = packed_rows(rows, out.shape[1])
        out[:part, :] = pack_rows(low(dkey[at]), out.shape[1])
        out[part:, :] = pack_rows(low(dvalue[at]), out.shape[1])


def project(scalars, hidden_ref, w_ref, out_ref):
    out_ref[...] = low(mm(hidden_ref[...], w_ref[:, : out_ref.shape[1]]))


def mix_out(
    total_heads, scalars, sums_ref, gated_ref, gain_ref, attn_ref, w_ref, normed_ref, keep_ref, give_ref, full_ref
):
    parity = scalars[scalars.shape[0] - 2]
    inv = as_column(lax.rsqrt(sums_ref[...] / (total_heads * PM) + EPSILON))
    normed = low(gated_ref[...] * inv * gain_ref[...])
    normed_ref[...] = normed
    act = jnp.concatenate([normed, attn_ref[...]], axis=1)
    full_ref[...] = mm_nt(act, w_ref[:, w_ref.shape[1] - act.shape[1] :])
    halves_to_sum(parity, full_ref, keep_ref, give_ref)


def feed_forward(
    scalars, total_ref, other_ref, tokens_ref, cot_ref, gain_ref, w_ref,
    middle_ref, hidden_ref, dgu_ref, swiglu_ref, keep_ref, give_ref, out_keep_ref, out_give_ref, full_ref,
):
    parity = scalars[scalars.shape[0] - 2]
    halves_joined(parity, total_ref, other_ref, full_ref)
    middle = tokens_ref[...].astype(F32) + full_ref[...]
    middle_ref[...] = middle
    inv = lax.rsqrt(jnp.mean(middle * middle, axis=-1, keepdims=True) + EPSILON)
    hidden_ref[...] = low(middle * inv * gain_ref[...])
    width = swiglu_ref.shape[1]
    gate_up = low(mm(hidden_ref[...], w_ref[:, : 2 * width])).astype(F32)
    gate, up = gate_up[:, :width], gate_up[:, width:]
    sig = sigmoid(gate)
    swish = gate * sig
    swiglu = low(swish * up)
    swiglu_ref[...] = swiglu
    grad = mm(cot_ref[...], w_ref[:, 2 * width :])
    dgate = low(grad * up * sig * (1.0 + gate * (1.0 - sig)))
    dup = low(grad * swish)
    dgu = jnp.concatenate([dgate, dup], axis=1)
    dgu_ref[...] = dgu
    full_ref[...] = mm_nt(dgu, w_ref[:, : 2 * width])
    halves_to_sum(parity, full_ref, keep_ref, give_ref)
    full_ref[...] = mm_nt(swiglu, w_ref[:, 2 * width :])
    halves_to_sum(parity, full_ref, out_keep_ref, out_give_ref)


def weight_products(count, scalars, *refs):
    outs = 1 if count == 1 else 2
    pairs, results = refs[:-outs], refs[-outs:]
    size = pairs[0].shape[1] // count
    for p in range(count):
        out = results[p * outs // count]
        rows = slice((p % (count // outs)) * size, (p % (count // outs) + 1) * size)
        at = 0
        for left, right in zip(pairs[0::2], pairs[1::2]):
            out[rows, at : at + right.shape[1]] = low(mm_tn(left[:, lanes_of(scalars, p, size)], right[...]))
            at += right.shape[1]


def middle_back(
    total_heads, scalars, total_ref, other_ref, middle_ref, cot_ref, gain_ref, sums_ref, gated_ref,
    gate_gain_ref, w_ref,
    dmiddle_ref, dmix_ref, dgain_ref, dnormed_ref, dattn_ref, cross_ref, dgate_gain_ref, full_ref,
):
    parity = scalars[scalars.shape[0] - 2]
    halves_joined(parity, total_ref, other_ref, full_ref)
    grad = full_ref[...]
    middle = middle_ref[...]
    inv = lax.rsqrt(jnp.mean(middle * middle, axis=-1, keepdims=True) + EPSILON)
    rows = middle * inv
    dgain_ref[...] = jnp.broadcast_to(jnp.sum(grad * rows, axis=0, keepdims=True), dgain_ref.shape)
    scaled = grad * gain_ref[...]
    dmiddle = cot_ref[...].astype(F32) + inv * (
        scaled - rows * jnp.mean(scaled * rows, axis=-1, keepdims=True)
    )
    dmiddle_ref[...] = dmiddle
    dmix_ref[...] = low(dmiddle)
    width = gated_ref.shape[1]
    first = w_ref.shape[1] - width - dattn_ref.shape[1]
    both = mm(dmix_ref[...], w_ref[:, first:])
    dnormed = both[:, :width]
    dnormed_ref[...] = dnormed
    dattn_ref[...] = low(both[:, width:])
    gated = gated_ref[...]
    product = dnormed * gated
    cross_ref[...] = token_sums(product * gate_gain_ref[...])
    inv_gate = as_column(lax.rsqrt(sums_ref[...] / (total_heads * PM) + EPSILON))
    dgate_gain_ref[...] = jnp.broadcast_to(
        jnp.sum(product * inv_gate, axis=0, keepdims=True), dgate_gain_ref.shape
    )


def gate_back(
    heads, total_heads, count, cross_ref, sums_ref, dnormed_ref, gated_ref, gain_ref, zq_ref, y_ref, cum_ref,
    bc_ref, dq_ref, *refs,
):
    msgs, kv = refs[: count - 1], refs[count - 1 : 2 * count - 1]
    dy_ref, dzq_ref = refs[2 * count - 1 : 2 * count + 1]
    sent = refs[2 * count + 1 :]
    width = y_ref.shape[1]
    size = total_heads * PM
    inv = as_column(lax.rsqrt(sums_ref[...] / size + EPSILON))
    cross = as_column(cross_ref[...])
    dgated = inv * dnormed_ref[...] * gain_ref[...] - gated_ref[...] * (inv * inv * inv * cross / size)
    z = zq_ref[:, :width].astype(F32)
    sig = sigmoid(z)
    dy = dgated * (z * sig)
    dy_ref[...] = dy
    dz = low(dgated * y_ref[...] * sig * (1.0 + z * (1.0 - sig)))
    dzq_ref[...] = jnp.concatenate([dz, dq_ref[...]], axis=1)
    weighted = dy * mm(jnp.exp(cum_ref[...]), head_lanes(heads), HIGHEST)
    state = mm_tn(low(bc_ref[:, NS:]), low(weighted))
    for j in range(count):
        sent[j][:NS, :] = low(state)
        sent[j][NS:, :] = kv[j][...]
        if j < count - 1:
            decay = msgs[j][NS : NS + HALO, :].astype(F32)
            state = state * (decay[0:1, :] + decay[1:2, :])


def conv_and_input_back(
    scalars, dpre_ref, next_ref, taps_ref, dkv_ref, ddt_ref, dzq_ref,
    hidden_ref, dgain_mid_ref, dtaps_ref, dgate_gain_ref, dsmall_ref, dskip_ref, tokens_ref, w_ref, more_ref,
    dall_ref, small_ref, keep_ref, give_ref, full_ref,
):
    parity = scalars[scalars.shape[0] - 2]
    dpre = dpre_ref[...]
    rows = dpre.shape[0]
    longer = jnp.concatenate([dpre, next_ref[...]], axis=0)
    total = taps_ref[KC - 1 : KC, :] * dpre
    for k in range(KC - 1):
        shift = KC - 1 - k
        total = total + taps_ref[k : k + 1, :] * pltpu.roll(longer, longer.shape[0] - shift, 0)[:rows]
    dall = jnp.concatenate([low(total), dkv_ref[...], ddt_ref[...]], axis=1)
    dall_ref[...] = dall
    dzq = dzq_ref[...]
    full_ref[...] = mm_nt(dall, w_ref[...]) + mm_nt(dzq, more_ref[:, : dzq.shape[1]])
    x = tokens_ref[...].astype(F32)
    inv = lax.rsqrt(jnp.mean(x * x, axis=-1, keepdims=True) + EPSILON)
    dgain = jnp.sum(full_ref[...] * (x * inv), axis=0, keepdims=True)
    model = x.shape[1]
    place = lax.broadcasted_iota(jnp.int32, (8, model), 0)
    ddt_w = mm_tn(ddt_ref[...], hidden_ref[...])[:8]
    small_ref[:, :model] = jnp.where(place == 6, dgain_mid_ref[...], jnp.where(place == 7, dgain, ddt_w))
    rest = jnp.concatenate([dgate_gain_ref[0:1, :], dsmall_ref[0:1, :], dsmall_ref[1:2, :]], axis=1)
    wide = taps_ref.shape[1]
    skip_row = jnp.concatenate([dskip_ref[0:1, :], jnp.zeros((1, wide - LANES), F32)], axis=1)
    place = lax.broadcasted_iota(jnp.int32, (8, wide), 0)
    small_ref[:, model:] = jnp.where(
        place < KC, dtaps_ref[...], jnp.where(place == KC, rest, jnp.where(place == KC + 1, skip_row, 0.0))
    )
    halves_to_sum(parity, full_ref, keep_ref, give_ref)


def input_back(scalars, total_ref, other_ref, tokens_ref, gain_ref, dmiddle_ref, dtokens_ref, full_ref):
    parity = scalars[scalars.shape[0] - 2]
    halves_joined(parity, total_ref, other_ref, full_ref)
    grad = full_ref[...]
    x = tokens_ref[...].astype(F32)
    inv = lax.rsqrt(jnp.mean(x * x, axis=-1, keepdims=True) + EPSILON)
    rows = x * inv
    scaled = grad * gain_ref[...]
    dtokens_ref[...] = dmiddle_ref[...] + inv * (
        scaled - rows * jnp.mean(scaled * rows, axis=-1, keepdims=True)
    )


def output_sum(scalars, total_ref, other_ref, middle_ref, out_ref, full_ref):
    halves_joined(scalars[scalars.shape[0] - 2], total_ref, other_ref, full_ref)
    out_ref[...] = low(middle_ref[...] + full_ref[...])


def send(x, axis, pairs):
    return lax.ppermute(x, axis, pairs)


def from_ahead(x, axis, distance):
    n = lax.axis_size(axis)
    return send(x, axis, [((i + distance) % n, i) for i in range(n)])


def from_earlier(x, distance):
    n = lax.axis_size("row")
    return send(x, "row", [(i - distance, i) for i in range(distance, n)])


def from_later(x, distance):
    n = lax.axis_size("row")
    return send(x, "row", [(i + distance, i) for i in range(n - distance)])


def swap(x, axis, bit):
    return send(x, axis, [(i, i ^ bit) for i in range(lax.axis_size(axis))])


def after(x, *others):
    return lax.optimization_barrier((x,) + others)[0]


def after_all(*values):
    return lax.optimization_barrier(values)


def direct():
    return lax.axis_size("dp") == 2 and lax.axis_size("row") == 4


def scatter_first(parts):
    if len(parts) == 1:
        return [lax.psum_scatter(parts[0], ("dp", "row"), scatter_dimension=0, tiled=True)]
    half = parts[1].shape[0] // 2
    return [swap(parts[1][half:], "dp", 1), swap(parts[1][:half], "dp", 1)]


def scatter_beside(parts, got):
    if len(parts) == 1:
        return got[0]
    half = parts[0].shape[0] // 2
    return swap(low(parts[0][half:].astype(F32) + got[0].astype(F32)), "row", 1)


def scatter_last(parts, got, beside, *late):
    if len(parts) == 1:
        return beside.astype(F32)
    blk = parts[0].shape[0] // 4
    total = parts[0][: 2 * blk].astype(F32) + got[1].astype(F32) + beside.astype(F32)
    across = swap(low(total[blk:]), "row", 2)
    return total[:blk] + (after(across, *late) if late else across).astype(F32)


def col_sum(keep, give, *others):
    part = low(keep + swap(give, "col", 1).astype(F32))
    if others:
        part = after(part, *others)
    total = low(part.astype(F32) + swap(part, "col", 2).astype(F32))
    return total, swap(total, "col", 1)


def low_col_sum(values):
    values = low(values)
    values = low(values.astype(F32) + swap(values, "col", 1).astype(F32))
    return values.astype(F32) + swap(values, "col", 2).astype(F32)


def tiny_col_sum(values):
    values = values + swap(values, "col", 1)
    return values + swap(values, "col", 2)


def tiny_row_sum(values, before_rows):
    if lax.axis_size("dp") == 2:
        values = values + swap(values, "dp", 1)
    else:
        values = lax.psum(values, "dp")
    values = after(values, before_rows)
    values = values + swap(values, "row", 1)
    return values + swap(values, "row", 2)


def per_device(
    tokens, cotangent, norm_in, z_weight, x_weight, dt_weight, q_weight, bc_weight, key_value_weight,
    conv_x, conv_bc, dt_bias, a_log, d_skip, gate_gain, mamba_weight, attn_weight, norm_mid,
    gate_weight, up_weight, down_weight,
):
    dp_n, row_n, col_n = (lax.axis_size(a) for a in ("dp", "row", "col"))
    dp, row, col = (lax.axis_index(a) for a in ("dp", "row", "col"))
    if row_n != 4 or col_n != 4:
        raise ValueError("row, col: 4")
    rows, model = tokens.shape
    seq = rows * row_n
    heads = dt_bias.shape[0]
    total_heads = heads * col_n
    width = heads * PM
    q_width = q_weight.shape[1]
    q_heads = q_width // HEAD_DIM
    hidden = gate_weight.shape[1]
    blk = model // (dp_n * row_n)
    kv_group = col * q_heads * KEY_HEADS // QUERY_HEADS
    conv_width = width + 2 * NS
    in_width = conv_width + 2 * LANES

    shard_in = jnp.concatenate(
        [
            x_weight,
            bc_weight,
            lax.dynamic_slice_in_dim(key_value_weight, kv_group * HEAD_DIM, HEAD_DIM, 1),
            lax.dynamic_slice_in_dim(key_value_weight, (KEY_HEADS + kv_group) * HEAD_DIM, HEAD_DIM, 1),
            dt_weight,
            jnp.zeros((blk, LANES - heads), BF16),
        ],
        axis=1,
    )
    shard_mix = jnp.concatenate([z_weight, q_weight, mamba_weight.T, attn_weight.T], axis=1)
    shard_ff = jnp.concatenate([gate_weight, up_weight, down_weight.T], axis=1)
    halo = from_earlier(tokens[rows - HALO :], 1)
    ext = jnp.concatenate([halo, tokens], axis=0).astype(F32)
    inv_in = lax.rsqrt(jnp.mean(ext * ext, axis=-1, keepdims=True) + EPSILON)
    hidden_ext = low(ext * inv_in * norm_in)
    hidden_in = hidden_ext[HALO:]

    if direct():
        order = [((dp + i) % 2) * row_n + (row ^ x) for i in range(2) for x in (0, 2, 1, 3)]
        across, beside = swap(shard_in, "row", 2), swap(shard_in, "row", 1)
        own = swap(shard_in, "dp", 1)
        across, beside, own, hidden_ext, shard_ff = after_all(across, beside, own, hidden_ext, shard_ff)
        corner = swap(across, "row", 1)
        over = [swap(across, "dp", 1), swap(beside, "dp", 1)]
        ff_across = swap(shard_ff, "row", 2)
        corner, ff_across, shard_mix, shard_ff, *over = after_all(corner, ff_across, shard_mix, shard_ff, *over)
        last = swap(corner, "dp", 1)
        mix_across, mix_beside = swap(shard_mix, "row", 2), swap(shard_mix, "row", 1)
        ff_beside = swap(shard_ff, "row", 1)
        mix_own, ff_own = swap(shard_mix, "dp", 1), swap(shard_ff, "dp", 1)
        last, mix_across, mix_beside, ff_beside, mix_own, ff_own = after_all(
            last, mix_across, mix_beside, ff_beside, mix_own, ff_own
        )
        in_blocks = [shard_in, across, beside, corner, own] + over + [last]
        mix_corner = swap(mix_across, "row", 1)
        mix_over = [swap(v, "dp", 1) for v in (mix_across, mix_beside)]
    else:
        in_blocks = [lax.all_gather(shard_in, ("dp", "row"), axis=0, tiled=True)]
        mix_blocks = [lax.all_gather(shard_mix, ("dp", "row"), axis=0, tiled=True)]
        ff_blocks = [lax.all_gather(shard_ff, ("dp", "row"), axis=0, tiled=True)]
        order = [jnp.int32(0)]
    scalars = jnp.stack([jnp.int32(v) for v in order] + [jnp.int32(col % 2), jnp.int32(row)])

    positions = (row * rows + jnp.arange(rows, dtype=jnp.int32)).astype(F32)
    half = HEAD_DIM // 2
    frequency = ROPE_BASE ** (-jnp.arange(half).astype(F32) / half)
    angles = positions[:, None] * frequency[None, :]
    cosine, sine = jnp.cos(angles), jnp.sin(angles)
    cos_q = jnp.concatenate([cosine] * (2 * q_heads), axis=1)
    sin_q = jnp.concatenate([sine] * (2 * q_heads), axis=1)
    cos_kv = jnp.concatenate([cosine, cosine, jnp.ones((rows, HEAD_DIM), F32)], axis=1)
    sin_kv = jnp.concatenate([sine, sine, jnp.zeros((rows, HEAD_DIM), F32)], axis=1)

    taps = jnp.concatenate([conv_x, conv_bc], axis=1)
    rate = -jnp.exp(a_log)

    def lane_row(v):
        return jnp.pad(v, (0, LANES - heads))[None, :]

    params = jnp.concatenate([lane_row(dt_bias), lane_row(rate), jnp.zeros((6, LANES), F32)], axis=0)
    skip = jnp.repeat(d_skip, PM)[None, :]
    area = rows * rows * heads
    part = packed_rows(rows, width)
    y_base, msg, proj, x_heads, bc_map, slope, cum, step, in_full = kernel_call(
        partial(scan_local, heads),
        (
            ((rows, width), F32),
            ((NS + HALO + 2 * part, width), BF16),
            ((HALO + rows, in_width), BF16),
            ((rows, width), F32),
            ((rows, 2 * NS), F32),
            ((rows, conv_width), F32),
            ((rows, LANES), F32),
            ((rows, LANES), F32),
        ),
        (area * 2 * PM * 10, 4000000, area),
        scalars,
        hidden_ext,
        taps,
        params,
        skip,
        cos_kv,
        sin_kv,
        in_blocks,
        keep=True,
        near=True,
    )
    if direct():
        msg, mix_corner, ff_across, *mix_over = after_all(msg, mix_corner, ff_across, *mix_over)
        msgs = [from_earlier(msg, j) for j in range(1, row_n)]
        mix_over.append(swap(mix_corner, "dp", 1))
        ff_over = [swap(ff_across, "dp", 1)]
        ff_across, ff_beside, ff_over[0], *moved = after_all(ff_across, ff_beside, ff_over[0], *mix_over, *msgs)
        mix_over, msgs = moved[:3], moved[3:]
        mix_blocks = [shard_mix, mix_across, mix_beside, mix_corner, mix_own] + mix_over
        ff_corner = swap(ff_across, "row", 1)
        ff_over.append(swap(ff_beside, "dp", 1))
    else:
        msgs = [from_earlier(msg, j) for j in range(1, row_n)]
    zq, mix_full = kernel_call(
        project,
        (((rows, width + q_width), BF16),),
        (2 * rows * model * (width + q_width), 4000000, 0),
        scalars,
        hidden_in,
        mix_blocks,
        keep=True,
    )

    (
        attn_value, probs, query, key, value, state_in, carried, y, gated, sums,
    ) = kernel_call(
        partial(mix_tokens, heads, row_n - 1),
        (
            ((rows, q_width), BF16),
            ((q_heads * rows, seq), BF16),
            ((q_heads * rows, HEAD_DIM), BF16),
            ((seq, HEAD_DIM), BF16),
            ((seq, HEAD_DIM), BF16),
            ((NS, width), F32),
            ((rows, width), F32),
            ((rows, width), F32),
            ((rows, width), F32),
            ((8, rows), F32),
        ),
        (8 * q_width * rows * seq, 6000000, q_heads * rows * seq),
        scalars,
        msg,
        *msgs,
        y_base,
        cum,
        bc_map,
        zq,
        cos_q,
        sin_q,
    )
    sums = tiny_col_sum(sums)
    gain_row = gate_gain[None, :]
    halves = (((rows // 2, model), F32), ((rows // 2, model), BF16))
    full_scratch = ((rows, model), F32)
    mamba_normed, keep, give, _ = kernel_call(
        partial(mix_out, total_heads),
        (((rows, width), BF16),) + halves + (full_scratch,),
        (2 * rows * model * (width + q_width), 4000000, 0),
        scalars,
        sums,
        gated,
        gain_row,
        attn_value,
        mix_full,
    )
    if direct():
        give, ff_corner, *ff_over = after_all(give, ff_corner, *ff_over)
        ff_blocks = [shard_ff, ff_across, ff_beside, ff_corner, ff_own] + ff_over + [swap(ff_corner, "dp", 1)]
    total, other = col_sum(keep, give)

    gain_mid = norm_mid[None, :]
    middle, hidden_mid, grad_gate_up, swiglu, keep, give, out_keep, out_give, _ = kernel_call(
        feed_forward,
        (
            ((rows, model), F32),
            ((rows, model), BF16),
            ((rows, 2 * hidden), BF16),
            ((rows, hidden), BF16),
        )
        + halves
        + halves
        + (full_scratch,),
        (14 * rows * model * hidden, 8000000, rows * hidden),
        scalars,
        total,
        other,
        [tokens],
        [cotangent],
        gain_mid,
        ff_blocks,
    )

    def weight_grad(*operands):
        columns = sum(v.shape[1] for v in operands[1::2])
        outs = 2 if direct() else 1
        return kernel_call(
            partial(weight_products, len(order)),
            (((model // outs, columns), BF16),) * outs,
            (2 * rows * model * columns, 5000000, 0),
            scalars,
            *operands,
        )

    ff_parts = weight_grad(hidden_mid, grad_gate_up, cotangent, swiglu)
    total, other = col_sum(keep, give, *ff_parts)
    if direct():
        near = ff_parts[1].shape[0] // 2
        ff_got = [swap(ff_parts[1][near:], "dp", 1)]
    else:
        ff_got = scatter_first(ff_parts)

    grad_middle, grad_mix, dgain_mid, grad_normed, grad_attn, cross, dgate_gain, _ = kernel_call(
        partial(middle_back, total_heads),
        (
            ((rows, model), F32),
            ((rows, model), BF16),
            ((8, model), F32),
            ((rows, width), F32),
            ((rows, q_width), BF16),
            ((8, rows), F32),
            ((8, width), F32),
            full_scratch,
        ),
        (2 * rows * model * (width + q_width), 6000000, 0),
        scalars,
        total,
        other,
        middle,
        [cotangent],
        gain_mid,
        sums,
        gated,
        gain_row,
        mix_full,
    )
    cross = tiny_col_sum(cross)
    if direct():
        ff_got.append(swap(after(ff_parts[1][:near], grad_mix), "dp", 1))
        cross, ff_got[0] = after_all(cross, ff_got[0])
    grad_query, grad_kv_own, *kv_sent = kernel_call(
        attend_back,
        (((rows, q_width), BF16), ((rows, LANES), F32)) + (((2 * part, width), BF16),) * (row_n - 1),
        (16 * q_width * rows * seq, 4000000, 0),
        None,
        grad_attn,
        probs,
        query,
        cos_q,
        sin_q,
        key,
        value,
    )
    grad_y, grad_zq, *sent = kernel_call(
        partial(gate_back, heads, total_heads, row_n - 1),
        (((rows, width), F32), ((rows, width + q_width), BF16)) + (((NS + 2 * part, width), BF16),) * (row_n - 1),
        (2 * rows * NS * width, 4000000, rows * width),
        None,
        cross,
        sums,
        grad_normed,
        gated,
        gain_row,
        zq,
        y,
        cum,
        bc_map,
        grad_query,
        *msgs[: row_n - 2],
        *kv_sent,
    )
    got = [from_later(sent[j - 1], j) for j in range(1, row_n)]
    dx_local, dbc_local, dcum, dstep, dskip = kernel_call(
        partial(scan_back_local, heads),
        (
            ((rows, width), F32),
            ((rows, 2 * NS), F32),
            ((rows, LANES), F32),
            ((rows, LANES), F32),
            ((8, LANES), F32),
        ),
        (area * 2 * PM * 20, 4000000, area),
        None,
        grad_y,
        x_heads,
        bc_map,
        cum,
        step,
        carried,
        state_in,
        skip,
    )
    act = jnp.concatenate([mamba_normed, attn_value], axis=1)
    mix_parts = weight_grad(hidden_in, grad_zq, grad_mix, act)
    mix_got = scatter_first(mix_parts)
    got = list(after(tuple(got), mix_parts, mix_got[0]))

    dpre, first, grad_dt, grad_kv, dsmall, dtaps = kernel_call(
        partial(scan_back_end, heads, row_n - 1),
        (
            ((rows, conv_width), F32),
            ((8, conv_width), F32),
            ((rows, LANES), BF16),
            ((rows, LANES), BF16),
            ((8, LANES), F32),
            ((8, conv_width), F32),
        ),
        (rows * NS * width * 10, 4000000, rows * LANES * 3),
        None,
        *got,
        state_in,
        x_heads,
        bc_map,
        cum,
        step,
        dx_local,
        dbc_local,
        dcum,
        dstep,
        slope,
        proj,
        params,
        grad_kv_own,
        cos_kv,
        sin_kv,
    )
    following = from_later(first, 1)
    ff_beside = scatter_beside(ff_parts, [after(ff_got[0], got[0])])
    following = after(following, ff_got, mix_got, ff_beside)

    grad_all, small, keep, give, _ = kernel_call(
        conv_and_input_back,
        (((rows, in_width), BF16), ((8, model + conv_width), F32)) + halves + (full_scratch,),
        (2 * rows * model * (in_width + width + q_width), 8000000, 0),
        scalars,
        dpre,
        following,
        taps,
        grad_kv,
        grad_dt,
        grad_zq,
        hidden_in,
        dgain_mid,
        dtaps,
        dgate_gain,
        dsmall,
        dskip,
        [tokens],
        in_full,
        mix_full,
    )
    tail_width = conv_width + LANES
    tail_parts = weight_grad(hidden_in, grad_all[:, :tail_width])
    tail_got = scatter_first(tail_parts)
    mix_beside = scatter_beside(mix_parts, [after(mix_got[0], ff_beside, tail_got)])
    total, other = col_sum(keep, give)
    out_total, out_other = col_sum(out_keep, after(out_give, total))
    layer_out, _ = kernel_call(
        output_sum,
        (((rows, model), BF16), full_scratch),
        (rows * model, 3000000, 0),
        scalars,
        out_total,
        out_other,
        middle,
    )
    tail_beside = scatter_beside(tail_parts, [after(tail_got[0], ff_beside)])
    grad_in_w = scatter_last(tail_parts, tail_got, tail_beside)
    grad_ff = scatter_last(ff_parts, ff_got, after(ff_beside, grad_all), tail_beside)
    grad_mix_w = scatter_last(mix_parts, mix_got, after(mix_beside, tail_beside), grad_in_w)
    grad_tokens, _ = kernel_call(
        input_back,
        (((rows, model), F32), full_scratch),
        (rows * model * 10, 4000000, 0),
        scalars,
        total,
        other,
        [tokens],
        norm_in[None, :],
        [grad_middle],
    )

    bc_w = grad_in_w[:, width:conv_width]
    kv_w = grad_in_w[:, conv_width:]
    spot = (jnp.arange(KEY_HEADS) == kv_group).astype(F32)
    wide = [spot[i] * kv_w[:, :HEAD_DIM] for i in range(KEY_HEADS)]
    wide += [spot[i] * kv_w[:, HEAD_DIM:] for i in range(KEY_HEADS)]
    shared = jnp.concatenate([bc_w] + wide, axis=1)
    shared = low_col_sum(shared)

    line = lax.broadcasted_iota(jnp.int32, small.shape, 0)
    lane = lax.broadcasted_iota(jnp.int32, small.shape, 1)
    partial_lanes = ((line == 7) & (lane < model)) | ((line < KC) & (lane >= model + width))
    small = jnp.where(partial_lanes, tiny_col_sum(small), small)
    small = tiny_row_sum(small, grad_in_w)
    taps_at = model + width
    place = (dp * row_n + row) * blk
    return (
        layer_out,
        grad_tokens,
        small[7, :model],
        grad_mix_w[:, :width],
        grad_in_w[:, :width],
        lax.dynamic_slice(small, (0, place), (heads, blk)).T,
        grad_mix_w[:, width : width + q_width],
        shared[:, : 2 * NS],
        shared[:, 2 * NS :],
        small[:KC, model:taps_at],
        small[:KC, taps_at:],
        small[KC, taps_at : taps_at + heads],
        small[KC, taps_at + LANES : taps_at + LANES + heads],
        small[KC + 1, model : model + heads],
        small[KC, model:taps_at],
        grad_mix_w[:, width + q_width : 2 * width + q_width].T,
        grad_mix_w[:, 2 * width + q_width :].T,
        small[6, :model],
        grad_ff[:, :hidden],
        grad_ff[:, hidden : 2 * hidden],
        grad_ff[:, 2 * hidden :].T,
    )


def solution(mesh):
    by_rows = P(("dp", "row"), None)
    both = P(("dp", "row"), "col")
    turned = P("col", ("dp", "row"))
    per_col = P("col")
    taps = P(None, "col")
    in_specs = (
        by_rows, by_rows, P(), both, both, both, both, by_rows, by_rows, taps, P(), per_col, per_col,
        per_col, per_col, turned, turned, P(), both, both, turned,
    )
    out_specs = (
        by_rows, by_rows, P(), both, both, both, both, by_rows, by_rows, taps, P(), per_col, per_col,
        per_col, per_col, turned, turned, P(), both, both, turned,
    )
    return jax.shard_map(
        per_device, mesh=mesh, in_specs=in_specs, out_specs=out_specs, check_vma=False
    )
```
